128 devices in a mesh: inline: 8 (over y, core), xline: 16 (over z, x).
Axes of the slice: x: 4, y: 4, z: 4, core: 2. Of those that a mesh axis runs over, the one named last changes fastest.
Arguments:
- records: bfloat16 [2, 8, 16, 8, 8192], P(None, 'inline', 'xline'), may hold values from -6 to 6
- beam_count: int32 [8, 16], P('inline', 'xline'), may hold values from 1 to 8, 80 in all within a row
- owner_list: int32 [10240, 1], P(('inline', 'xline')), may hold values from 0 to 15; in each aligned block of 80 rows (0 to 79, 80 to 159, ...) at most 10 rows name the same one
- block_list: int32 [10240, 1], P(('inline', 'xline')), may hold values from 0 to 127
- travel_table: float32 [2048, 64, 128], P('xline'), may hold values from 1 to 126
- amp_table: float32 [2048, 64, 128], P('xline'), may hold values from -6 to 6
Outputs:
- image: float32 [8, 16, 128], P('inline', 'xline')
The draws below stay inside these ranges and needn't reach their ends.
Inputs may be any that keep to these rules, and one draw needn't show every extreme that they name: `owner_list`: the 80 rows of one tile name each owner at most 10 times, a bound that some block reaches. `beam_count`: some tile of every inline row has all 8 beams live.
All inputs are finite; a program needn't handle non-finite values. No bound on the sum of `beam_count` on one device may be relied on, other than what follows from the above.
Results may differ from the reference program's by a relative error of at most 0.0026.
Values may be sent and summed in bfloat16 or wider, within the bound.
A program may use at most 64 MiB of HBM per device.

```python
import math
import jax
import jax.numpy as jnp
import numpy as np
from jax import lax

NS = 128
NP = 64
PTS = 128
BEAM_DEV = 8
SHOTS = 2
BLK_DEV = 128
REQ = 80
CAP = 10
NBLK = 2048
N_INLINE = 8
N_XLINE = 16


def with_ends(drawn, stream_key, smallest, high):
    place = [jax.random.randint(jax.random.fold_in(stream_key, axis), (), 0, length) for axis, length in enumerate(drawn.shape)]
    widest = drawn.shape.index(max(drawn.shape))
    neighbour = place[:widest] + [(place[widest] + 1) % drawn.shape[widest]] + place[widest + 1:]
    return drawn.at[tuple(place)].set(smallest).at[tuple(neighbour)].set(high)


def block_scale(key, shape, cuts, least, largest):
    factor_of = 1.0
    for dim, parts in cuts:
        steps = jax.random.uniform(jax.random.fold_in(jax.random.fold_in(key, 6), dim), (parts,), jnp.float32, least / len(cuts), largest / len(cuts))
        factor_of = factor_of * jnp.repeat(jnp.exp(steps), shape[dim] // parts).reshape((-1,) + (1,) * (len(shape) - 1 - dim))
    return factor_of


def profile(count, total, bound, lean):
    weights = [(1 << 20) // math.isqrt(grade ** lean) + 1 for grade in range(2, count + 1)]
    rest, holding = total - bound - (count - 1), [1] * (count - 1)
    while rest > 0:
        free = [i for i in range(count - 1) if holding[i] < bound]
        whole, left = sum([weights[i] for i in free]), rest
        for i in free:
            extra = min(bound - holding[i], max(1, left * weights[i] // whole), rest)
            holding[i] = holding[i] + extra
            rest = rest - extra
    return np.array([bound] + holding)


def uneven_parts(key, number_of, total, bound, lean):
    if number_of == 2:
        one = jax.random.randint(key, (), max(1, total - bound), min(bound, total - 1) + 1)
        return jnp.stack([one, total - one])
    sizes = jnp.asarray(profile(number_of, total, bound, lean), jnp.int32)
    twos = (number_of - 1) // 2
    donor, taker = sizes[1:1 + 2 * twos:2], sizes[2:2 + 2 * twos:2]
    margin = jnp.minimum(donor - 1, bound - taker)
    moved = jax.random.randint(jax.random.fold_in(key, 1), (twos,), 0, 1 << 20) % (margin + 1)
    sizes = sizes.at[1:1 + 2 * twos:2].set(donor - moved).at[2:2 + 2 * twos:2].set(taker + moved)
    return sizes[jax.random.permutation(jax.random.fold_in(key, 2), number_of)]


def deal_out(stream_key, own, number, rows, amount, top, limit, slope):
    sequence = jax.random.permutation(stream_key, amount)
    heavy_load, common = load_shares(amount, rows * top, limit, slope, True), load_shares(amount, rows * top, limit, slope, False)
    places = jnp.arange(amount)

    def named(tallies, turn):
        used = int((tallies > 0).sum())
        fixed = max(1, used // 4)
        shifted = fixed + (places - fixed + turn * (used - fixed)) % max(1, amount - fixed)
        return jnp.zeros((amount,), jnp.int32).at[sequence[jnp.where(places < fixed, places, shifted)]].set(jnp.asarray(tallies, jnp.int32))

    tallies = jnp.where(number % 4 == 0, named(heavy_load, number // 4), named(common, number - number // 4 - 1))
    mixed = jax.random.permutation(jax.random.fold_in(own, 3), amount)
    giver, taker = mixed[0:amount // 2 * 2:2], mixed[1:amount // 2 * 2:2]
    room = jnp.minimum(tallies[giver] - 1, limit - tallies[taker]) // 2
    room = jnp.where((giver == sequence[0]) | (taker == sequence[0]) | (tallies[taker] == 0), 0, jnp.maximum(room, 0))
    shifted = jax.random.randint(jax.random.fold_in(own, 4), (amount // 2,), 0, 1 << 20) % (room + 1)
    tallies = tallies.at[giver].add(-shifted).at[taker].add(shifted)
    items = jnp.searchsorted(jnp.cumsum(tallies), jnp.arange(rows * top), side="right").astype(jnp.int32)
    grid = items.reshape(top, rows).T
    grid = grid[jax.random.permutation(jax.random.fold_in(own, 1), rows)]
    turn = jax.random.randint(jax.random.fold_in(own, 2), (rows, 1), 0, top)
    return jnp.take_along_axis(grid, (jnp.arange(top)[None, :] + turn) % top, axis=1)


def load_shares(number_of, total, most, slope, full):
    portions = [(1 << 20) // math.isqrt(standing ** slope) + 1 for standing in range(1, number_of + 1)]
    largest = most if full else min(most, max(-(-total // number_of), total * portions[0] // sum(portions)))
    least = 1 if total - largest >= number_of - 1 else 0
    counts, rest = [largest] + [least] * (number_of - 1), total - largest - least * (number_of - 1)
    while rest > 0:
        movable = [i for i in range(1, number_of) if counts[i] < largest] or [i for i in range(1, number_of) if counts[i] < most]
        pool, budget = sum([portions[i] for i in movable]), rest
        for i in movable:
            addition = min(most - counts[i], max(1, budget * portions[i] // pool), rest)
            counts[i] = counts[i] + addition
            rest = rest - addition
    return np.array(counts)


def normal_values(key, dims, spread, limit, cuts=(), held_as=jnp.bfloat16):
    loudness = block_scale(key, dims, cuts, -0.22, 0.18) if cuts else 1.0
    entries = jax.random.normal(key, dims, jnp.float32) * spread * loudness
    return jnp.minimum(jnp.maximum(entries, -limit), limit).astype(held_as)


def setup_inputs(seed: int = 0) -> dict:
    streams_of = jax.random.split(jax.random.key(seed), 7)
    records = normal_values(streams_of[0], (SHOTS, N_INLINE, N_XLINE, BEAM_DEV, NP * NS), 1.0, 6.0, ((1, 8), (2, 16)))
    beam_count = jax.vmap(lambda own: uneven_parts(own, N_XLINE, N_XLINE * BEAM_DEV * 5 // 8, BEAM_DEV, 2))(jax.random.split(streams_of[1], N_INLINE)).reshape((N_INLINE, N_XLINE)).astype(jnp.int32)
    owner_list_keys = jax.random.split(jax.random.fold_in(streams_of[2], 1), (N_INLINE * N_XLINE * REQ) // REQ)
    owner_list_turns = jax.random.permutation(jax.random.fold_in(streams_of[2], 3), (N_INLINE * N_XLINE * REQ) // REQ)
    owner_list = jax.vmap(lambda own, number: deal_out(jax.random.fold_in(streams_of[2], 2), own, number, REQ, N_XLINE, 1, CAP, 2))(owner_list_keys, owner_list_turns).reshape((N_INLINE * N_XLINE * REQ, 1))
    block_list = with_ends(jax.random.randint(streams_of[3], (N_INLINE * N_XLINE * REQ, 1), 0, BLK_DEV), jax.random.fold_in(streams_of[3], 1), 0, BLK_DEV - 1).astype(jnp.int32)
    travel_table = jnp.clip(1.0 + 125.0 * jax.random.uniform(streams_of[4], (NBLK, NP, PTS), jnp.float32) ** block_scale(streams_of[4], (NBLK, NP, PTS), ((0, 16),), -0.2, 0.2), 1.0, 126.0)
    amp_table = normal_values(streams_of[5], (NBLK, NP, PTS), 1.0, 6.0, ((0, 16),), jnp.float32)
    return {"records": records, "beam_count": beam_count, "owner_list": owner_list, "block_list": block_list, "travel_table": travel_table, "amp_table": amp_table}


def image_beam(record, travel, amplitude):
    samples = jnp.arange(NS, dtype=jnp.float32)
    weights = jnp.maximum(0.0, 1.0 - jnp.abs(samples[None, :, None] - travel[:, None, :])).astype(jnp.bfloat16)
    weights = lax.optimization_barrier(weights).astype(jnp.float32)
    traces = jnp.einsum('pt,ptx->px', record.reshape(NP, NS).astype(jnp.float32), weights)
    contrib = lax.optimization_barrier(jnp.sum(amplitude * traces, axis=0))
    energy = jnp.mean(jnp.square(record.astype(jnp.float32)))
    lighting = energy * lax.optimization_barrier(jnp.sum(amplitude * amplitude, axis=0))
    return (contrib, lighting)

def reference(records, beam_count, owner_list, block_list, travel_table, amp_table):
    alive_mask = (jnp.arange(BEAM_DEV, dtype=jnp.int32)[None, None, :] < beam_count[:, :, None]).astype(records.dtype)
    live_records = records * alive_mask[None, :, :, :, None]
    padded = jnp.pad(live_records, ((0, 0), (1, 1), (1, 1), (0, 0), (0, 0)))
    sources = jnp.stack([padded[:, 1:-1, 1:-1], padded[:, :-2, 1:-1], padded[:, 2:, 1:-1], padded[:, 1:-1, :-2], padded[:, 1:-1, 2:]], axis=1)
    sources = jnp.transpose(sources, (2, 3, 0, 1, 4, 5)).reshape(N_INLINE * N_XLINE * REQ, NP * NS)
    block_ids = (owner_list[:, 0] * BLK_DEV + block_list[:, 0]).astype(jnp.int32)

    def one_beam(inputs):
        record, block_id = inputs
        return image_beam(record, travel_table[block_id], amp_table[block_id])
    contrib, lighting = lax.map(one_beam, (sources, block_ids), batch_size=16)
    summed = contrib.reshape(N_INLINE, N_XLINE, REQ, PTS).sum(axis=2)
    lighting_sum = lighting.reshape(N_INLINE, N_XLINE, REQ, PTS).sum(axis=2)
    return summed / jnp.sqrt(1.0 + lighting_sum)
```

```python
import jax
import jax.numpy as jnp
from jax import lax
from jax.experimental import pallas as pl
from jax.experimental.pallas import tpu as pltpu
from jax.sharding import PartitionSpec as P

NS = 128
NP = 64
BEAMS = 8
SHOTS = 2
RECS = SHOTS * BEAMS
COLS = 16
USES = 5 * RECS
LIST = 512
DEPTH = 8


def image_kernel(count, uses, energy, records, travel, amp, out, rec_buf, trav_buf, amp_buf, acc, sems):
    n = count[0]

    def copies(u):
        slot = lax.rem(u, DEPTH)
        word = uses[u]
        rec, block = word // 128 % 256, word % 128
        return (
            pltpu.make_async_copy(records.at[rec], rec_buf.at[slot], sems.at[slot, 0]),
            pltpu.make_async_copy(travel.at[block], trav_buf.at[slot], sems.at[slot, 1]),
            pltpu.make_async_copy(amp.at[block], amp_buf.at[slot], sems.at[slot, 2]),
        )

    def start(u):
        @pl.when(u < n)
        def _():
            for c in copies(u):
                c.start()

    for u in range(DEPTH - 1):
        start(jnp.int32(u))
    acc[...] = jnp.zeros_like(acc)

    def step(u, carry):
        start(u + DEPTH - 1)
        for c in copies(u):
            c.wait()
        slot = lax.rem(u, DEPTH)
        word = uses[u]
        rec, target = word // 128 % 256, word // (128 * 256)
        total = jnp.zeros((8, NS), jnp.float32)
        square = jnp.zeros((8, NS), jnp.float32)
        for q in range(NP // 8):
            rows = pl.ds(8 * q, 8)
            t = trav_buf[slot, rows, :]
            a = amp_buf[slot, rows, :]
            if q % 2 == 0:
                pair = rec_buf[slot, pl.ds(8 * q, 16), :].astype(jnp.float32)
            r = pair[8 * (q % 2) : 8 * (q % 2) + 8]
            k = t.astype(jnp.int32)
            f = t - k.astype(jnp.float32)
            w0 = (1.0 - f).astype(jnp.bfloat16).astype(jnp.float32)
            w1 = f.astype(jnp.bfloat16).astype(jnp.float32)
            v0 = jnp.take_along_axis(r, k, axis=1, mode="promise_in_bounds")
            v1 = jnp.take_along_axis(r, k + 1, axis=1, mode="promise_in_bounds")
            total += a * (v0 * w0 + v1 * w1)
            square += a * a
        acc[target, 0] += total
        acc[target, 1] += square * energy[rec]
        return carry

    lax.fori_loop(0, n, step, 0)
    out[...] = jnp.sum(acc[...], axis=2)


def image_uses(count, uses, energy, records, travel, amp):
    smem = pl.BlockSpec(memory_space=pltpu.SMEM)
    hbm = pl.BlockSpec(memory_space=pl.ANY)
    return pl.pallas_call(
        image_kernel,
        out_shape=jax.ShapeDtypeStruct((3 * COLS, 2, NS), jnp.float32),
        in_specs=[smem, smem, smem, hbm, hbm, hbm],
        out_specs=pl.BlockSpec(memory_space=pltpu.VMEM),
        scratch_shapes=[
            pltpu.VMEM((DEPTH, NP, NS), jnp.bfloat16),
            pltpu.VMEM((DEPTH, NP, NS), jnp.float32),
            pltpu.VMEM((DEPTH, NP, NS), jnp.float32),
            pltpu.VMEM((3 * COLS, 2, 8, NS), jnp.float32),
            pltpu.SemaphoreType.DMA((DEPTH, 3)),
        ],
        compiler_params=pltpu.CompilerParams(vmem_limit_bytes=16 << 20),
        cost_estimate=pl.CostEstimate(flops=10_000_000, bytes_accessed=8_000_000, transcendentals=0),
        name="image_uses",
    )(count, uses, energy, records, travel, amp)


def per_device(records, beam_count, owner_list, block_list, travel_table, amp_table):
    row, col = lax.axis_index("inline"), lax.axis_index("xline")
    rows = lax.axis_size("inline")
    up = [(i, i + 1) for i in range(rows - 1)]
    down = [(i + 1, i) for i in range(rows - 1)]
    records = records.reshape(RECS, NP, NS)
    gathered = lax.all_gather(records, "xline", axis=0, tiled=True)

    named = (owner_list * 128 + block_list)[:, 0].astype(jnp.float32)
    named = named.reshape(SHOTS, 5, BEAMS).transpose(1, 0, 2).reshape(5, RECS)
    from_next = lax.ppermute(named[1], "inline", down)
    from_prev = lax.ppermute(named[2], "inline", up)
    energy = jnp.mean(jnp.square(records.astype(jnp.float32)), axis=(1, 2))
    meta = jnp.concatenate(
        [
            named[0],
            from_next,
            from_prev,
            named[3],
            named[4],
            energy,
            jnp.full((32,), beam_count[0, 0].astype(jnp.float32)),
        ]
    )
    meta = lax.all_gather(meta, "xline", axis=0)
    names = meta[:, :USES].reshape(COLS, 5, SHOTS, BEAMS).astype(jnp.int32)
    energies = meta[:, USES : USES + RECS].reshape(COLS * RECS)
    counts = meta[:, USES + RECS].astype(jnp.int32)
    j = lax.broadcasted_iota(jnp.int32, names.shape, 0)
    k = lax.broadcasted_iota(jnp.int32, names.shape, 1)
    s = lax.broadcasted_iota(jnp.int32, names.shape, 2)
    b = lax.broadcasted_iota(jnp.int32, names.shape, 3)
    none = jnp.zeros((1,), jnp.int32)
    before = jnp.concatenate([none, counts[:-1]])
    after = jnp.concatenate([counts[1:], none])
    live = jnp.stack(
        [
            counts,
            jnp.where(row + 1 < rows, counts, 0),
            jnp.where(row > 0, counts, 0),
            before,
            after,
        ],
        axis=1,
    )
    wanted = (b < live[:, :, None, None]) & (names // 128 == col)
    source = j + (k == 4) - (k == 3)
    shift = 1 + (k == 1) - (k == 2)
    word = names % 128 + 128 * (source * RECS + s * BEAMS + b) + 128 * 256 * (shift * COLS + j)
    wanted, word = wanted.reshape(-1, NS), word.reshape(-1)
    marks = wanted.astype(jnp.float32)
    lanes = jnp.arange(NS)
    lines = jnp.arange(marks.shape[0])
    within = jnp.dot(marks, (lanes[:, None] <= lanes[None, :]).astype(jnp.float32))
    ahead = jnp.dot((lines[None, :] < lines[:, None]).astype(jnp.float32), within[:, -1:])
    place = jnp.where(wanted, (within + ahead).astype(jnp.int32) - 1, -1).reshape(-1)
    slots = jnp.arange(LIST, dtype=jnp.int32)
    uses = jnp.sum(jnp.where(place[None, :] == slots[:, None], word[None, :], 0), axis=1)
    count = jnp.sum(wanted.astype(jnp.int32)).reshape(1)

    sums = image_uses(count, uses, energies, gathered, travel_table, amp_table)
    sums = sums.reshape(3, COLS, 2 * NS)
    total = sums[1] + lax.ppermute(sums[0], "inline", down) + lax.ppermute(sums[2], "inline", up)
    mine = lax.psum_scatter(total, "xline", scatter_dimension=0, tiled=True)
    image = mine[0, :NS] / jnp.sqrt(1.0 + mine[0, NS:])
    return image[None, None, :]


def solution(mesh):
    placed = (
        P(None, "inline", "xline", None, None),
        P("inline", "xline"),
        P(("inline", "xline"), None),
        P(("inline", "xline"), None),
        P("xline", None, None),
        P("xline", None, None),
    )
    return jax.shard_map(
        per_device,
        mesh=mesh,
        in_specs=placed,
        out_specs=P("inline", "xline", None),
        check_vma=False,
    )
```

```python
import jax
import jax.numpy as jnp
from jax import lax
from jax.experimental import pallas as pl
from jax.experimental.pallas import tpu as pltpu
from jax.sharding import PartitionSpec as P

NS = 128
NP = 64
BEAMS = 8
SHOTS = 2
RECS = SHOTS * BEAMS
SIDE = 4
COLS = SIDE * SIDE
ROWS = 8
USES = 5 * RECS
LIST = 512
TARGETS = 3 * COLS
GROUP = 8
MESH = pl.DeviceIdType.MESH

ENERGY = USES
COUNT = USES + RECS


def greet(row, col):
    barrier = pltpu.get_barrier_semaphore()
    for other in range(1, COLS):
        pl.semaphore_signal(
            barrier, inc=1, device_id=(row, lax.rem(col + other, COLS)), device_id_type=MESH
        )

    @pl.when(row > 0)
    def _():
        pl.semaphore_signal(barrier, inc=1, device_id=(row - 1, col), device_id_type=MESH)

    @pl.when(row < ROWS - 1)
    def _():
        pl.semaphore_signal(barrier, inc=1, device_id=(row + 1, col), device_id_type=MESH)

    edges = (row > 0).astype(jnp.int32) + (row < ROWS - 1).astype(jnp.int32)
    pl.semaphore_wait(barrier, COLS - 1 + edges)


def gather_kernel(
    records, index, travel, amp,
    held, travel_out, amp_out, uses_out, index_out,
    near, mixed, lines, uses_vmem, index_vmem,
    local_sems, send_sems, recv_sems, near_send, near_recv, line_send, line_recv,
):
    row, col = lax.axis_index("inline"), lax.axis_index("xline")
    z, x = col // SIDE, lax.rem(col, SIDE)
    loads = [
        pltpu.make_async_copy(travel, travel_out, local_sems.at[0]),
        pltpu.make_async_copy(amp, amp_out, local_sems.at[1]),
        pltpu.make_async_copy(records, held.at[pl.ds(col * RECS, RECS)], local_sems.at[2]),
    ]
    near[...] = jnp.zeros_like(near)
    greet(row, col)

    def at(dz, dx):
        return lax.rem(z + dz + SIDE, SIDE) * SIDE + lax.rem(x + dx + SIDE, SIDE)

    started = {}

    def block(route, first, second, lo, size):
        tile = at(second, first) if route == 0 else at(first, second)
        return pl.ds(tile * RECS + route * BEAMS + lo, size)

    def toward(route, axis, step):
        along_x = (axis == 0) == (route == 0)
        return (row, at(0, step) if along_x else at(step, 0))

    def send(key, route, axis, step, first, second, lo, size):
        here = block(route, first, second, lo, size)
        n = len(started)
        if first == 0 and second == 0:
            source = records.at[pl.ds(route * BEAMS + lo, size)]
        else:
            source = held.at[here]
        copy = pltpu.make_async_remote_copy(
            src_ref=source,
            dst_ref=held.at[here],
            send_sem=send_sems.at[n],
            recv_sem=recv_sems.at[n],
            device_id=toward(route, axis, step),
            device_id_type=MESH,
        )
        copy.start()
        started[key] = copy

    half = BEAMS // 2
    both = (0, 1)
    for route in both:
        for step in (1, -1):
            send(("a", route, step), route, 0, step, 0, 0, 0, BEAMS)
    for route in both:
        for step in (1, -1):
            send(("c", route, 0, step), route, 1, step, 0, 0, 0, BEAMS)
    for copy in loads:
        copy.start()

    up = pltpu.make_async_remote_copy(
        index, near.at[0], near_send.at[0], near_recv.at[0], device_id=(row + 1, col), device_id_type=MESH
    )
    down = pltpu.make_async_remote_copy(
        index, near.at[1], near_send.at[1], near_recv.at[1], device_id=(row - 1, col), device_id_type=MESH
    )
    @pl.when(row < ROWS - 1)
    def _():
        up.start()

    @pl.when(row > 0)
    def _():
        down.start()

    @pl.when(row > 0)
    def _():
        up.wait_recv()

    @pl.when(row < ROWS - 1)
    def _():
        down.wait_recv()

    @pl.when(row < ROWS - 1)
    def _():
        up.wait_send()

    @pl.when(row > 0)
    def _():
        down.wait_send()

    kind = lax.broadcasted_iota(jnp.int32, (8, NS), 1) // RECS
    mixed[...] = jnp.where(kind == 1, near[1], jnp.where(kind == 2, near[0], index[...]))
    shares = []
    for other in range(1, COLS):
        share = pltpu.make_async_remote_copy(
            mixed,
            lines.at[other],
            line_send.at[other],
            line_recv.at[other],
            device_id=(row, lax.rem(col + other, COLS)),
            device_id_type=MESH,
        )
        share.start()
        shares.append(share)
    lines[0] = mixed[...]

    for route in both:
        for step in (1, -1):
            started["a", route, step].wait_recv()
            lo = 0 if step > 0 else half
            send(("b", route, step), route, 0, step, -step, 0, lo, half)
            for way in (1, -1):
                send(("c", route, -step, way), route, 1, way, -step, 0, 0, BEAMS)
    for route in both:
        for way in (1, -1):
            started["c", route, 0, way].wait_recv()
            lo = 0 if way > 0 else half
            send(("d", route, 0, way), route, 1, way, 0, -way, lo, half)

    build_list(row, col, shares, lines, index_vmem, uses_vmem)

    for route in both:
        for step in (1, -1):
            started["b", route, step].wait_recv()
        for way in (1, -1):
            send(("c", route, 2, way), route, 1, way, 2, 0, 0, BEAMS)
    for first in (-1, 1, 2):
        for route in both:
            for way in (1, -1):
                started["c", route, first, way].wait_recv()
                lo = 0 if way > 0 else half
                send(("d", route, first, way), route, 1, way, first, -way, lo, half)
    finish = [
        pltpu.make_async_copy(uses_vmem, uses_out, local_sems.at[3]),
        pltpu.make_async_copy(index_vmem, index_out, local_sems.at[4]),
    ]
    for copy in finish:
        copy.start()
    for first in (0, -1, 1, 2):
        for route in both:
            for way in (1, -1):
                started["d", route, first, way].wait_recv()
    for copy in started.values():
        copy.wait_send()
    for share in shares:
        share.wait_send()
    for copy in loads + finish:
        copy.wait()


def build_list(row, col, shares, lines, index_vmem, uses_vmem):
    for share in shares:
        share.wait_recv()
    for tile in range(COLS):
        index_vmem[pl.ds(tile, 1), :] = lines[lax.rem(col - tile + COLS, COLS)][0:1, :]
    table = index_vmem[...]
    names = table.astype(jnp.int32)
    shape = (COLS, NS)
    lane = lax.broadcasted_iota(jnp.int32, shape, 1)
    tile = lax.broadcasted_iota(jnp.int32, shape, 0)
    kind, beam = lane // RECS, lax.rem(lane, BEAMS)
    counts = jnp.broadcast_to(names[:, COUNT : COUNT + 1], shape)
    before = jnp.where(tile > 0, pltpu.roll(counts, 1, 0), 0)
    after = jnp.where(tile < COLS - 1, pltpu.roll(counts, COLS - 1, 0), 0)
    last, first = (row == ROWS - 1).astype(jnp.int32), (row == 0).astype(jnp.int32)
    live = jnp.where(kind == 3, before, jnp.where(kind == 4, after, counts))
    live = jnp.where(kind == 1, counts * (1 - last), live)
    live = jnp.where(kind == 2, counts * (1 - first), live)
    wanted = (lane < USES) & (beam < live) & (names // 128 == col)
    marks = wanted.astype(jnp.float32)
    earlier = lax.broadcasted_iota(jnp.int32, (NS, NS), 0) <= lax.broadcasted_iota(jnp.int32, (NS, NS), 1)
    within = jnp.dot(marks, earlier.astype(jnp.float32), preferred_element_type=jnp.float32)
    above = lax.broadcasted_iota(jnp.int32, (COLS, COLS), 1) < lax.broadcasted_iota(jnp.int32, (COLS, COLS), 0)
    totals = jnp.broadcast_to(jnp.sum(marks, axis=1, keepdims=True), shape)
    ahead = jnp.dot(above.astype(jnp.float32), totals, preferred_element_type=jnp.float32)
    place = jnp.where(wanted, within + ahead - 1.0, -1.0)
    number = jnp.sum(marks)

    source = tile + (kind == 4).astype(jnp.int32) - (kind == 3).astype(jnp.int32)
    shift = 1 + (kind == 1).astype(jnp.int32) - (kind == 2).astype(jnp.int32)
    fields = (
        lax.rem(names, 128).astype(jnp.float32),
        (source * RECS + lax.rem(lane, RECS)).astype(jnp.float32),
        (shift * COLS + tile).astype(jnp.float32),
    )
    upright = jnp.transpose(place)
    slot = lax.broadcasted_iota(jnp.int32, (NS, LIST), 1).astype(jnp.float32)
    line = lax.broadcasted_iota(jnp.int32, (8, NS), 0)
    listed = jnp.zeros((8, LIST), jnp.float32)
    for t in range(COLS):
        here = (jnp.broadcast_to(upright[:, t : t + 1], (NS, LIST)) == slot).astype(jnp.bfloat16)
        rows = jnp.zeros((8, NS), jnp.float32)
        for f, field in enumerate(fields):
            rows = jnp.where(line == f, jnp.broadcast_to(field[t : t + 1, :], (8, NS)), rows)
        listed += jnp.dot(rows.astype(jnp.bfloat16), here, preferred_element_type=jnp.float32)
    place_in = lax.broadcasted_iota(jnp.int32, (8, LIST), 1).astype(jnp.float32)
    part = lax.broadcasted_iota(jnp.int32, (8, LIST), 0)
    listed = jnp.where((part == 2) & (place_in >= number), float(TARGETS), listed)
    listed = jnp.where(part == 3, number, listed)
    uses_vmem[...] = listed.astype(jnp.int32)


def gather(records, index, travel, amp):
    hbm = pl.BlockSpec(memory_space=pl.ANY)
    vmem = pl.BlockSpec(memory_space=pltpu.VMEM)
    smem = pl.BlockSpec(memory_space=pltpu.SMEM)
    return pl.pallas_call(
        gather_kernel,
        out_shape=(
            pltpu.VMEM((COLS * RECS, NP, NS), jnp.bfloat16),
            pltpu.VMEM(travel.shape, jnp.float32),
            pltpu.VMEM(amp.shape, jnp.float32),
            jax.ShapeDtypeStruct((8, LIST), jnp.int32),
            jax.ShapeDtypeStruct((COLS, NS), jnp.float32),
        ),
        in_specs=[hbm, vmem, hbm, hbm],
        out_specs=(vmem, vmem, vmem, hbm, hbm),
        scratch_shapes=[
            pltpu.VMEM((2, 8, NS), jnp.float32),
            pltpu.VMEM((8, NS), jnp.float32),
            pltpu.VMEM((COLS, 8, NS), jnp.float32),
            pltpu.VMEM((8, LIST), jnp.int32),
            pltpu.VMEM((COLS, NS), jnp.float32),
            pltpu.SemaphoreType.DMA((5,)),
            pltpu.SemaphoreType.DMA((40,)),
            pltpu.SemaphoreType.DMA((40,)),
            pltpu.SemaphoreType.DMA((2,)),
            pltpu.SemaphoreType.DMA((2,)),
            pltpu.SemaphoreType.DMA((COLS,)),
            pltpu.SemaphoreType.DMA((COLS,)),
        ],
        compiler_params=pltpu.CompilerParams(
            collective_id=0, has_side_effects=True, vmem_limit_bytes=32 << 20
        ),
        cost_estimate=pl.CostEstimate(flops=10_000_000, bytes_accessed=16_000_000, transcendentals=0),
        name="gather_records",
    )(records, index, travel, amp)


def image_kernel(uses, index, records, travel, amp, out, acc):
    acc[...] = jnp.zeros_like(acc)

    def step(i, carry):
        picked = []
        for d in range(GROUP):
            u = i * GROUP + d
            picked.append((uses[0, u], uses[1, u], uses[2, u]))
        totals = [jnp.zeros((8, NS), jnp.float32) for _ in picked]
        squares = [jnp.zeros((8, NS), jnp.float32) for _ in picked]
        for q in range(NP // 8):
            rows = pl.ds(8 * q, 8)
            for d, (block, rec, _) in enumerate(picked):
                t = travel[block, rows, :]
                a = amp[block, rows, :]
                pair = records[rec, pl.ds(16 * (q // 2), 16), :].astype(jnp.float32)
                r = pair[8 * (q % 2) : 8 * (q % 2) + 8]
                k = t.astype(jnp.int32)
                f = t - k.astype(jnp.float32)
                w0 = (1.0 - f).astype(jnp.bfloat16).astype(jnp.float32)
                w1 = f.astype(jnp.bfloat16).astype(jnp.float32)
                v0 = jnp.take_along_axis(r, k, axis=1, mode="promise_in_bounds")
                v1 = jnp.take_along_axis(r, k + 1, axis=1, mode="promise_in_bounds")
                totals[d] += a * (v0 * w0 + v1 * w1)
                squares[d] += a * a
        for d, (_, rec, target) in enumerate(picked):
            energy = index[rec // RECS, ENERGY + lax.rem(rec, RECS)]
            acc[target, 0] += totals[d]
            acc[target, 1] += squares[d] * energy
        return carry

    lax.fori_loop(0, (uses[3, 0] + GROUP - 1) // GROUP, step, 0)
    out[...] = jnp.sum(acc[pl.ds(0, TARGETS)], axis=2)


def image(uses, index, records, travel, amp):
    vmem = pl.BlockSpec(memory_space=pltpu.VMEM)
    smem = pl.BlockSpec(memory_space=pltpu.SMEM)
    return pl.pallas_call(
        image_kernel,
        out_shape=pltpu.VMEM((TARGETS, 2, NS), jnp.float32),
        in_specs=[smem, smem, vmem, vmem, vmem],
        out_specs=vmem,
        scratch_shapes=[pltpu.VMEM((TARGETS + 1, 2, 8, NS), jnp.float32)],
        compiler_params=pltpu.CompilerParams(vmem_limit_bytes=32 << 20),
        cost_estimate=pl.CostEstimate(flops=10_000_000, bytes_accessed=8_000_000, transcendentals=0),
        name="image_uses",
    )(uses, index, records, travel, amp)


def exchange_kernel(sums, out, near, total, parts, near_send, near_recv, part_send, part_recv):
    row, col = lax.axis_index("inline"), lax.axis_index("xline")
    greet(row, col)
    up = pltpu.make_async_remote_copy(
        sums.at[2], near.at[0], near_send.at[0], near_recv.at[0], device_id=(row + 1, col), device_id_type=MESH
    )
    down = pltpu.make_async_remote_copy(
        sums.at[0], near.at[1], near_send.at[1], near_recv.at[1], device_id=(row - 1, col), device_id_type=MESH
    )

    @pl.when(row < ROWS - 1)
    def _():
        up.start()

    @pl.when(row > 0)
    def _():
        down.start()

    total[...] = sums[1]

    @pl.when(row > 0)
    def _():
        up.wait_recv()
        total[...] += near[0]

    @pl.when(row < ROWS - 1)
    def _():
        down.wait_recv()
        total[...] += near[1]

    copies = []
    for other in range(1, COLS):
        there = lax.rem(col + other, COLS)
        copy = pltpu.make_async_remote_copy(
            total.at[there],
            parts.at[other],
            part_send.at[other],
            part_recv.at[other],
            device_id=(row, there),
            device_id_type=MESH,
        )
        copy.start()
        copies.append(copy)
    mine = total[col]
    for copy, other in zip(copies, range(1, COLS)):
        copy.wait_recv()
        mine += parts[other]
    out[0] = mine[0:1] / jnp.sqrt(1.0 + mine[1:2])
    for copy in copies:
        copy.wait_send()

    @pl.when(row < ROWS - 1)
    def _():
        up.wait_send()

    @pl.when(row > 0)
    def _():
        down.wait_send()


def exchange(sums):
    vmem = pl.BlockSpec(memory_space=pltpu.VMEM)
    return pl.pallas_call(
        exchange_kernel,
        out_shape=jax.ShapeDtypeStruct((1, 1, NS), jnp.float32),
        in_specs=[vmem],
        out_specs=vmem,
        scratch_shapes=[
            pltpu.VMEM((2, COLS, 2, NS), jnp.float32),
            pltpu.VMEM((COLS, 2, NS), jnp.float32),
            pltpu.VMEM((COLS, 2, NS), jnp.float32),
            pltpu.SemaphoreType.DMA((2,)),
            pltpu.SemaphoreType.DMA((2,)),
            pltpu.SemaphoreType.DMA((COLS,)),
            pltpu.SemaphoreType.DMA((COLS,)),
        ],
        compiler_params=pltpu.CompilerParams(collective_id=1, has_side_effects=True),
        cost_estimate=pl.CostEstimate(flops=10_000, bytes_accessed=100_000, transcendentals=0),
        name="exchange_sums",
    )(sums)


def per_device(records, beam_count, owner_list, block_list, travel_table, amp_table):
    records = records.reshape(RECS, NP, NS)
    named = (owner_list * 128 + block_list)[:, 0].astype(jnp.float32)
    named = named.reshape(SHOTS, 5, BEAMS).transpose(1, 0, 2).reshape(USES)
    energy = jnp.mean(jnp.square(records.astype(jnp.float32)), axis=(1, 2))
    count = jnp.broadcast_to(beam_count[0].astype(jnp.float32), (NS - COUNT,))
    index = jnp.broadcast_to(jnp.concatenate([named, energy, count]), (8, NS))
    gathered, travel, amp, uses, index = gather(records, index, travel_table, amp_table)
    sums = image(uses, index, gathered, travel, amp)
    return exchange(sums.reshape(3, COLS, 2, NS))


def solution(mesh):
    placed = (
        P(None, "inline", "xline", None, None),
        P("inline", "xline"),
        P(("inline", "xline"), None),
        P(("inline", "xline"), None),
        P("xline", None, None),
        P("xline", None, None),
    )
    return jax.shard_map(
        per_device,
        mesh=mesh,
        in_specs=placed,
        out_specs=P("inline", "xline", None),
        check_vma=False,
    )
```

```python
import jax
import jax.numpy as jnp
from jax import lax
from jax.experimental import pallas as pl
from jax.experimental.pallas import tpu as pltpu
from jax.sharding import PartitionSpec as P

NS = 128
NP = 64
BEAMS = 8
SHOTS = 2
RECS = SHOTS * BEAMS
SIDE = 4
COLS = SIDE * SIDE
ROWS = 8
USES = 5 * RECS
LIST = 512
TARGETS = 3 * COLS
GROUP = 8
MESH = pl.DeviceIdType.MESH

ENERGY = USES
COUNT = USES + RECS


def greet(row, col):
    barrier = pltpu.get_barrier_semaphore()
    for other in range(1, COLS):
        pl.semaphore_signal(
            barrier, inc=1, device_id=(row, lax.rem(col + other, COLS)), device_id_type=MESH
        )

    @pl.when(row > 0)
    def _():
        pl.semaphore_signal(barrier, inc=1, device_id=(row - 1, col), device_id_type=MESH)

    @pl.when(row < ROWS - 1)
    def _():
        pl.semaphore_signal(barrier, inc=1, device_id=(row + 1, col), device_id_type=MESH)

    edges = (row > 0).astype(jnp.int32) + (row < ROWS - 1).astype(jnp.int32)
    pl.semaphore_wait(barrier, COLS - 1 + edges)


def gather_kernel(
    records, index, travel, amp,
    held, travel_out, amp_out, uses_out, index_out,
    near, mixed, lines, uses_vmem, index_vmem,
    local_sems, send_sems, recv_sems, near_send, near_recv, line_send, line_recv,
):
    row, col = lax.axis_index("inline"), lax.axis_index("xline")
    z, x = col // SIDE, lax.rem(col, SIDE)
    loads = [
        pltpu.make_async_copy(travel, travel_out, local_sems.at[0]),
        pltpu.make_async_copy(amp, amp_out, local_sems.at[1]),
        pltpu.make_async_copy(records, held.at[pl.ds(col * RECS, RECS)], local_sems.at[2]),
    ]
    near[...] = jnp.zeros_like(near)
    greet(row, col)

    def at(dz, dx):
        return lax.rem(z + dz + SIDE, SIDE) * SIDE + lax.rem(x + dx + SIDE, SIDE)

    started = {}

    def block(route, first, second, lo, size):
        tile = at(second, first) if route == 0 else at(first, second)
        return pl.ds(tile * RECS + route * BEAMS + lo, size)

    def toward(route, axis, step):
        along_x = (axis == 0) == (route == 0)
        return (row, at(0, step) if along_x else at(step, 0))

    def send(key, route, axis, step, first, second, lo, size):
        here = block(route, first, second, lo, size)
        n = len(started)
        if first == 0 and second == 0:
            source = records.at[pl.ds(route * BEAMS + lo, size)]
        else:
            source = held.at[here]
        copy = pltpu.make_async_remote_copy(
            src_ref=source,
            dst_ref=held.at[here],
            send_sem=send_sems.at[n],
            recv_sem=recv_sems.at[n],
            device_id=toward(route, axis, step),
            device_id_type=MESH,
        )
        copy.start()
        started[key] = copy

    half = BEAMS // 2
    both = (0, 1)
    for route in both:
        for step in (1, -1):
            send(("a", route, step), route, 0, step, 0, 0, 0, BEAMS)
    for route in both:
        for step in (1, -1):
            send(("c", route, 0, step), route, 1, step, 0, 0, 0, BEAMS)
    for copy in loads:
        copy.start()

    up = pltpu.make_async_remote_copy(
        index, near.at[0], near_send.at[0], near_recv.at[0], device_id=(row + 1, col), device_id_type=MESH
    )
    down = pltpu.make_async_remote_copy(
        index, near.at[1], near_send.at[1], near_recv.at[1], device_id=(row - 1, col), device_id_type=MESH
    )
    @pl.when(row < ROWS - 1)
    def _():
        up.start()

    @pl.when(row > 0)
    def _():
        down.start()

    @pl.when(row > 0)
    def _():
        up.wait_recv()

    @pl.when(row < ROWS - 1)
    def _():
        down.wait_recv()

    @pl.when(row < ROWS - 1)
    def _():
        up.wait_send()

    @pl.when(row > 0)
    def _():
        down.wait_send()

    kind = lax.broadcasted_iota(jnp.int32, (8, NS), 1) // RECS
    mixed[...] = jnp.where(kind == 1, near[1], jnp.where(kind == 2, near[0], index[...]))
    shares = []
    for other in range(1, COLS):
        share = pltpu.make_async_remote_copy(
            mixed,
            lines.at[other],
            line_send.at[other],
            line_recv.at[other],
            device_id=(row, lax.rem(col + other, COLS)),
            device_id_type=MESH,
        )
        share.start()
        shares.append(share)
    lines[0] = mixed[...]

    for route in both:
        for step in (1, -1):
            started["a", route, step].wait_recv()
            lo = 0 if step > 0 else half
            send(("b", route, step), route, 0, step, -step, 0, lo, half)
            for way in (1, -1):
                send(("c", route, -step, way), route, 1, way, -step, 0, 0, BEAMS)
    for route in both:
        for way in (1, -1):
            started["c", route, 0, way].wait_recv()
            lo = 0 if way > 0 else half
            send(("d", route, 0, way), route, 1, way, 0, -way, lo, half)

    build_list(row, col, shares, lines, index_vmem, uses_vmem)

    for route in both:
        for step in (1, -1):
            started["b", route, step].wait_recv()
        for way in (1, -1):
            send(("c", route, 2, way), route, 1, way, 2, 0, 0, BEAMS)
    for first in (-1, 1, 2):
        for route in both:
            for way in (1, -1):
                started["c", route, first, way].wait_recv()
                lo = 0 if way > 0 else half
                send(("d", route, first, way), route, 1, way, first, -way, lo, half)
    finish = [
        pltpu.make_async_copy(uses_vmem, uses_out, local_sems.at[3]),
        pltpu.make_async_copy(index_vmem, index_out, local_sems.at[4]),
    ]
    for copy in finish:
        copy.start()
    for first in (0, -1, 1, 2):
        for route in both:
            for way in (1, -1):
                started["d", route, first, way].wait_recv()
    for copy in started.values():
        copy.wait_send()
    for share in shares:
        share.wait_send()
    for copy in loads + finish:
        copy.wait()


def build_list(row, col, shares, lines, index_vmem, uses_vmem):
    for share in shares:
        share.wait_recv()
    for tile in range(COLS):
        index_vmem[pl.ds(tile, 1), :] = lines[lax.rem(col - tile + COLS, COLS)][0:1, :]
    table = index_vmem[...]
    names = table.astype(jnp.int32)
    shape = (COLS, NS)
    lane = lax.broadcasted_iota(jnp.int32, shape, 1)
    tile = lax.broadcasted_iota(jnp.int32, shape, 0)
    kind, beam = lane // RECS, lax.rem(lane, BEAMS)
    counts = jnp.broadcast_to(names[:, COUNT : COUNT + 1], shape)
    before = jnp.where(tile > 0, pltpu.roll(counts, 1, 0), 0)
    after = jnp.where(tile < COLS - 1, pltpu.roll(counts, COLS - 1, 0), 0)
    last, first = (row == ROWS - 1).astype(jnp.int32), (row == 0).astype(jnp.int32)
    live = jnp.where(kind == 3, before, jnp.where(kind == 4, after, counts))
    live = jnp.where(kind == 1, counts * (1 - last), live)
    live = jnp.where(kind == 2, counts * (1 - first), live)
    wanted = (lane < USES) & (beam < live) & (names // 128 == col)
    marks = wanted.astype(jnp.float32)
    earlier = lax.broadcasted_iota(jnp.int32, (NS, NS), 0) <= lax.broadcasted_iota(jnp.int32, (NS, NS), 1)
    within = jnp.dot(marks, earlier.astype(jnp.float32), preferred_element_type=jnp.float32)
    above = lax.broadcasted_iota(jnp.int32, (COLS, COLS), 1) < lax.broadcasted_iota(jnp.int32, (COLS, COLS), 0)
    totals = jnp.broadcast_to(jnp.sum(marks, axis=1, keepdims=True), shape)
    ahead = jnp.dot(above.astype(jnp.float32), totals, preferred_element_type=jnp.float32)
    place = jnp.where(wanted, within + ahead - 1.0, -1.0)
    number = jnp.sum(marks)

    source = tile + (kind == 4).astype(jnp.int32) - (kind == 3).astype(jnp.int32)
    shift = 1 + (kind == 1).astype(jnp.int32) - (kind == 2).astype(jnp.int32)
    fields = (
        lax.rem(names, 128).astype(jnp.float32),
        (source * RECS + lax.rem(lane, RECS)).astype(jnp.float32),
        (shift * COLS + tile).astype(jnp.float32),
    )
    upright = jnp.transpose(place)
    slot = lax.broadcasted_iota(jnp.int32, (NS, LIST), 1).astype(jnp.float32)
    line = lax.broadcasted_iota(jnp.int32, (8, NS), 0)
    listed = jnp.zeros((8, LIST), jnp.float32)
    for t in range(COLS):
        here = (jnp.broadcast_to(upright[:, t : t + 1], (NS, LIST)) == slot).astype(jnp.bfloat16)
        rows = jnp.zeros((8, NS), jnp.float32)
        for f, field in enumerate(fields):
            rows = jnp.where(line == f, jnp.broadcast_to(field[t : t + 1, :], (8, NS)), rows)
        listed += jnp.dot(rows.astype(jnp.bfloat16), here, preferred_element_type=jnp.float32)
    place_in = lax.broadcasted_iota(jnp.int32, (8, LIST), 1).astype(jnp.float32)
    part = lax.broadcasted_iota(jnp.int32, (8, LIST), 0)
    listed = jnp.where((part == 2) & (place_in >= number), float(TARGETS), listed)
    listed = jnp.where(part == 3, number, listed)
    uses_vmem[...] = listed.astype(jnp.int32)


def gather(records, index, travel, amp):
    hbm = pl.BlockSpec(memory_space=pl.ANY)
    vmem = pl.BlockSpec(memory_space=pltpu.VMEM)
    smem = pl.BlockSpec(memory_space=pltpu.SMEM)
    return pl.pallas_call(
        gather_kernel,
        out_shape=(
            pltpu.VMEM((COLS * RECS, NP, NS), jnp.bfloat16),
            pltpu.VMEM(travel.shape, jnp.float32),
            pltpu.VMEM(amp.shape, jnp.float32),
            jax.ShapeDtypeStruct((8, LIST), jnp.int32),
            jax.ShapeDtypeStruct((COLS, NS), jnp.float32),
        ),
        in_specs=[hbm, vmem, hbm, hbm],
        out_specs=(vmem, vmem, vmem, hbm, hbm),
        scratch_shapes=[
            pltpu.VMEM((2, 8, NS), jnp.float32),
            pltpu.VMEM((8, NS), jnp.float32),
            pltpu.VMEM((COLS, 8, NS), jnp.float32),
            pltpu.VMEM((8, LIST), jnp.int32),
            pltpu.VMEM((COLS, NS), jnp.float32),
            pltpu.SemaphoreType.DMA((5,)),
            pltpu.SemaphoreType.DMA((40,)),
            pltpu.SemaphoreType.DMA((40,)),
            pltpu.SemaphoreType.DMA((2,)),
            pltpu.SemaphoreType.DMA((2,)),
            pltpu.SemaphoreType.DMA((COLS,)),
            pltpu.SemaphoreType.DMA((COLS,)),
        ],
        compiler_params=pltpu.CompilerParams(
            collective_id=0, has_side_effects=True, vmem_limit_bytes=32 << 20
        ),
        cost_estimate=pl.CostEstimate(flops=10_000_000, bytes_accessed=16_000_000, transcendentals=0),
        name="gather_records",
    )(records, index, travel, amp)


def image_kernel(uses, index, records, travel, amp, out, acc):
    acc[...] = jnp.zeros_like(acc)

    def step(i, carry):
        picked = []
        for d in range(GROUP):
            u = i * GROUP + d
            picked.append((uses[0, u], uses[1, u], uses[2, u]))
        totals = [jnp.zeros((8, NS), jnp.float32) for _ in picked]
        squares = [jnp.zeros((8, NS), jnp.float32) for _ in picked]
        for q in range(NP // 8):
            rows = pl.ds(8 * q, 8)
            for d, (block, rec, _) in enumerate(picked):
                t = travel[block, rows, :]
                a = amp[block, rows, :]
                pair = records[rec, pl.ds(16 * (q // 2), 16), :].astype(jnp.float32)
                r = pair[8 * (q % 2) : 8 * (q % 2) + 8]
                k = t.astype(jnp.int32)
                f = t - k.astype(jnp.float32)
                w0 = (1.0 - f).astype(jnp.bfloat16).astype(jnp.float32)
                w1 = f.astype(jnp.bfloat16).astype(jnp.float32)
                v0 = jnp.take_along_axis(r, k, axis=1, mode="promise_in_bounds")
                v1 = jnp.take_along_axis(r, k + 1, axis=1, mode="promise_in_bounds")
                totals[d] += a * (v0 * w0 + v1 * w1)
                squares[d] += a * a
        for d, (_, rec, target) in enumerate(picked):
            energy = index[rec // RECS, ENERGY + lax.rem(rec, RECS)]
            acc[target, 0] += totals[d]
            acc[target, 1] += squares[d] * energy
        return carry

    lax.fori_loop(0, (uses[3, 0] + GROUP - 1) // GROUP, step, 0)
    out[...] = jnp.sum(acc[pl.ds(0, TARGETS)], axis=2)


def image(uses, index, records, travel, amp):
    vmem = pl.BlockSpec(memory_space=pltpu.VMEM)
    smem = pl.BlockSpec(memory_space=pltpu.SMEM)
    return pl.pallas_call(
        image_kernel,
        out_shape=pltpu.VMEM((TARGETS, 2, NS), jnp.float32),
        in_specs=[smem, smem, vmem, vmem, vmem],
        out_specs=vmem,
        scratch_shapes=[pltpu.VMEM((TARGETS + 1, 2, 8, NS), jnp.float32)],
        compiler_params=pltpu.CompilerParams(vmem_limit_bytes=32 << 20),
        cost_estimate=pl.CostEstimate(flops=10_000_000, bytes_accessed=8_000_000, transcendentals=0),
        name="image_uses",
    )(uses, index, records, travel, amp)


def exchange_kernel(sums, out, near, total, parts, near_send, near_recv, part_send, part_recv):
    row, col = lax.axis_index("inline"), lax.axis_index("xline")
    greet(row, col)
    up = pltpu.make_async_remote_copy(
        sums.at[2], near.at[0], near_send.at[0], near_recv.at[0], device_id=(row + 1, col), device_id_type=MESH
    )
    down = pltpu.make_async_remote_copy(
        sums.at[0], near.at[1], near_send.at[1], near_recv.at[1], device_id=(row - 1, col), device_id_type=MESH
    )

    @pl.when(row < ROWS - 1)
    def _():
        up.start()

    @pl.when(row > 0)
    def _():
        down.start()

    total[...] = sums[1]

    @pl.when(row > 0)
    def _():
        up.wait_recv()
        total[...] += near[0]

    @pl.when(row < ROWS - 1)
    def _():
        down.wait_recv()
        total[...] += near[1]

    copies = []
    for other in range(1, COLS):
        there = lax.rem(col + other, COLS)
        copy = pltpu.make_async_remote_copy(
            total.at[there],
            parts.at[other],
            part_send.at[other],
            part_recv.at[other],
            device_id=(row, there),
            device_id_type=MESH,
        )
        copy.start()
        copies.append(copy)
    mine = total[col]
    for copy, other in zip(copies, range(1, COLS)):
        copy.wait_recv()
        mine += parts[other]
    out[0] = mine[0:1] / jnp.sqrt(1.0 + mine[1:2])
    for copy in copies:
        copy.wait_send()

    @pl.when(row < ROWS - 1)
    def _():
        up.wait_send()

    @pl.when(row > 0)
    def _():
        down.wait_send()


def exchange(sums):
    vmem = pl.BlockSpec(memory_space=pltpu.VMEM)
    return pl.pallas_call(
        exchange_kernel,
        out_shape=jax.ShapeDtypeStruct((1, 1, NS), jnp.float32),
        in_specs=[vmem],
        out_specs=vmem,
        scratch_shapes=[
            pltpu.VMEM((2, COLS, 2, NS), jnp.float32),
            pltpu.VMEM((COLS, 2, NS), jnp.float32),
            pltpu.VMEM((COLS, 2, NS), jnp.float32),
            pltpu.SemaphoreType.DMA((2,)),
            pltpu.SemaphoreType.DMA((2,)),
            pltpu.SemaphoreType.DMA((COLS,)),
            pltpu.SemaphoreType.DMA((COLS,)),
        ],
        compiler_params=pltpu.CompilerParams(collective_id=1, has_side_effects=True),
        cost_estimate=pl.CostEstimate(flops=10_000, bytes_accessed=100_000, transcendentals=0),
        name="exchange_sums",
    )(sums)


def per_device(records, beam_count, owner_list, block_list, travel_table, amp_table):
    records = records.reshape(RECS, NP, NS)
    named = (owner_list * 128 + block_list)[:, 0].astype(jnp.float32)
    named = named.reshape(SHOTS, 5, BEAMS).transpose(1, 0, 2).reshape(USES)
    energy = jnp.mean(jnp.square(records.astype(jnp.float32)), axis=(1, 2))
    count = jnp.broadcast_to(beam_count[0].astype(jnp.float32), (NS - COUNT,))
    index = jnp.broadcast_to(jnp.concatenate([named, energy, count]), (8, NS))
    travel_table = pltpu.with_memory_space_constraint(travel_table, pltpu.HBM)
    amp_table = pltpu.with_memory_space_constraint(amp_table, pltpu.HBM)
    gathered, travel, amp, uses, index = gather(records, index, travel_table, amp_table)
    sums = image(uses, index, gathered, travel, amp)
    return exchange(sums.reshape(3, COLS, 2, NS))


def solution(mesh):
    placed = (
        P(None, "inline", "xline", None, None),
        P("inline", "xline"),
        P(("inline", "xline"), None),
        P(("inline", "xline"), None),
        P("xline", None, None),
        P("xline", None, None),
    )
    return jax.shard_map(
        per_device,
        mesh=mesh,
        in_specs=placed,
        out_specs=P("inline", "xline", None),
        check_vma=False,
    )
```

```python
import jax
import jax.numpy as jnp
from jax import lax
from jax.experimental import pallas as pl
from jax.experimental.pallas import tpu as pltpu
from jax.sharding import PartitionSpec as P

NS = 128
NP = 64
BEAMS = 8
SHOTS = 2
RECS = SHOTS * BEAMS
SIDE = 4
COLS = SIDE * SIDE
ROWS = 8
USES = 5 * RECS
LIST = 512
TARGETS = 3 * COLS
GROUP = 8
MESH = pl.DeviceIdType.MESH

ENERGY = USES
COUNT = USES + RECS


def greet(row, col):
    barrier = pltpu.get_barrier_semaphore()
    for other in range(1, COLS):
        pl.semaphore_signal(
            barrier, inc=1, device_id=(row, lax.rem(col + other, COLS)), device_id_type=MESH
        )

    @pl.when(row > 0)
    def _():
        pl.semaphore_signal(barrier, inc=1, device_id=(row - 1, col), device_id_type=MESH)

    @pl.when(row < ROWS - 1)
    def _():
        pl.semaphore_signal(barrier, inc=1, device_id=(row + 1, col), device_id_type=MESH)

    edges = (row > 0).astype(jnp.int32) + (row < ROWS - 1).astype(jnp.int32)
    pl.semaphore_wait(barrier, COLS - 1 + edges)


def gather_kernel(
    records, index, travel, amp,
    held, travel_out, amp_out, uses_out, index_out,
    near, mixed, lines, uses_vmem, index_vmem,
    local_sems, send_sems, recv_sems, near_send, near_recv, line_send, line_recv,
):
    row, col = lax.axis_index("inline"), lax.axis_index("xline")
    z, x = col // SIDE, lax.rem(col, SIDE)
    loads = [
        pltpu.make_async_copy(travel, travel_out, local_sems.at[0]),
        pltpu.make_async_copy(amp, amp_out, local_sems.at[1]),
        pltpu.make_async_copy(records, held.at[pl.ds(col * RECS, RECS)], local_sems.at[2]),
    ]
    near[...] = jnp.zeros_like(near)
    greet(row, col)

    def at(dz, dx):
        return lax.rem(z + dz + SIDE, SIDE) * SIDE + lax.rem(x + dx + SIDE, SIDE)

    started = {}

    def block(route, first, second, lo, size):
        tile = at(second, first) if route == 0 else at(first, second)
        return pl.ds(tile * RECS + route * BEAMS + lo, size)

    def toward(route, axis, step):
        along_x = (axis == 0) == (route == 0)
        return (row, at(0, step) if along_x else at(step, 0))

    def send(key, route, axis, step, first, second, lo, size):
        here = block(route, first, second, lo, size)
        n = len(started)
        if first == 0 and second == 0:
            source = records.at[pl.ds(route * BEAMS + lo, size)]
        else:
            source = held.at[here]
        copy = pltpu.make_async_remote_copy(
            src_ref=source,
            dst_ref=held.at[here],
            send_sem=send_sems.at[n],
            recv_sem=recv_sems.at[n],
            device_id=toward(route, axis, step),
            device_id_type=MESH,
        )
        copy.start()
        started[key] = copy

    half = BEAMS // 2
    both = (0, 1)
    for route in both:
        for step in (1, -1):
            send(("a", route, step), route, 0, step, 0, 0, 0, BEAMS)
    for route in both:
        for step in (1, -1):
            send(("c", route, 0, step), route, 1, step, 0, 0, 0, BEAMS)
    for copy in loads:
        copy.start()

    up = pltpu.make_async_remote_copy(
        index, near.at[0], near_send.at[0], near_recv.at[0], device_id=(row + 1, col), device_id_type=MESH
    )
    down = pltpu.make_async_remote_copy(
        index, near.at[1], near_send.at[1], near_recv.at[1], device_id=(row - 1, col), device_id_type=MESH
    )
    @pl.when(row < ROWS - 1)
    def _():
        up.start()

    @pl.when(row > 0)
    def _():
        down.start()

    @pl.when(row > 0)
    def _():
        up.wait_recv()

    @pl.when(row < ROWS - 1)
    def _():
        down.wait_recv()

    @pl.when(row < ROWS - 1)
    def _():
        up.wait_send()

    @pl.when(row > 0)
    def _():
        down.wait_send()

    kind = lax.broadcasted_iota(jnp.int32, (8, NS), 1) // RECS
    mixed[...] = jnp.where(kind == 1, near[1], jnp.where(kind == 2, near[0], index[...]))
    shares = []
    for other in range(1, COLS):
        share = pltpu.make_async_remote_copy(
            mixed,
            lines.at[other],
            line_send.at[other],
            line_recv.at[other],
            device_id=(row, lax.rem(col + other, COLS)),
            device_id_type=MESH,
        )
        share.start()
        shares.append(share)
    lines[0] = mixed[...]

    for route in both:
        for step in (1, -1):
            started["a", route, step].wait_recv()
            lo = 0 if step > 0 else half
            send(("b", route, step), route, 0, step, -step, 0, lo, half)
            for way in (1, -1):
                send(("c", route, -step, way), route, 1, way, -step, 0, 0, BEAMS)
    for route in both:
        for way in (1, -1):
            started["c", route, 0, way].wait_recv()
            lo = 0 if way > 0 else half
            send(("d", route, 0, way), route, 1, way, 0, -way, lo, half)

    build_list(row, col, shares, lines, index_vmem, uses_vmem)

    for route in both:
        for step in (1, -1):
            started["b", route, step].wait_recv()
        for way in (1, -1):
            send(("c", route, 2, way), route, 1, way, 2, 0, 0, BEAMS)
    for first in (-1, 1, 2):
        for route in both:
            for way in (1, -1):
                started["c", route, first, way].wait_recv()
                lo = 0 if way > 0 else half
                send(("d", route, first, way), route, 1, way, first, -way, lo, half)
    finish = [
        pltpu.make_async_copy(uses_vmem, uses_out, local_sems.at[3]),
        pltpu.make_async_copy(index_vmem, index_out, local_sems.at[4]),
    ]
    for copy in finish:
        copy.start()
    for first in (0, -1, 1, 2):
        for route in both:
            for way in (1, -1):
                started["d", route, first, way].wait_recv()
    for copy in started.values():
        copy.wait_send()
    for share in shares:
        share.wait_send()
    for copy in loads + finish:
        copy.wait()


def build_list(row, col, shares, lines, index_vmem, uses_vmem):
    for share in shares:
        share.wait_recv()
    for tile in range(COLS):
        index_vmem[pl.ds(tile, 1), :] = lines[lax.rem(col - tile + COLS, COLS)][0:1, :]
    table = index_vmem[...]
    names = table.astype(jnp.int32)
    shape = (COLS, NS)
    lane = lax.broadcasted_iota(jnp.int32, shape, 1)
    tile = lax.broadcasted_iota(jnp.int32, shape, 0)
    kind, beam = lane // RECS, lax.rem(lane, BEAMS)
    counts = jnp.broadcast_to(names[:, COUNT : COUNT + 1], shape)
    before = jnp.where(tile > 0, pltpu.roll(counts, 1, 0), 0)
    after = jnp.where(tile < COLS - 1, pltpu.roll(counts, COLS - 1, 0), 0)
    last, first = (row == ROWS - 1).astype(jnp.int32), (row == 0).astype(jnp.int32)
    live = jnp.where(kind == 3, before, jnp.where(kind == 4, after, counts))
    live = jnp.where(kind == 1, counts * (1 - last), live)
    live = jnp.where(kind == 2, counts * (1 - first), live)
    wanted = (lane < USES) & (beam < live) & (names // 128 == col)
    marks = wanted.astype(jnp.float32)
    earlier = lax.broadcasted_iota(jnp.int32, (NS, NS), 0) <= lax.broadcasted_iota(jnp.int32, (NS, NS), 1)
    within = jnp.dot(marks, earlier.astype(jnp.float32), preferred_element_type=jnp.float32)
    above = lax.broadcasted_iota(jnp.int32, (COLS, COLS), 1) < lax.broadcasted_iota(jnp.int32, (COLS, COLS), 0)
    totals = jnp.broadcast_to(jnp.sum(marks, axis=1, keepdims=True), shape)
    ahead = jnp.dot(above.astype(jnp.float32), totals, preferred_element_type=jnp.float32)
    place = jnp.where(wanted, within + ahead - 1.0, -1.0)
    number = jnp.sum(marks)

    source = tile + (kind == 4).astype(jnp.int32) - (kind == 3).astype(jnp.int32)
    shift = 1 + (kind == 1).astype(jnp.int32) - (kind == 2).astype(jnp.int32)
    fields = (
        lax.rem(names, 128).astype(jnp.float32),
        (source * RECS + lax.rem(lane, RECS)).astype(jnp.float32),
        (shift * COLS + tile).astype(jnp.float32),
    )
    upright = jnp.transpose(place)
    slot = lax.broadcasted_iota(jnp.int32, (NS, LIST), 1).astype(jnp.float32)
    line = lax.broadcasted_iota(jnp.int32, (8, NS), 0)
    listed = jnp.zeros((8, LIST), jnp.float32)
    for t in range(COLS):
        here = (jnp.broadcast_to(upright[:, t : t + 1], (NS, LIST)) == slot).astype(jnp.bfloat16)
        rows = jnp.zeros((8, NS), jnp.float32)
        for f, field in enumerate(fields):
            rows = jnp.where(line == f, jnp.broadcast_to(field[t : t + 1, :], (8, NS)), rows)
        listed += jnp.dot(rows.astype(jnp.bfloat16), here, preferred_element_type=jnp.float32)
    place_in = lax.broadcasted_iota(jnp.int32, (8, LIST), 1).astype(jnp.float32)
    part = lax.broadcasted_iota(jnp.int32, (8, LIST), 0)
    listed = jnp.where((part == 2) & (place_in >= number), float(TARGETS), listed)
    listed = jnp.where(part == 3, number, listed)
    uses_vmem[...] = listed.astype(jnp.int32)


def gather(records, index, travel, amp):
    hbm = pl.BlockSpec(memory_space=pl.ANY)
    vmem = pl.BlockSpec(memory_space=pltpu.VMEM)
    smem = pl.BlockSpec(memory_space=pltpu.SMEM)
    return pl.pallas_call(
        gather_kernel,
        out_shape=(
            pltpu.VMEM((COLS * RECS, NP, NS), jnp.bfloat16),
            pltpu.VMEM(travel.shape, jnp.float32),
            pltpu.VMEM(amp.shape, jnp.float32),
            jax.ShapeDtypeStruct((8, LIST), jnp.int32),
            jax.ShapeDtypeStruct((COLS, NS), jnp.float32),
        ),
        in_specs=[hbm, vmem, hbm, hbm],
        out_specs=(vmem, vmem, vmem, hbm, hbm),
        scratch_shapes=[
            pltpu.VMEM((2, 8, NS), jnp.float32),
            pltpu.VMEM((8, NS), jnp.float32),
            pltpu.VMEM((COLS, 8, NS), jnp.float32),
            pltpu.VMEM((8, LIST), jnp.int32),
            pltpu.VMEM((COLS, NS), jnp.float32),
            pltpu.SemaphoreType.DMA((5,)),
            pltpu.SemaphoreType.DMA((40,)),
            pltpu.SemaphoreType.DMA((40,)),
            pltpu.SemaphoreType.DMA((2,)),
            pltpu.SemaphoreType.DMA((2,)),
            pltpu.SemaphoreType.DMA((COLS,)),
            pltpu.SemaphoreType.DMA((COLS,)),
        ],
        compiler_params=pltpu.CompilerParams(
            collective_id=1, has_side_effects=True, vmem_limit_bytes=32 << 20
        ),
        cost_estimate=pl.CostEstimate(flops=10_000_000, bytes_accessed=16_000_000, transcendentals=0),
        name="gather_records",
    )(records, index, travel, amp)


def image_kernel(uses, index, records, travel, amp, out, acc):
    acc[...] = jnp.zeros_like(acc)

    def step(i, carry):
        picked = []
        for d in range(GROUP):
            u = i * GROUP + d
            picked.append((uses[0, u], uses[1, u], uses[2, u]))
        totals = [jnp.zeros((8, NS), jnp.float32) for _ in picked]
        squares = [jnp.zeros((8, NS), jnp.float32) for _ in picked]
        for q in range(NP // 8):
            rows = pl.ds(8 * q, 8)
            for d, (block, rec, _) in enumerate(picked):
                t = travel[block, rows, :]
                a = amp[block, rows, :]
                pair = records[rec, pl.ds(16 * (q // 2), 16), :].astype(jnp.float32)
                r = pair[8 * (q % 2) : 8 * (q % 2) + 8]
                k = t.astype(jnp.int32)
                f = t - k.astype(jnp.float32)
                w0 = (1.0 - f).astype(jnp.bfloat16).astype(jnp.float32)
                w1 = f.astype(jnp.bfloat16).astype(jnp.float32)
                v0 = jnp.take_along_axis(r, k, axis=1, mode="promise_in_bounds")
                v1 = jnp.take_along_axis(r, k + 1, axis=1, mode="promise_in_bounds")
                totals[d] += a * (v0 * w0 + v1 * w1)
                squares[d] += a * a
        for d, (_, rec, target) in enumerate(picked):
            energy = index[rec // RECS, ENERGY + lax.rem(rec, RECS)]
            acc[target, 0] += totals[d]
            acc[target, 1] += squares[d] * energy
        return carry

    lax.fori_loop(0, (uses[3, 0] + GROUP - 1) // GROUP, step, 0)
    out[...] = jnp.sum(acc[pl.ds(0, TARGETS)], axis=2)


def image(uses, index, records, travel, amp):
    vmem = pl.BlockSpec(memory_space=pltpu.VMEM)
    smem = pl.BlockSpec(memory_space=pltpu.SMEM)
    return pl.pallas_call(
        image_kernel,
        out_shape=pltpu.VMEM((TARGETS, 2, NS), jnp.float32),
        in_specs=[smem, smem, vmem, vmem, vmem],
        out_specs=vmem,
        scratch_shapes=[pltpu.VMEM((TARGETS + 1, 2, 8, NS), jnp.float32)],
        compiler_params=pltpu.CompilerParams(vmem_limit_bytes=32 << 20),
        cost_estimate=pl.CostEstimate(flops=10_000_000, bytes_accessed=8_000_000, transcendentals=0),
        name="image_uses",
    )(uses, index, records, travel, amp)


def exchange_kernel(sums, out, near, total, parts, near_send, near_recv, part_send, part_recv):
    row, col = lax.axis_index("inline"), lax.axis_index("xline")
    greet(row, col)
    up = pltpu.make_async_remote_copy(
        sums.at[2], near.at[0], near_send.at[0], near_recv.at[0], device_id=(row + 1, col), device_id_type=MESH
    )
    down = pltpu.make_async_remote_copy(
        sums.at[0], near.at[1], near_send.at[1], near_recv.at[1], device_id=(row - 1, col), device_id_type=MESH
    )

    @pl.when(row < ROWS - 1)
    def _():
        up.start()

    @pl.when(row > 0)
    def _():
        down.start()

    total[...] = sums[1]

    @pl.when(row > 0)
    def _():
        up.wait_recv()
        total[...] += near[0]

    @pl.when(row < ROWS - 1)
    def _():
        down.wait_recv()
        total[...] += near[1]

    copies = []
    for other in range(1, COLS):
        there = lax.rem(col + other, COLS)
        copy = pltpu.make_async_remote_copy(
            total.at[there],
            parts.at[other],
            part_send.at[other],
            part_recv.at[other],
            device_id=(row, there),
            device_id_type=MESH,
        )
        copy.start()
        copies.append(copy)
    mine = total[col]
    for copy, other in zip(copies, range(1, COLS)):
        copy.wait_recv()
        mine += parts[other]
    out[0] = mine[0:1] / jnp.sqrt(1.0 + mine[1:2])
    for copy in copies:
        copy.wait_send()

    @pl.when(row < ROWS - 1)
    def _():
        up.wait_send()

    @pl.when(row > 0)
    def _():
        down.wait_send()


def exchange(sums):
    vmem = pl.BlockSpec(memory_space=pltpu.VMEM)
    return pl.pallas_call(
        exchange_kernel,
        out_shape=jax.ShapeDtypeStruct((1, 1, NS), jnp.float32),
        in_specs=[vmem],
        out_specs=vmem,
        scratch_shapes=[
            pltpu.VMEM((2, COLS, 2, NS), jnp.float32),
            pltpu.VMEM((COLS, 2, NS), jnp.float32),
            pltpu.VMEM((COLS, 2, NS), jnp.float32),
            pltpu.SemaphoreType.DMA((2,)),
            pltpu.SemaphoreType.DMA((2,)),
            pltpu.SemaphoreType.DMA((COLS,)),
            pltpu.SemaphoreType.DMA((COLS,)),
        ],
        compiler_params=pltpu.CompilerParams(collective_id=2, has_side_effects=True),
        cost_estimate=pl.CostEstimate(flops=10_000, bytes_accessed=100_000, transcendentals=0),
        name="exchange_sums",
    )(sums)


def imaged_by_any_count(records, beam_count, owner_list, block_list, travel_table, amp_table):
    records = records.reshape(RECS, NP, NS)
    named = (owner_list * 128 + block_list)[:, 0].astype(jnp.float32)
    named = named.reshape(SHOTS, 5, BEAMS).transpose(1, 0, 2).reshape(USES)
    energy = jnp.mean(jnp.square(records.astype(jnp.float32)), axis=(1, 2))
    count = jnp.broadcast_to(beam_count[0].astype(jnp.float32), (NS - COUNT,))
    index = jnp.broadcast_to(jnp.concatenate([named, energy, count]), (8, NS))
    gathered, travel, amp, uses, index = gather(records, index, travel_table, amp_table)
    sums = image(uses, index, gathered, travel, amp)
    return exchange(sums.reshape(3, COLS, 2, NS))


PHASES = ((0, 4, 96, 0), (4, 2, 40, 128), (6, 2, 32, 192))
SLOTS = 256
NBLOCKS = 128
COPIES = 40


def fused_kernel(
    records, owner, block, count, travel, amp,
    out, flag_out,
    wide, buf0, buf1, buf2, travel_v, amp_v,
    mine, near, mixed, lines, uses_v, uses_s,
    con0, con1, con2, lit0, lit1, lit2,
    flag_mine, flags, sums, parts, edge, edges,
    local_sems, send_sems, recv_sems, near_send, near_recv, line_send, line_recv,
    flag_send, flag_recv, part_send, part_recv, edge_send, edge_recv,
):
    row, col = lax.axis_index("inline"), lax.axis_index("xline")
    z, x = col // SIDE, lax.rem(col, SIDE)
    bufs, cons, lits = (buf0, buf1, buf2), (con0, con1, con2), (lit0, lit1, lit2)
    near[...] = jnp.zeros_like(near)
    edges[...] = jnp.zeros_like(edges)

    barrier = pltpu.get_barrier_semaphore()
    for other in range(1, COLS):
        there = (row, lax.rem(col + other, COLS))
        pl.semaphore_signal(barrier, inc=1, device_id=there, device_id_type=MESH)
    for other in range(1, ROWS):
        there = (lax.rem(row + other, ROWS), col)
        pl.semaphore_signal(barrier, inc=1, device_id=there, device_id_type=MESH)

    loads = [
        pltpu.make_async_copy(travel, travel_v, local_sems.at[0]),
        pltpu.make_async_copy(amp, amp_v, local_sems.at[1]),
    ]
    for copy in loads:
        copy.start()

    wide[pl.ds(0, SHOTS * NP * BEAMS), :] = records[...].astype(jnp.float32).reshape(SHOTS * NP * BEAMS, NS)
    energies = jnp.zeros((8, NS), jnp.float32)
    lane8 = lax.broadcasted_iota(jnp.int32, (8, NS), 1)
    for s in range(SHOTS):
        for p, (begin, beams, _, _) in enumerate(PHASES):
            for b in range(beams):
                rec = wide[pl.ds(s * NP * BEAMS + begin + b, NP, stride=BEAMS), :]
                bufs[p][(s * COLS + col) * beams + b] = rec.astype(jnp.bfloat16)
                energy = jnp.sum(rec * rec, keepdims=True) * (1.0 / (NP * NS))
                energies = jnp.where(
                    lane8 == ENERGY + s * BEAMS + begin + b, jnp.broadcast_to(energy, (8, NS)), energies
                )
    named = (owner[...] * 128 + block[...]).astype(jnp.float32)
    mine[...] = jnp.where(lane8 >= COUNT, count[0, 0].astype(jnp.float32), energies)
    mine[:, 0:USES] = jnp.broadcast_to(named, (8, USES))
    pl.semaphore_wait(barrier, COLS + ROWS - 2)

    def at(dz, dx):
        return lax.rem(z + dz + SIDE, SIDE) * SIDE + lax.rem(x + dx + SIDE, SIDE)

    started = {}

    def send(key, axis, step, first, second, lo, size):
        p, route = key[0], key[1]
        tile = at(second, first) if route == 0 else at(first, second)
        here = bufs[p].at[pl.ds((route * COLS + tile) * PHASES[p][1] + lo, size)]
        along_x = (axis == 0) == (route == 0)
        n = len(started)
        copy = pltpu.make_async_remote_copy(
            src_ref=here,
            dst_ref=here,
            send_sem=send_sems.at[n],
            recv_sem=recv_sems.at[n],
            device_id=(row, at(0, step) if along_x else at(step, 0)),
            device_id_type=MESH,
        )
        copy.start()
        started[key] = copy

    both, ways = (0, 1), (1, -1)

    def own(p):
        beams = PHASES[p][1]
        for route in both:
            for step in ways:
                send((p, route, "a", step), 0, step, 0, 0, 0, beams)
        for route in both:
            for way in ways:
                send((p, route, "c", 0, way), 1, way, 0, 0, 0, beams)

    def first_neighbours(p):
        beams = PHASES[p][1]
        half = beams // 2
        for step in ways:
            for route in both:
                started[p, route, "a", step].wait_recv()
                lo = 0 if step > 0 else half
                send((p, route, "b", step), 0, step, -step, 0, lo, half)
                for way in ways:
                    send((p, route, "c", -step, way), 1, way, -step, 0, 0, beams)

    def pass_on(p, which):
        half = PHASES[p][1] // 2
        for first in which:
            for way in ways:
                for route in both:
                    started[p, route, "c", first, way].wait_recv()
                    lo = 0 if way > 0 else half
                    send((p, route, "d", first, way), 1, way, first, -way, lo, half)

    def opposite(p):
        for route in both:
            for step in ways:
                started[p, route, "b", step].wait_recv()
            for way in ways:
                send((p, route, "c", 2, way), 1, way, 2, 0, 0, PHASES[p][1])

    def arrived(p):
        for first in (0, -1, 1, 2):
            for route in both:
                for way in ways:
                    started[p, route, "d", first, way].wait_recv()

    def image_some(p, begin, end):
        _, beams, slots, base = PHASES[p]
        buf, con, lit = bufs[p], cons[p], lits[p]
        held = SHOTS * COLS * beams

        def step(i, carry):
            places = [base + i * GROUP + d for d in range(GROUP)]
            picked = [(uses_s[0, u] & (NBLOCKS - 1), uses_s[1, u] & (held - 1)) for u in places]
            totals = [jnp.zeros((8, NS), jnp.float32) for _ in picked]
            squares = [jnp.zeros((8, NS), jnp.float32) for _ in picked]
            for q in range(NP // 8):
                rows = pl.ds(8 * q, 8)
                for d, (number, rec) in enumerate(picked):
                    t = travel_v[number, rows, :]
                    a = amp_v[number, rows, :]
                    pair = buf[rec, pl.ds(16 * (q // 2), 16), :].astype(jnp.float32)
                    r = pair[8 * (q % 2) : 8 * (q % 2) + 8]
                    k = t.astype(jnp.int32)
                    f = t - k.astype(jnp.float32)
                    w0 = (1.0 - f).astype(jnp.bfloat16).astype(jnp.float32)
                    w1 = f.astype(jnp.bfloat16).astype(jnp.float32)
                    v0 = jnp.take_along_axis(r, k, axis=1, mode="promise_in_bounds")
                    v1 = jnp.take_along_axis(r, k + 1, axis=1, mode="promise_in_bounds")
                    totals[d] += a * (v0 * w0 + v1 * w1)
                    squares[d] += a * a
            for d in range(GROUP):
                con[pl.ds(i * GROUP + d, 8, stride=slots), :] = totals[d]
                lit[pl.ds(i * GROUP + d, 8, stride=slots), :] = squares[d]
            return carry

        lax.fori_loop(begin // GROUP, end // GROUP, step, 0)

    def total_of(p, listed, energy):
        _, _, slots, base = PHASES[p]
        con = sum(cons[p][pl.ds(s * slots, slots), :] for s in range(8))
        lit = sum(lits[p][pl.ds(s * slots, slots), :] for s in range(8))
        target = jnp.broadcast_to(listed[2:3, base : base + slots], (NS, slots))
        weight = jnp.broadcast_to(energy[:, base : base + slots], (NS, slots))
        line = (lax.broadcasted_iota(jnp.int32, (NS, slots), 0) + 1).astype(jnp.float32)
        to_con = jnp.where(target == line, 1.0, 0.0)
        to_lit = jnp.where((target + 4.0 == line) & (target > 0.0), weight, 0.0)
        dot = lambda m, v: jnp.dot(m, v, precision=lax.Precision.HIGHEST, preferred_element_type=jnp.float32)
        return dot(to_con, con) + dot(to_lit, lit)

    own(0)
    own(1)

    up = pltpu.make_async_remote_copy(
        mine, near.at[0], near_send.at[0], near_recv.at[0], device_id=(row + 1, col), device_id_type=MESH
    )
    down = pltpu.make_async_remote_copy(
        mine, near.at[1], near_send.at[1], near_recv.at[1], device_id=(row - 1, col), device_id_type=MESH
    )
    upward, downward = pl.when(row < ROWS - 1), pl.when(row > 0)
    upward(up.start)
    downward(down.start)
    downward(up.wait_recv)
    upward(down.wait_recv)
    kind8 = lax.rem(lane8, 5 * BEAMS) // BEAMS
    kind8 = jnp.where(lane8 < USES, kind8, 0)
    mixed[...] = jnp.where(kind8 == 1, near[1], jnp.where(kind8 == 2, near[0], mine[...]))
    shares = []
    for other in range(1, COLS):
        share = pltpu.make_async_remote_copy(
            mixed, lines.at[other], line_send.at[other], line_recv.at[other],
            device_id=(row, lax.rem(col + other, COLS)), device_id_type=MESH,
        )
        share.start()
        shares.append(share)
    lines[0] = mixed[...]

    first_neighbours(0)
    pass_on(0, (0,))
    own(2)
    first_neighbours(1)

    for share in shares:
        share.wait_recv()
    listed, energy, over = list_uses(row, col, lines)
    uses_v[...] = listed.astype(jnp.int32)
    to_smem = pltpu.make_async_copy(uses_v, uses_s, local_sems.at[2])
    to_smem.start()
    flag_mine[...] = over
    alarms = []
    for other in range(1, ROWS):
        alarm = pltpu.make_async_remote_copy(
            flag_mine, flags.at[other], flag_send.at[other], flag_recv.at[other],
            device_id=(lax.rem(row + other, ROWS), col), device_id_type=MESH,
        )
        alarm.start()
        alarms.append(alarm)

    opposite(0)
    pass_on(0, (-1, 1))
    pass_on(1, (0,))
    pass_on(0, (2,))
    opposite(1)
    first_neighbours(2)
    pass_on(1, (-1, 1))
    to_smem.wait()
    for copy in loads:
        copy.wait()
    arrived(0)
    image_some(0, 0, 32)
    pass_on(2, (0,))
    pass_on(1, (2,))
    opposite(2)
    image_some(0, 32, 64)
    pass_on(2, (-1, 1))
    image_some(0, 64, 96)
    pass_on(2, (2,))
    arrived(1)
    image_some(1, 0, 40)
    early = total_of(0, listed, energy) + total_of(1, listed, energy)
    raised = flag_mine[...]
    for alarm, other in zip(alarms, range(1, ROWS)):
        alarm.wait_recv()
        raised = jnp.maximum(raised, flags[other])
    flag_out[0] = jnp.max(raised).astype(jnp.int32)
    arrived(2)
    image_some(2, 0, 32)
    sums[...] = (early + total_of(2, listed, energy)).reshape(COLS, 8, NS)

    pieces = []
    for other in range(1, COLS):
        there = lax.rem(col + other, COLS)
        piece = pltpu.make_async_remote_copy(
            sums.at[there], parts.at[other], part_send.at[other], part_recv.at[other],
            device_id=(row, there), device_id_type=MESH,
        )
        piece.start()
        pieces.append(piece)
    whole = sums[col]
    for piece, other in zip(pieces, range(1, COLS)):
        piece.wait_recv()
        whole += parts[other]
    edge[...] = whole
    to_next = pltpu.make_async_remote_copy(
        edge, edges.at[0], edge_send.at[0], edge_recv.at[0], device_id=(row + 1, col), device_id_type=MESH
    )
    to_prev = pltpu.make_async_remote_copy(
        edge, edges.at[1], edge_send.at[1], edge_recv.at[1], device_id=(row - 1, col), device_id_type=MESH
    )
    upward(to_next.start)
    downward(to_prev.start)
    for copy in started.values():
        copy.wait_send()
    for copy in shares + alarms + pieces:
        copy.wait_send()
    upward(up.wait_send)
    downward(down.wait_send)
    downward(to_next.wait_recv)
    upward(to_prev.wait_recv)
    contrib = whole[1:2] + edges[0][2:3] + edges[1][0:1]
    lighting = whole[5:6] + edges[0][6:7] + edges[1][4:5]
    out[0] = contrib / jnp.sqrt(1.0 + lighting)
    upward(to_next.wait_send)
    downward(to_prev.wait_send)


def list_uses(row, col, lines):
    table = jnp.concatenate([lines[lax.rem(col - tile + COLS, COLS)][0:1, :] for tile in range(COLS)], axis=0)
    shape = (COLS, NS)
    lane = lax.broadcasted_iota(jnp.int32, shape, 1)
    tile = lax.broadcasted_iota(jnp.int32, shape, 0)
    shot, kind, beam = lane // (5 * BEAMS), lax.rem(lane, 5 * BEAMS) // BEAMS, lax.rem(lane, BEAMS)
    names = table.astype(jnp.int32)

    def of_source(own):
        before, after = pltpu.roll(own, 1, 0), pltpu.roll(own, COLS - 1, 0)
        return jnp.where(kind == 3, before, jnp.where(kind == 4, after, own))

    last, first = (row == ROWS - 1).astype(jnp.int32), (row == 0).astype(jnp.int32)
    missing = (
        ((kind == 1) & (last == 1))
        | ((kind == 2) & (first == 1))
        | ((kind == 3) & (tile == 0))
        | ((kind == 4) & (tile == COLS - 1))
    )
    counts = of_source(jnp.broadcast_to(names[:, COUNT : COUNT + 1], shape))
    energy = of_source(
        jnp.take_along_axis(
            table, jnp.where(lane < USES, ENERGY + shot * BEAMS + beam, lane), axis=1, mode="promise_in_bounds"
        )
    )
    live = (lane < USES) & (beam < counts) & jnp.logical_not(missing)
    owners = jnp.where(live, names // 128, -1)

    per_owner = jnp.concatenate(
        [jnp.sum((owners == o).astype(jnp.float32), axis=0, keepdims=True) for o in range(COLS)], axis=0
    )
    source_beam = lax.rem(lax.broadcasted_iota(jnp.int32, (NS, NS), 0), BEAMS)
    column = lax.broadcasted_iota(jnp.int32, (NS, NS), 1)
    pick = jnp.zeros((NS, NS), jnp.bool_)
    limit = jnp.full(shape, float(LIST))
    for p, (begin, beams, slots, _) in enumerate(PHASES):
        pick = pick | ((column == p) & (source_beam >= begin) & (source_beam < begin + beams))
        limit = jnp.where(lane == p, float(slots), limit)
    held = jnp.dot(per_owner, pick.astype(jnp.float32), preferred_element_type=jnp.float32)
    over = jnp.max((held > limit).astype(jnp.float32), keepdims=True)

    earlier = lax.broadcasted_iota(jnp.int32, (NS, NS), 0) <= column
    above = lax.broadcasted_iota(jnp.int32, (COLS, COLS), 1) < lax.broadcasted_iota(jnp.int32, (COLS, COLS), 0)
    source = tile + (kind == 4).astype(jnp.int32) - (kind == 3).astype(jnp.int32)
    shift = 1 + (kind == 1).astype(jnp.int32) - (kind == 2).astype(jnp.int32)
    place = jnp.full(shape, -1.0)
    record = jnp.zeros(shape, jnp.int32)
    for begin, beams, slots, base in PHASES:
        marks = (owners == col) & (beam >= begin) & (beam < begin + beams)
        ones = marks.astype(jnp.float32)
        within = jnp.dot(ones, earlier.astype(jnp.float32), preferred_element_type=jnp.float32)
        totals = jnp.broadcast_to(jnp.sum(ones, axis=1, keepdims=True), shape)
        ahead = jnp.dot(above.astype(jnp.float32), totals, preferred_element_type=jnp.float32)
        rank = within + ahead - 1.0
        place = jnp.where(marks & (rank < float(slots)), rank + float(base), place)
        record = jnp.where(marks, (shot * COLS + source) * beams + beam - begin, record)
    high = energy.astype(jnp.bfloat16).astype(jnp.float32)
    middle = (energy - high).astype(jnp.bfloat16).astype(jnp.float32)
    low = energy - high - middle
    fields = (
        lax.rem(names, 128).astype(jnp.float32),
        record.astype(jnp.float32),
        (tile * 8 + shift + 1).astype(jnp.float32),
        high,
        middle,
        low,
    )
    upright = jnp.transpose(place)
    slot = lax.broadcasted_iota(jnp.int32, (NS, SLOTS), 1).astype(jnp.float32)
    line = lax.broadcasted_iota(jnp.int32, (8, NS), 0)
    listed = jnp.zeros((8, SLOTS), jnp.float32)
    for t in range(COLS):
        here = (jnp.broadcast_to(upright[:, t : t + 1], (NS, SLOTS)) == slot).astype(jnp.bfloat16)
        rows = jnp.zeros((8, NS), jnp.float32)
        for f, field in enumerate(fields):
            rows = jnp.where(line == f, jnp.broadcast_to(field[t : t + 1, :], (8, NS)), rows)
        listed += jnp.dot(rows.astype(jnp.bfloat16), here, preferred_element_type=jnp.float32)
    return listed, listed[3:4] + listed[4:5] + listed[5:6], jnp.broadcast_to(over, (8, NS))


def fused(records, owner, block, count, travel, amp):
    vmem = pl.BlockSpec(memory_space=pltpu.VMEM)
    smem = pl.BlockSpec(memory_space=pltpu.SMEM)
    hbm = pl.BlockSpec(memory_space=pl.ANY)
    dma = pltpu.SemaphoreType.DMA
    f32 = jnp.float32
    many = COPIES * len(PHASES)
    return pl.pallas_call(
        fused_kernel,
        out_shape=(jax.ShapeDtypeStruct((1, 1, NS), f32), jax.ShapeDtypeStruct((1,), jnp.int32)),
        in_specs=[vmem, vmem, vmem, smem, hbm, hbm],
        out_specs=(vmem, smem),
        scratch_shapes=[
            pltpu.VMEM(((SHOTS * NP + 1) * BEAMS, NS), f32),
            *[pltpu.VMEM((SHOTS * COLS * beams, NP, NS), jnp.bfloat16) for _, beams, _, _ in PHASES],
            pltpu.VMEM(travel.shape, f32),
            pltpu.VMEM(amp.shape, f32),
            pltpu.VMEM((8, NS), f32),
            pltpu.VMEM((2, 8, NS), f32),
            pltpu.VMEM((8, NS), f32),
            pltpu.VMEM((COLS, 8, NS), f32),
            pltpu.VMEM((8, SLOTS), jnp.int32),
            pltpu.SMEM((8, SLOTS), jnp.int32),
            *[pltpu.VMEM((9 * slots, NS), f32) for _, _, slots, _ in PHASES],
            *[pltpu.VMEM((9 * slots, NS), f32) for _, _, slots, _ in PHASES],
            pltpu.VMEM((8, NS), f32),
            pltpu.VMEM((ROWS, 8, NS), f32),
            pltpu.VMEM((COLS, 8, NS), f32),
            pltpu.VMEM((COLS, 8, NS), f32),
            pltpu.VMEM((8, NS), f32),
            pltpu.VMEM((2, 8, NS), f32),
            dma((3,)),
            dma((many,)),
            dma((many,)),
            dma((2,)),
            dma((2,)),
            dma((COLS,)),
            dma((COLS,)),
            dma((ROWS,)),
            dma((ROWS,)),
            dma((COLS,)),
            dma((COLS,)),
            dma((2,)),
            dma((2,)),
        ],
        compiler_params=pltpu.CompilerParams(
            collective_id=0, has_side_effects=True, vmem_limit_bytes=40 << 20
        ),
        cost_estimate=pl.CostEstimate(flops=10_000_000, bytes_accessed=16_000_000, transcendentals=0),
        name="migrate",
    )(records, owner, block, count, travel, amp)


def per_device(records, beam_count, owner_list, block_list, travel_table, amp_table):
    travel_table = pltpu.with_memory_space_constraint(travel_table, pltpu.HBM)
    amp_table = pltpu.with_memory_space_constraint(amp_table, pltpu.HBM)
    by_slowness = records.reshape(SHOTS, BEAMS, NP, NS).transpose(0, 2, 1, 3)
    owner, block = owner_list.reshape(1, USES), block_list.reshape(1, USES)
    quick, flag = fused(by_slowness, owner, block, beam_count, travel_table, amp_table)
    return lax.cond(
        flag[0] > 0,
        lambda: imaged_by_any_count(records, beam_count, owner_list, block_list, travel_table, amp_table),
        lambda: quick,
    )


def solution(mesh):
    placed = (
        P(None, "inline", "xline", None, None),
        P("inline", "xline"),
        P(("inline", "xline"), None),
        P(("inline", "xline"), None),
        P("xline", None, None),
        P("xline", None, None),
    )
    return jax.shard_map(
        per_device,
        mesh=mesh,
        in_specs=placed,
        out_specs=P("inline", "xline", None),
        check_vma=False,
    )
```

```python
import jax
import jax.numpy as jnp
from jax import lax
from jax.experimental import pallas as pl
from jax.experimental.pallas import tpu as pltpu
from jax.sharding import PartitionSpec as P

NS = 128
NP = 64
BEAMS = 8
SHOTS = 2
RECS = SHOTS * BEAMS
SIDE = 4
COLS = SIDE * SIDE
ROWS = 8
USES = 5 * RECS
LIST = 512
TARGETS = 3 * COLS
GROUP = 8
MESH = pl.DeviceIdType.MESH

ENERGY = USES
COUNT = USES + RECS


def greet(row, col):
    barrier = pltpu.get_barrier_semaphore()
    for other in range(1, COLS):
        pl.semaphore_signal(
            barrier, inc=1, device_id=(row, lax.rem(col + other, COLS)), device_id_type=MESH
        )

    @pl.when(row > 0)
    def _():
        pl.semaphore_signal(barrier, inc=1, device_id=(row - 1, col), device_id_type=MESH)

    @pl.when(row < ROWS - 1)
    def _():
        pl.semaphore_signal(barrier, inc=1, device_id=(row + 1, col), device_id_type=MESH)

    edges = (row > 0).astype(jnp.int32) + (row < ROWS - 1).astype(jnp.int32)
    pl.semaphore_wait(barrier, COLS - 1 + edges)


def gather_kernel(
    records, index, travel, amp,
    held, travel_out, amp_out, uses_out, index_out,
    near, mixed, lines, uses_vmem, index_vmem,
    local_sems, send_sems, recv_sems, near_send, near_recv, line_send, line_recv,
):
    row, col = lax.axis_index("inline"), lax.axis_index("xline")
    z, x = col // SIDE, lax.rem(col, SIDE)
    loads = [
        pltpu.make_async_copy(travel, travel_out, local_sems.at[0]),
        pltpu.make_async_copy(amp, amp_out, local_sems.at[1]),
        pltpu.make_async_copy(records, held.at[pl.ds(col * RECS, RECS)], local_sems.at[2]),
    ]
    near[...] = jnp.zeros_like(near)
    greet(row, col)

    def at(dz, dx):
        return lax.rem(z + dz + SIDE, SIDE) * SIDE + lax.rem(x + dx + SIDE, SIDE)

    started = {}

    def block(route, first, second, lo, size):
        tile = at(second, first) if route == 0 else at(first, second)
        return pl.ds(tile * RECS + route * BEAMS + lo, size)

    def toward(route, axis, step):
        along_x = (axis == 0) == (route == 0)
        return (row, at(0, step) if along_x else at(step, 0))

    def send(key, route, axis, step, first, second, lo, size):
        here = block(route, first, second, lo, size)
        n = len(started)
        if first == 0 and second == 0:
            source = records.at[pl.ds(route * BEAMS + lo, size)]
        else:
            source = held.at[here]
        copy = pltpu.make_async_remote_copy(
            src_ref=source,
            dst_ref=held.at[here],
            send_sem=send_sems.at[n],
            recv_sem=recv_sems.at[n],
            device_id=toward(route, axis, step),
            device_id_type=MESH,
        )
        copy.start()
        started[key] = copy

    half = BEAMS // 2
    both = (0, 1)
    for route in both:
        for step in (1, -1):
            send(("a", route, step), route, 0, step, 0, 0, 0, BEAMS)
    for route in both:
        for step in (1, -1):
            send(("c", route, 0, step), route, 1, step, 0, 0, 0, BEAMS)
    for copy in loads:
        copy.start()

    up = pltpu.make_async_remote_copy(
        index, near.at[0], near_send.at[0], near_recv.at[0], device_id=(row + 1, col), device_id_type=MESH
    )
    down = pltpu.make_async_remote_copy(
        index, near.at[1], near_send.at[1], near_recv.at[1], device_id=(row - 1, col), device_id_type=MESH
    )
    @pl.when(row < ROWS - 1)
    def _():
        up.start()

    @pl.when(row > 0)
    def _():
        down.start()

    @pl.when(row > 0)
    def _():
        up.wait_recv()

    @pl.when(row < ROWS - 1)
    def _():
        down.wait_recv()

    @pl.when(row < ROWS - 1)
    def _():
        up.wait_send()

    @pl.when(row > 0)
    def _():
        down.wait_send()

    kind = lax.broadcasted_iota(jnp.int32, (8, NS), 1) // RECS
    mixed[...] = jnp.where(kind == 1, near[1], jnp.where(kind == 2, near[0], index[...]))
    shares = []
    for other in range(1, COLS):
        share = pltpu.make_async_remote_copy(
            mixed,
            lines.at[other],
            line_send.at[other],
            line_recv.at[other],
            device_id=(row, lax.rem(col + other, COLS)),
            device_id_type=MESH,
        )
        share.start()
        shares.append(share)
    lines[0] = mixed[...]

    for route in both:
        for step in (1, -1):
            started["a", route, step].wait_recv()
            lo = 0 if step > 0 else half
            send(("b", route, step), route, 0, step, -step, 0, lo, half)
            for way in (1, -1):
                send(("c", route, -step, way), route, 1, way, -step, 0, 0, BEAMS)
    for route in both:
        for way in (1, -1):
            started["c", route, 0, way].wait_recv()
            lo = 0 if way > 0 else half
            send(("d", route, 0, way), route, 1, way, 0, -way, lo, half)

    build_list(row, col, shares, lines, index_vmem, uses_vmem)

    for route in both:
        for step in (1, -1):
            started["b", route, step].wait_recv()
        for way in (1, -1):
            send(("c", route, 2, way), route, 1, way, 2, 0, 0, BEAMS)
    for first in (-1, 1, 2):
        for route in both:
            for way in (1, -1):
                started["c", route, first, way].wait_recv()
                lo = 0 if way > 0 else half
                send(("d", route, first, way), route, 1, way, first, -way, lo, half)
    finish = [
        pltpu.make_async_copy(uses_vmem, uses_out, local_sems.at[3]),
        pltpu.make_async_copy(index_vmem, index_out, local_sems.at[4]),
    ]
    for copy in finish:
        copy.start()
    for first in (0, -1, 1, 2):
        for route in both:
            for way in (1, -1):
                started["d", route, first, way].wait_recv()
    for copy in started.values():
        copy.wait_send()
    for share in shares:
        share.wait_send()
    for copy in loads + finish:
        copy.wait()


def build_list(row, col, shares, lines, index_vmem, uses_vmem):
    for share in shares:
        share.wait_recv()
    for tile in range(COLS):
        index_vmem[pl.ds(tile, 1), :] = lines[lax.rem(col - tile + COLS, COLS)][0:1, :]
    table = index_vmem[...]
    names = table.astype(jnp.int32)
    shape = (COLS, NS)
    lane = lax.broadcasted_iota(jnp.int32, shape, 1)
    tile = lax.broadcasted_iota(jnp.int32, shape, 0)
    kind, beam = lane // RECS, lax.rem(lane, BEAMS)
    counts = jnp.broadcast_to(names[:, COUNT : COUNT + 1], shape)
    before = jnp.where(tile > 0, pltpu.roll(counts, 1, 0), 0)
    after = jnp.where(tile < COLS - 1, pltpu.roll(counts, COLS - 1, 0), 0)
    last, first = (row == ROWS - 1).astype(jnp.int32), (row == 0).astype(jnp.int32)
    live = jnp.where(kind == 3, before, jnp.where(kind == 4, after, counts))
    live = jnp.where(kind == 1, counts * (1 - last), live)
    live = jnp.where(kind == 2, counts * (1 - first), live)
    wanted = (lane < USES) & (beam < live) & (names // 128 == col)
    marks = wanted.astype(jnp.float32)
    earlier = lax.broadcasted_iota(jnp.int32, (NS, NS), 0) <= lax.broadcasted_iota(jnp.int32, (NS, NS), 1)
    within = jnp.dot(marks, earlier.astype(jnp.float32), preferred_element_type=jnp.float32)
    above = lax.broadcasted_iota(jnp.int32, (COLS, COLS), 1) < lax.broadcasted_iota(jnp.int32, (COLS, COLS), 0)
    totals = jnp.broadcast_to(jnp.sum(marks, axis=1, keepdims=True), shape)
    ahead = jnp.dot(above.astype(jnp.float32), totals, preferred_element_type=jnp.float32)
    place = jnp.where(wanted, within + ahead - 1.0, -1.0)
    number = jnp.sum(marks)

    source = tile + (kind == 4).astype(jnp.int32) - (kind == 3).astype(jnp.int32)
    shift = 1 + (kind == 1).astype(jnp.int32) - (kind == 2).astype(jnp.int32)
    fields = (
        lax.rem(names, 128).astype(jnp.float32),
        (source * RECS + lax.rem(lane, RECS)).astype(jnp.float32),
        (shift * COLS + tile).astype(jnp.float32),
    )
    upright = jnp.transpose(place)
    slot = lax.broadcasted_iota(jnp.int32, (NS, LIST), 1).astype(jnp.float32)
    line = lax.broadcasted_iota(jnp.int32, (8, NS), 0)
    listed = jnp.zeros((8, LIST), jnp.float32)
    for t in range(COLS):
        here = (jnp.broadcast_to(upright[:, t : t + 1], (NS, LIST)) == slot).astype(jnp.bfloat16)
        rows = jnp.zeros((8, NS), jnp.float32)
        for f, field in enumerate(fields):
            rows = jnp.where(line == f, jnp.broadcast_to(field[t : t + 1, :], (8, NS)), rows)
        listed += jnp.dot(rows.astype(jnp.bfloat16), here, preferred_element_type=jnp.float32)
    place_in = lax.broadcasted_iota(jnp.int32, (8, LIST), 1).astype(jnp.float32)
    part = lax.broadcasted_iota(jnp.int32, (8, LIST), 0)
    listed = jnp.where((part == 2) & (place_in >= number), float(TARGETS), listed)
    listed = jnp.where(part == 3, number, listed)
    uses_vmem[...] = listed.astype(jnp.int32)


def gather(records, index, travel, amp):
    hbm = pl.BlockSpec(memory_space=pl.ANY)
    vmem = pl.BlockSpec(memory_space=pltpu.VMEM)
    smem = pl.BlockSpec(memory_space=pltpu.SMEM)
    return pl.pallas_call(
        gather_kernel,
        out_shape=(
            pltpu.VMEM((COLS * RECS, NP, NS), jnp.bfloat16),
            pltpu.VMEM(travel.shape, jnp.float32),
            pltpu.VMEM(amp.shape, jnp.float32),
            jax.ShapeDtypeStruct((8, LIST), jnp.int32),
            jax.ShapeDtypeStruct((COLS, NS), jnp.float32),
        ),
        in_specs=[hbm, vmem, hbm, hbm],
        out_specs=(vmem, vmem, vmem, hbm, hbm),
        scratch_shapes=[
            pltpu.VMEM((2, 8, NS), jnp.float32),
            pltpu.VMEM((8, NS), jnp.float32),
            pltpu.VMEM((COLS, 8, NS), jnp.float32),
            pltpu.VMEM((8, LIST), jnp.int32),
            pltpu.VMEM((COLS, NS), jnp.float32),
            pltpu.SemaphoreType.DMA((5,)),
            pltpu.SemaphoreType.DMA((40,)),
            pltpu.SemaphoreType.DMA((40,)),
            pltpu.SemaphoreType.DMA((2,)),
            pltpu.SemaphoreType.DMA((2,)),
            pltpu.SemaphoreType.DMA((COLS,)),
            pltpu.SemaphoreType.DMA((COLS,)),
        ],
        compiler_params=pltpu.CompilerParams(
            collective_id=1, has_side_effects=True, vmem_limit_bytes=32 << 20
        ),
        cost_estimate=pl.CostEstimate(flops=10_000_000, bytes_accessed=16_000_000, transcendentals=0),
        name="gather_records",
    )(records, index, travel, amp)


def image_kernel(uses, index, records, travel, amp, out, acc):
    acc[...] = jnp.zeros_like(acc)

    def step(i, carry):
        picked = []
        for d in range(GROUP):
            u = i * GROUP + d
            picked.append((uses[0, u], uses[1, u], uses[2, u]))
        totals = [jnp.zeros((8, NS), jnp.float32) for _ in picked]
        squares = [jnp.zeros((8, NS), jnp.float32) for _ in picked]
        for q in range(NP // 8):
            rows = pl.ds(8 * q, 8)
            for d, (block, rec, _) in enumerate(picked):
                t = travel[block, rows, :]
                a = amp[block, rows, :]
                pair = records[rec, pl.ds(16 * (q // 2), 16), :].astype(jnp.float32)
                r = pair[8 * (q % 2) : 8 * (q % 2) + 8]
                k = t.astype(jnp.int32)
                f = t - k.astype(jnp.float32)
                w0 = (1.0 - f).astype(jnp.bfloat16).astype(jnp.float32)
                w1 = f.astype(jnp.bfloat16).astype(jnp.float32)
                v0 = jnp.take_along_axis(r, k, axis=1, mode="promise_in_bounds")
                v1 = jnp.take_along_axis(r, k + 1, axis=1, mode="promise_in_bounds")
                totals[d] += a * (v0 * w0 + v1 * w1)
                squares[d] += a * a
        for d, (_, rec, target) in enumerate(picked):
            energy = index[rec // RECS, ENERGY + lax.rem(rec, RECS)]
            acc[target, 0] += totals[d]
            acc[target, 1] += squares[d] * energy
        return carry

    lax.fori_loop(0, (uses[3, 0] + GROUP - 1) // GROUP, step, 0)
    out[...] = jnp.sum(acc[pl.ds(0, TARGETS)], axis=2)


def image(uses, index, records, travel, amp):
    vmem = pl.BlockSpec(memory_space=pltpu.VMEM)
    smem = pl.BlockSpec(memory_space=pltpu.SMEM)
    return pl.pallas_call(
        image_kernel,
        out_shape=pltpu.VMEM((TARGETS, 2, NS), jnp.float32),
        in_specs=[smem, smem, vmem, vmem, vmem],
        out_specs=vmem,
        scratch_shapes=[pltpu.VMEM((TARGETS + 1, 2, 8, NS), jnp.float32)],
        compiler_params=pltpu.CompilerParams(vmem_limit_bytes=32 << 20),
        cost_estimate=pl.CostEstimate(flops=10_000_000, bytes_accessed=8_000_000, transcendentals=0),
        name="image_uses",
    )(uses, index, records, travel, amp)


def exchange_kernel(sums, out, near, total, parts, near_send, near_recv, part_send, part_recv):
    row, col = lax.axis_index("inline"), lax.axis_index("xline")
    greet(row, col)
    up = pltpu.make_async_remote_copy(
        sums.at[2], near.at[0], near_send.at[0], near_recv.at[0], device_id=(row + 1, col), device_id_type=MESH
    )
    down = pltpu.make_async_remote_copy(
        sums.at[0], near.at[1], near_send.at[1], near_recv.at[1], device_id=(row - 1, col), device_id_type=MESH
    )

    @pl.when(row < ROWS - 1)
    def _():
        up.start()

    @pl.when(row > 0)
    def _():
        down.start()

    total[...] = sums[1]

    @pl.when(row > 0)
    def _():
        up.wait_recv()
        total[...] += near[0]

    @pl.when(row < ROWS - 1)
    def _():
        down.wait_recv()
        total[...] += near[1]

    copies = []
    for other in range(1, COLS):
        there = lax.rem(col + other, COLS)
        copy = pltpu.make_async_remote_copy(
            total.at[there],
            parts.at[other],
            part_send.at[other],
            part_recv.at[other],
            device_id=(row, there),
            device_id_type=MESH,
        )
        copy.start()
        copies.append(copy)
    mine = total[col]
    for copy, other in zip(copies, range(1, COLS)):
        copy.wait_recv()
        mine += parts[other]
    out[0] = mine[0:1] / jnp.sqrt(1.0 + mine[1:2])
    for copy in copies:
        copy.wait_send()

    @pl.when(row < ROWS - 1)
    def _():
        up.wait_send()

    @pl.when(row > 0)
    def _():
        down.wait_send()


def exchange(sums):
    vmem = pl.BlockSpec(memory_space=pltpu.VMEM)
    return pl.pallas_call(
        exchange_kernel,
        out_shape=jax.ShapeDtypeStruct((1, 1, NS), jnp.float32),
        in_specs=[vmem],
        out_specs=vmem,
        scratch_shapes=[
            pltpu.VMEM((2, COLS, 2, NS), jnp.float32),
            pltpu.VMEM((COLS, 2, NS), jnp.float32),
            pltpu.VMEM((COLS, 2, NS), jnp.float32),
            pltpu.SemaphoreType.DMA((2,)),
            pltpu.SemaphoreType.DMA((2,)),
            pltpu.SemaphoreType.DMA((COLS,)),
            pltpu.SemaphoreType.DMA((COLS,)),
        ],
        compiler_params=pltpu.CompilerParams(collective_id=2, has_side_effects=True),
        cost_estimate=pl.CostEstimate(flops=10_000, bytes_accessed=100_000, transcendentals=0),
        name="exchange_sums",
    )(sums)


def imaged_by_any_count(records, beam_count, owner_list, block_list, travel_table, amp_table):
    records = records.reshape(RECS, NP, NS)
    named = (owner_list * 128 + block_list)[:, 0].astype(jnp.float32)
    named = named.reshape(SHOTS, 5, BEAMS).transpose(1, 0, 2).reshape(USES)
    energy = jnp.mean(jnp.square(records.astype(jnp.float32)), axis=(1, 2))
    count = jnp.broadcast_to(beam_count[0].astype(jnp.float32), (NS - COUNT,))
    index = jnp.broadcast_to(jnp.concatenate([named, energy, count]), (8, NS))
    gathered, travel, amp, uses, index = gather(records, index, travel_table, amp_table)
    sums = image(uses, index, gathered, travel, amp)
    return exchange(sums.reshape(3, COLS, 2, NS))


CLASSES = (
    (((0, 0), (1, 0), (-1, 0), (2, 0)), 56, 0, 64),
    (((0, 1), (0, -1), (1, 1), (1, -1), (-1, 1), (-1, -1)), 80, 64, 128),
    (((2, 1), (2, -1), (0, 2)), 40, 144, 64),
    (((1, 2), (-1, 2)), 32, 184, 32),
    (((2, 2),), 24, 216, 16),
)
WHERE = {tile: (c, n) for c, (tiles, _, _, _) in enumerate(CLASSES) for n, tile in enumerate(tiles)}
SLOTS = 256
NBLOCKS = 128
COPIES = 40


def wrap(steps):
    return (steps + 1) % SIDE - 1


def fused_kernel(
    records, owner, block, count, travel, amp,
    out, flag_out,
    wide, buf0, buf1, buf2, buf3, buf4, travel_v, amp_v,
    mine, near, mixed, lines, uses_v, uses_s,
    con0, con1, con2, con3, con4, lit0, lit1, lit2, lit3, lit4,
    flag_mine, flags, sums, parts, edge, edges,
    local_sems, send_sems, recv_sems, near_send, near_recv, line_send, line_recv,
    flag_send, flag_recv, part_send, part_recv, edge_send, edge_recv,
):
    row, col = lax.axis_index("inline"), lax.axis_index("xline")
    z, x = col // SIDE, lax.rem(col, SIDE)
    bufs = (buf0, buf1, buf2, buf3, buf4)
    cons, lits = (con0, con1, con2, con3, con4), (lit0, lit1, lit2, lit3, lit4)
    near[...] = jnp.zeros_like(near)
    edges[...] = jnp.zeros_like(edges)

    barrier = pltpu.get_barrier_semaphore()
    for other in range(1, COLS):
        there = (row, lax.rem(col + other, COLS))
        pl.semaphore_signal(barrier, inc=1, device_id=there, device_id_type=MESH)
    for other in range(1, ROWS):
        there = (lax.rem(row + other, ROWS), col)
        pl.semaphore_signal(barrier, inc=1, device_id=there, device_id_type=MESH)

    loads = [
        pltpu.make_async_copy(travel, travel_v, local_sems.at[0]),
        pltpu.make_async_copy(amp, amp_v, local_sems.at[1]),
    ]
    for copy in loads:
        copy.start()

    wide[pl.ds(0, SHOTS * NP * BEAMS), :] = records[...].astype(jnp.float32).reshape(SHOTS * NP * BEAMS, NS)
    energies = jnp.zeros((8, NS), jnp.float32)
    lane8 = lax.broadcasted_iota(jnp.int32, (8, NS), 1)
    for s in range(SHOTS):
        for b in range(BEAMS):
            rec = wide[pl.ds(s * NP * BEAMS + b, NP, stride=BEAMS), :]
            bufs[0][row_of(s, 0, 0) + b] = rec.astype(jnp.bfloat16)
            energy = jnp.sum(rec * rec, keepdims=True) * (1.0 / (NP * NS))
            energies = jnp.where(lane8 == ENERGY + s * BEAMS + b, jnp.broadcast_to(energy, (8, NS)), energies)
    named = (owner[...] * 128 + block[...]).astype(jnp.float32)
    mine[...] = jnp.where(lane8 >= COUNT, count[0, 0].astype(jnp.float32), energies)
    mine[:, 0:USES] = jnp.broadcast_to(named, (8, USES))
    pl.semaphore_wait(barrier, COLS + ROWS - 2)

    def at(dz, dx):
        return lax.rem(z + dz + SIDE, SIDE) * SIDE + lax.rem(x + dx + SIDE, SIDE)

    started = {}

    def send(kind, route, axis, step, first, second, lo, size):
        seen = (wrap(first - step), second) if axis == 0 else (first, wrap(second - step))
        here, there = WHERE[first, second][0], WHERE[seen][0]
        along_x = (axis == 0) == (route == 0)
        n = len(started)
        copy = pltpu.make_async_remote_copy(
            src_ref=bufs[here].at[pl.ds(row_of(route, first, second) + lo, size)],
            dst_ref=bufs[there].at[pl.ds(row_of(route, *seen) + lo, size)],
            send_sem=send_sems.at[n],
            recv_sem=recv_sems.at[n],
            device_id=(row, at(0, step) if along_x else at(step, 0)),
            device_id_type=MESH,
        )
        copy.start()
        key = (kind, route, step) if axis == 0 else (kind, route, first, step)
        started[key] = copy

    both, ways = (0, 1), (1, -1)
    half = BEAMS // 2

    def along_second(first):
        for way in ways:
            for route in both:
                send("c", route, 1, way, first, 0, 0, BEAMS)

    def pass_on(first):
        for way in ways:
            for route in both:
                started["c", route, first, way].wait_recv()
                send("d", route, 1, way, first, -way, 0 if way > 0 else half, half)

    def arrived(first):
        for route in both:
            for way in ways:
                started["d", route, first, way].wait_recv()

    def image_some(p, begin, end):
        _, slots, base, held = CLASSES[p]
        buf, con, lit = bufs[p], cons[p], lits[p]

        def step(i, carry):
            places = [base + i * GROUP + d for d in range(GROUP)]
            picked = [(uses_s[0, u] & (NBLOCKS - 1), uses_s[1, u] & (held - 1)) for u in places]
            totals = [jnp.zeros((8, NS), jnp.float32) for _ in picked]
            squares = [jnp.zeros((8, NS), jnp.float32) for _ in picked]
            for q in range(NP // 8):
                rows = pl.ds(8 * q, 8)
                for d, (number, rec) in enumerate(picked):
                    t = travel_v[number, rows, :]
                    a = amp_v[number, rows, :]
                    pair = buf[rec, pl.ds(16 * (q // 2), 16), :].astype(jnp.float32)
                    r = pair[8 * (q % 2) : 8 * (q % 2) + 8]
                    k = t.astype(jnp.int32)
                    f = t - k.astype(jnp.float32)
                    w0 = (1.0 - f).astype(jnp.bfloat16).astype(jnp.float32)
                    w1 = f.astype(jnp.bfloat16).astype(jnp.float32)
                    v0 = jnp.take_along_axis(r, k, axis=1, mode="promise_in_bounds")
                    v1 = jnp.take_along_axis(r, k + 1, axis=1, mode="promise_in_bounds")
                    totals[d] += a * (v0 * w0 + v1 * w1)
                    squares[d] += a * a
            for d in range(GROUP):
                con[pl.ds(i * GROUP + d, 8, stride=slots), :] = totals[d]
                lit[pl.ds(i * GROUP + d, 8, stride=slots), :] = squares[d]
            return carry

        lax.fori_loop(begin // GROUP, end // GROUP, step, 0)

    def total_of(p, listed, energy):
        _, slots, base, _ = CLASSES[p]
        con = sum(cons[p][pl.ds(s * slots, slots), :] for s in range(8))
        lit = sum(lits[p][pl.ds(s * slots, slots), :] for s in range(8))
        target = jnp.broadcast_to(listed[2:3, base : base + slots], (NS, slots))
        weight = jnp.broadcast_to(energy[:, base : base + slots], (NS, slots))
        line = (lax.broadcasted_iota(jnp.int32, (NS, slots), 0) + 1).astype(jnp.float32)
        to_con = jnp.where(target == line, 1.0, 0.0)
        to_lit = jnp.where((target + 4.0 == line) & (target > 0.0), weight, 0.0)
        dot = lambda m, v: jnp.dot(m, v, precision=lax.Precision.HIGHEST, preferred_element_type=jnp.float32)
        return dot(to_con, con) + dot(to_lit, lit)

    for step in ways:
        for route in both:
            send("a", route, 0, step, 0, 0, 0, BEAMS)
    along_second(0)

    up = pltpu.make_async_remote_copy(
        mine, near.at[0], near_send.at[0], near_recv.at[0], device_id=(row + 1, col), device_id_type=MESH
    )
    down = pltpu.make_async_remote_copy(
        mine, near.at[1], near_send.at[1], near_recv.at[1], device_id=(row - 1, col), device_id_type=MESH
    )
    upward, downward = pl.when(row < ROWS - 1), pl.when(row > 0)
    upward(up.start)
    downward(down.start)
    downward(up.wait_recv)
    upward(down.wait_recv)
    kind8 = lax.rem(lane8, 5 * BEAMS) // BEAMS
    kind8 = jnp.where(lane8 < USES, kind8, 0)
    mixed[...] = jnp.where(kind8 == 1, near[1], jnp.where(kind8 == 2, near[0], mine[...]))
    shares = []
    for other in range(1, COLS):
        share = pltpu.make_async_remote_copy(
            mixed, lines.at[other], line_send.at[other], line_recv.at[other],
            device_id=(row, lax.rem(col + other, COLS)), device_id_type=MESH,
        )
        share.start()
        shares.append(share)
    lines[0] = mixed[...]

    for step in ways:
        for route in both:
            started["a", route, step].wait_recv()
            send("b", route, 0, step, -step, 0, 0 if step > 0 else half, half)
        along_second(-step)

    for share in shares:
        share.wait_recv()
    listed, energy, over = list_uses(row, col, lines)
    uses_v[...] = listed.astype(jnp.int32)
    to_smem = pltpu.make_async_copy(uses_v, uses_s, local_sems.at[2])
    to_smem.start()
    flag_mine[...] = over
    alarms = []
    for other in range(1, ROWS):
        alarm = pltpu.make_async_remote_copy(
            flag_mine, flags.at[other], flag_send.at[other], flag_recv.at[other],
            device_id=(lax.rem(row + other, ROWS), col), device_id_type=MESH,
        )
        alarm.start()
        alarms.append(alarm)

    pass_on(0)
    for route in both:
        for step in ways:
            started["b", route, step].wait_recv()
    along_second(2)
    to_smem.wait()
    for copy in loads:
        copy.wait()
    image_some(0, 0, 56)
    pass_on(1)
    pass_on(-1)
    image_some(1, 0, 80)
    pass_on(2)
    arrived(0)
    image_some(2, 0, 40)
    early = total_of(0, listed, energy) + total_of(1, listed, energy) + total_of(2, listed, energy)
    raised = flag_mine[...]
    for alarm, other in zip(alarms, range(1, ROWS)):
        alarm.wait_recv()
        raised = jnp.maximum(raised, flags[other])
    flag_out[0] = jnp.max(raised).astype(jnp.int32)
    arrived(1)
    arrived(-1)
    image_some(3, 0, 32)
    early += total_of(3, listed, energy)
    arrived(2)
    image_some(4, 0, 24)
    sums[...] = (early + total_of(4, listed, energy)).reshape(COLS, 8, NS)

    pieces = []
    for other in range(1, COLS):
        there = lax.rem(col + other, COLS)
        piece = pltpu.make_async_remote_copy(
            sums.at[there], parts.at[other], part_send.at[other], part_recv.at[other],
            device_id=(row, there), device_id_type=MESH,
        )
        piece.start()
        pieces.append(piece)
    whole = sums[col]
    for piece, other in zip(pieces, range(1, COLS)):
        piece.wait_recv()
        whole += parts[other]
    edge[...] = whole
    to_next = pltpu.make_async_remote_copy(
        edge, edges.at[0], edge_send.at[0], edge_recv.at[0], device_id=(row + 1, col), device_id_type=MESH
    )
    to_prev = pltpu.make_async_remote_copy(
        edge, edges.at[1], edge_send.at[1], edge_recv.at[1], device_id=(row - 1, col), device_id_type=MESH
    )
    upward(to_next.start)
    downward(to_prev.start)
    for copy in started.values():
        copy.wait_send()
    for copy in shares + alarms + pieces:
        copy.wait_send()
    upward(up.wait_send)
    downward(down.wait_send)
    downward(to_next.wait_recv)
    upward(to_prev.wait_recv)
    contrib = whole[1:2] + edges[0][2:3] + edges[1][0:1]
    lighting = whole[5:6] + edges[0][6:7] + edges[1][4:5]
    out[0] = contrib / jnp.sqrt(1.0 + lighting)
    upward(to_next.wait_send)
    downward(to_prev.wait_send)


def row_of(route, first, second):
    c, n = WHERE[first, second]
    return (route * len(CLASSES[c][0]) + n) * BEAMS


def list_uses(row, col, lines):
    table = jnp.concatenate([lines[lax.rem(col - tile + COLS, COLS)][0:1, :] for tile in range(COLS)], axis=0)
    shape = (COLS, NS)
    lane = lax.broadcasted_iota(jnp.int32, shape, 1)
    tile = lax.broadcasted_iota(jnp.int32, shape, 0)
    shot, kind, beam = lane // (5 * BEAMS), lax.rem(lane, 5 * BEAMS) // BEAMS, lax.rem(lane, BEAMS)
    names = table.astype(jnp.int32)

    def of_source(own):
        before, after = pltpu.roll(own, 1, 0), pltpu.roll(own, COLS - 1, 0)
        return jnp.where(kind == 3, before, jnp.where(kind == 4, after, own))

    last, first = (row == ROWS - 1).astype(jnp.int32), (row == 0).astype(jnp.int32)
    missing = (
        ((kind == 1) & (last == 1))
        | ((kind == 2) & (first == 1))
        | ((kind == 3) & (tile == 0))
        | ((kind == 4) & (tile == COLS - 1))
    )
    counts = of_source(jnp.broadcast_to(names[:, COUNT : COUNT + 1], shape))
    energy = of_source(
        jnp.take_along_axis(
            table, jnp.where(lane < USES, ENERGY + shot * BEAMS + beam, lane), axis=1, mode="promise_in_bounds"
        )
    )
    live = (lane < USES) & (beam < counts) & jnp.logical_not(missing)
    owners = names // 128

    source = tile + (kind == 4).astype(jnp.int32) - (kind == 3).astype(jnp.int32)
    along_z = (source // SIDE - owners // SIDE) & (SIDE - 1)
    along_x = (source - owners) & (SIDE - 1)
    code = jnp.where(shot == 0, along_x * SIDE + along_z, along_z * SIDE + along_x)
    group, record = jnp.zeros(shape, jnp.int32), jnp.zeros(shape, jnp.int32)
    for (first_step, second_step), (c, _) in WHERE.items():
        same = code == first_step % SIDE * SIDE + second_step % SIDE
        group = jnp.where(same, c, group)
        begin = [row_of(route, first_step, second_step) for route in (0, 1)]
        record = jnp.where(same, jnp.where(shot == 0, begin[0], begin[1]) + beam, record)

    column = lax.broadcasted_iota(jnp.int32, (NS, NS), 1)
    owned = jnp.where(live, owners * 8 + group, -1)
    over = jnp.zeros((1, 1), jnp.float32)
    for c, (_, slots, _, _) in enumerate(CLASSES):
        per_owner = jnp.concatenate(
            [jnp.sum((owned == o * 8 + c).astype(jnp.float32), axis=0, keepdims=True) for o in range(COLS)], axis=0
        )
        held = jnp.sum(per_owner, axis=1, keepdims=True)
        over = jnp.maximum(over, jnp.max((held > float(slots)).astype(jnp.float32), keepdims=True))

    earlier = lax.broadcasted_iota(jnp.int32, (NS, NS), 0) <= column
    above = lax.broadcasted_iota(jnp.int32, (COLS, COLS), 1) < lax.broadcasted_iota(jnp.int32, (COLS, COLS), 0)
    shift = 1 + (kind == 1).astype(jnp.int32) - (kind == 2).astype(jnp.int32)
    place = jnp.full(shape, -1.0)
    for c, (_, slots, base, _) in enumerate(CLASSES):
        marks = live & (owners == col) & (group == c)
        ones = marks.astype(jnp.float32)
        within = jnp.dot(ones, earlier.astype(jnp.float32), preferred_element_type=jnp.float32)
        totals = jnp.broadcast_to(jnp.sum(ones, axis=1, keepdims=True), shape)
        ahead = jnp.dot(above.astype(jnp.float32), totals, preferred_element_type=jnp.float32)
        rank = within + ahead - 1.0
        place = jnp.where(marks & (rank < float(slots)), rank + float(base), place)
    high = energy.astype(jnp.bfloat16).astype(jnp.float32)
    middle = (energy - high).astype(jnp.bfloat16).astype(jnp.float32)
    low = energy - high - middle
    fields = (
        lax.rem(names, 128).astype(jnp.float32),
        record.astype(jnp.float32),
        (tile * 8 + shift + 1).astype(jnp.float32),
        high,
        middle,
        low,
    )
    upright = jnp.transpose(place)
    slot = lax.broadcasted_iota(jnp.int32, (NS, SLOTS), 1).astype(jnp.float32)
    line = lax.broadcasted_iota(jnp.int32, (8, NS), 0)
    listed = jnp.zeros((8, SLOTS), jnp.float32)
    for t in range(COLS):
        here = (jnp.broadcast_to(upright[:, t : t + 1], (NS, SLOTS)) == slot).astype(jnp.bfloat16)
        rows = jnp.zeros((8, NS), jnp.float32)
        for f, field in enumerate(fields):
            rows = jnp.where(line == f, jnp.broadcast_to(field[t : t + 1, :], (8, NS)), rows)
        listed += jnp.dot(rows.astype(jnp.bfloat16), here, preferred_element_type=jnp.float32)
    return listed, listed[3:4] + listed[4:5] + listed[5:6], jnp.broadcast_to(over, (8, NS))


def fused(records, owner, block, count, travel, amp):
    vmem = pl.BlockSpec(memory_space=pltpu.VMEM)
    smem = pl.BlockSpec(memory_space=pltpu.SMEM)
    hbm = pl.BlockSpec(memory_space=pl.ANY)
    dma = pltpu.SemaphoreType.DMA
    f32 = jnp.float32
    return pl.pallas_call(
        fused_kernel,
        out_shape=(jax.ShapeDtypeStruct((1, 1, NS), f32), jax.ShapeDtypeStruct((1,), jnp.int32)),
        in_specs=[vmem, vmem, vmem, smem, hbm, hbm],
        out_specs=(vmem, smem),
        scratch_shapes=[
            pltpu.VMEM(((SHOTS * NP + 1) * BEAMS, NS), f32),
            *[pltpu.VMEM((held, NP, NS), jnp.bfloat16) for _, _, _, held in CLASSES],
            pltpu.VMEM(travel.shape, f32),
            pltpu.VMEM(amp.shape, f32),
            pltpu.VMEM((8, NS), f32),
            pltpu.VMEM((2, 8, NS), f32),
            pltpu.VMEM((8, NS), f32),
            pltpu.VMEM((COLS, 8, NS), f32),
            pltpu.VMEM((8, SLOTS), jnp.int32),
            pltpu.SMEM((8, SLOTS), jnp.int32),
            *[pltpu.VMEM((9 * slots, NS), f32) for _, slots, _, _ in CLASSES],
            *[pltpu.VMEM((9 * slots, NS), f32) for _, slots, _, _ in CLASSES],
            pltpu.VMEM((8, NS), f32),
            pltpu.VMEM((ROWS, 8, NS), f32),
            pltpu.VMEM((COLS, 8, NS), f32),
            pltpu.VMEM((COLS, 8, NS), f32),
            pltpu.VMEM((8, NS), f32),
            pltpu.VMEM((2, 8, NS), f32),
            dma((3,)),
            dma((COPIES,)),
            dma((COPIES,)),
            dma((2,)),
            dma((2,)),
            dma((COLS,)),
            dma((COLS,)),
            dma((ROWS,)),
            dma((ROWS,)),
            dma((COLS,)),
            dma((COLS,)),
            dma((2,)),
            dma((2,)),
        ],
        compiler_params=pltpu.CompilerParams(
            collective_id=0, has_side_effects=True, vmem_limit_bytes=40 << 20
        ),
        cost_estimate=pl.CostEstimate(flops=10_000_000, bytes_accessed=16_000_000, transcendentals=0),
        name="migrate",
    )(records, owner, block, count, travel, amp)


def per_device(records, beam_count, owner_list, block_list, travel_table, amp_table):
    travel_table = pltpu.with_memory_space_constraint(travel_table, pltpu.HBM)
    amp_table = pltpu.with_memory_space_constraint(amp_table, pltpu.HBM)
    by_slowness = records.reshape(SHOTS, BEAMS, NP, NS).transpose(0, 2, 1, 3)
    owner, block = owner_list.reshape(1, USES), block_list.reshape(1, USES)
    quick, flag = fused(by_slowness, owner, block, beam_count, travel_table, amp_table)
    return lax.cond(
        flag[0] > 0,
        lambda: imaged_by_any_count(records, beam_count, owner_list, block_list, travel_table, amp_table),
        lambda: quick,
    )


def solution(mesh):
    placed = (
        P(None, "inline", "xline", None, None),
        P("inline", "xline"),
        P(("inline", "xline"), None),
        P(("inline", "xline"), None),
        P("xline", None, None),
        P("xline", None, None),
    )
    return jax.shard_map(
        per_device,
        mesh=mesh,
        in_specs=placed,
        out_specs=P("inline", "xline", None),
        check_vma=False,
    )
```

```python
import jax
import jax.numpy as jnp
from jax import lax
from jax.experimental import pallas as pl
from jax.experimental.pallas import tpu as pltpu
from jax.sharding import PartitionSpec as P

NS = 128
NP = 64
BEAMS = 8
SHOTS = 2
RECS = SHOTS * BEAMS
SIDE = 4
COLS = SIDE * SIDE
ROWS = 8
USES = 5 * RECS
LIST = 512
TARGETS = 3 * COLS
GROUP = 8
MESH = pl.DeviceIdType.MESH

ENERGY = USES
COUNT = USES + RECS


def greet(row, col):
    barrier = pltpu.get_barrier_semaphore()
    for other in range(1, COLS):
        pl.semaphore_signal(
            barrier, inc=1, device_id=(row, lax.rem(col + other, COLS)), device_id_type=MESH
        )

    @pl.when(row > 0)
    def _():
        pl.semaphore_signal(barrier, inc=1, device_id=(row - 1, col), device_id_type=MESH)

    @pl.when(row < ROWS - 1)
    def _():
        pl.semaphore_signal(barrier, inc=1, device_id=(row + 1, col), device_id_type=MESH)

    edges = (row > 0).astype(jnp.int32) + (row < ROWS - 1).astype(jnp.int32)
    pl.semaphore_wait(barrier, COLS - 1 + edges)


def gather_kernel(
    records, index, travel, amp,
    held, travel_out, amp_out, uses_out, index_out,
    near, mixed, lines, uses_vmem, index_vmem,
    local_sems, send_sems, recv_sems, near_send, near_recv, line_send, line_recv,
):
    row, col = lax.axis_index("inline"), lax.axis_index("xline")
    z, x = col // SIDE, lax.rem(col, SIDE)
    loads = [
        pltpu.make_async_copy(travel, travel_out, local_sems.at[0]),
        pltpu.make_async_copy(amp, amp_out, local_sems.at[1]),
        pltpu.make_async_copy(records, held.at[pl.ds(col * RECS, RECS)], local_sems.at[2]),
    ]
    near[...] = jnp.zeros_like(near)
    greet(row, col)

    def at(dz, dx):
        return lax.rem(z + dz + SIDE, SIDE) * SIDE + lax.rem(x + dx + SIDE, SIDE)

    started = {}

    def block(route, first, second, lo, size):
        tile = at(second, first) if route == 0 else at(first, second)
        return pl.ds(tile * RECS + route * BEAMS + lo, size)

    def toward(route, axis, step):
        along_x = (axis == 0) == (route == 0)
        return (row, at(0, step) if along_x else at(step, 0))

    def send(key, route, axis, step, first, second, lo, size):
        here = block(route, first, second, lo, size)
        n = len(started)
        if first == 0 and second == 0:
            source = records.at[pl.ds(route * BEAMS + lo, size)]
        else:
            source = held.at[here]
        copy = pltpu.make_async_remote_copy(
            src_ref=source,
            dst_ref=held.at[here],
            send_sem=send_sems.at[n],
            recv_sem=recv_sems.at[n],
            device_id=toward(route, axis, step),
            device_id_type=MESH,
        )
        copy.start()
        started[key] = copy

    half = BEAMS // 2
    both = (0, 1)
    for route in both:
        for step in (1, -1):
            send(("a", route, step), route, 0, step, 0, 0, 0, BEAMS)
    for route in both:
        for step in (1, -1):
            send(("c", route, 0, step), route, 1, step, 0, 0, 0, BEAMS)
    for copy in loads:
        copy.start()

    up = pltpu.make_async_remote_copy(
        index, near.at[0], near_send.at[0], near_recv.at[0], device_id=(row + 1, col), device_id_type=MESH
    )
    down = pltpu.make_async_remote_copy(
        index, near.at[1], near_send.at[1], near_recv.at[1], device_id=(row - 1, col), device_id_type=MESH
    )
    @pl.when(row < ROWS - 1)
    def _():
        up.start()

    @pl.when(row > 0)
    def _():
        down.start()

    @pl.when(row > 0)
    def _():
        up.wait_recv()

    @pl.when(row < ROWS - 1)
    def _():
        down.wait_recv()

    @pl.when(row < ROWS - 1)
    def _():
        up.wait_send()

    @pl.when(row > 0)
    def _():
        down.wait_send()

    kind = lax.broadcasted_iota(jnp.int32, (8, NS), 1) // RECS
    mixed[...] = jnp.where(kind == 1, near[1], jnp.where(kind == 2, near[0], index[...]))
    shares = []
    for other in range(1, COLS):
        share = pltpu.make_async_remote_copy(
            mixed,
            lines.at[other],
            line_send.at[other],
            line_recv.at[other],
            device_id=(row, lax.rem(col + other, COLS)),
            device_id_type=MESH,
        )
        share.start()
        shares.append(share)
    lines[0] = mixed[...]

    for route in both:
        for step in (1, -1):
            started["a", route, step].wait_recv()
            lo = 0 if step > 0 else half
            send(("b", route, step), route, 0, step, -step, 0, lo, half)
            for way in (1, -1):
                send(("c", route, -step, way), route, 1, way, -step, 0, 0, BEAMS)
    for route in both:
        for way in (1, -1):
            started["c", route, 0, way].wait_recv()
            lo = 0 if way > 0 else half
            send(("d", route, 0, way), route, 1, way, 0, -way, lo, half)

    build_list(row, col, shares, lines, index_vmem, uses_vmem)

    for route in both:
        for step in (1, -1):
            started["b", route, step].wait_recv()
        for way in (1, -1):
            send(("c", route, 2, way), route, 1, way, 2, 0, 0, BEAMS)
    for first in (-1, 1, 2):
        for route in both:
            for way in (1, -1):
                started["c", route, first, way].wait_recv()
                lo = 0 if way > 0 else half
                send(("d", route, first, way), route, 1, way, first, -way, lo, half)
    finish = [
        pltpu.make_async_copy(uses_vmem, uses_out, local_sems.at[3]),
        pltpu.make_async_copy(index_vmem, index_out, local_sems.at[4]),
    ]
    for copy in finish:
        copy.start()
    for first in (0, -1, 1, 2):
        for route in both:
            for way in (1, -1):
                started["d", route, first, way].wait_recv()
    for copy in started.values():
        copy.wait_send()
    for share in shares:
        share.wait_send()
    for copy in loads + finish:
        copy.wait()


def build_list(row, col, shares, lines, index_vmem, uses_vmem):
    for share in shares:
        share.wait_recv()
    for tile in range(COLS):
        index_vmem[pl.ds(tile, 1), :] = lines[lax.rem(col - tile + COLS, COLS)][0:1, :]
    table = index_vmem[...]
    names = table.astype(jnp.int32)
    shape = (COLS, NS)
    lane = lax.broadcasted_iota(jnp.int32, shape, 1)
    tile = lax.broadcasted_iota(jnp.int32, shape, 0)
    kind, beam = lane // RECS, lax.rem(lane, BEAMS)
    counts = jnp.broadcast_to(names[:, COUNT : COUNT + 1], shape)
    before = jnp.where(tile > 0, pltpu.roll(counts, 1, 0), 0)
    after = jnp.where(tile < COLS - 1, pltpu.roll(counts, COLS - 1, 0), 0)
    last, first = (row == ROWS - 1).astype(jnp.int32), (row == 0).astype(jnp.int32)
    live = jnp.where(kind == 3, before, jnp.where(kind == 4, after, counts))
    live = jnp.where(kind == 1, counts * (1 - last), live)
    live = jnp.where(kind == 2, counts * (1 - first), live)
    wanted = (lane < USES) & (beam < live) & (names // 128 == col)
    marks = wanted.astype(jnp.float32)
    earlier = lax.broadcasted_iota(jnp.int32, (NS, NS), 0) <= lax.broadcasted_iota(jnp.int32, (NS, NS), 1)
    within = jnp.dot(marks, earlier.astype(jnp.float32), preferred_element_type=jnp.float32)
    above = lax.broadcasted_iota(jnp.int32, (COLS, COLS), 1) < lax.broadcasted_iota(jnp.int32, (COLS, COLS), 0)
    totals = jnp.broadcast_to(jnp.sum(marks, axis=1, keepdims=True), shape)
    ahead = jnp.dot(above.astype(jnp.float32), totals, preferred_element_type=jnp.float32)
    place = jnp.where(wanted, within + ahead - 1.0, -1.0)
    number = jnp.sum(marks)

    source = tile + (kind == 4).astype(jnp.int32) - (kind == 3).astype(jnp.int32)
    shift = 1 + (kind == 1).astype(jnp.int32) - (kind == 2).astype(jnp.int32)
    fields = (
        lax.rem(names, 128).astype(jnp.float32),
        (source * RECS + lax.rem(lane, RECS)).astype(jnp.float32),
        (shift * COLS + tile).astype(jnp.float32),
    )
    upright = jnp.transpose(place)
    slot = lax.broadcasted_iota(jnp.int32, (NS, LIST), 1).astype(jnp.float32)
    line = lax.broadcasted_iota(jnp.int32, (8, NS), 0)
    listed = jnp.zeros((8, LIST), jnp.float32)
    for t in range(COLS):
        here = (jnp.broadcast_to(upright[:, t : t + 1], (NS, LIST)) == slot).astype(jnp.bfloat16)
        rows = jnp.zeros((8, NS), jnp.float32)
        for f, field in enumerate(fields):
            rows = jnp.where(line == f, jnp.broadcast_to(field[t : t + 1, :], (8, NS)), rows)
        listed += jnp.dot(rows.astype(jnp.bfloat16), here, preferred_element_type=jnp.float32)
    place_in = lax.broadcasted_iota(jnp.int32, (8, LIST), 1).astype(jnp.float32)
    part = lax.broadcasted_iota(jnp.int32, (8, LIST), 0)
    listed = jnp.where((part == 2) & (place_in >= number), float(TARGETS), listed)
    listed = jnp.where(part == 3, number, listed)
    uses_vmem[...] = listed.astype(jnp.int32)


def gather(records, index, travel, amp):
    hbm = pl.BlockSpec(memory_space=pl.ANY)
    vmem = pl.BlockSpec(memory_space=pltpu.VMEM)
    smem = pl.BlockSpec(memory_space=pltpu.SMEM)
    return pl.pallas_call(
        gather_kernel,
        out_shape=(
            pltpu.VMEM((COLS * RECS, NP, NS), jnp.bfloat16),
            pltpu.VMEM(travel.shape, jnp.float32),
            pltpu.VMEM(amp.shape, jnp.float32),
            jax.ShapeDtypeStruct((8, LIST), jnp.int32),
            jax.ShapeDtypeStruct((COLS, NS), jnp.float32),
        ),
        in_specs=[hbm, vmem, hbm, hbm],
        out_specs=(vmem, vmem, vmem, hbm, hbm),
        scratch_shapes=[
            pltpu.VMEM((2, 8, NS), jnp.float32),
            pltpu.VMEM((8, NS), jnp.float32),
            pltpu.VMEM((COLS, 8, NS), jnp.float32),
            pltpu.VMEM((8, LIST), jnp.int32),
            pltpu.VMEM((COLS, NS), jnp.float32),
            pltpu.SemaphoreType.DMA((5,)),
            pltpu.SemaphoreType.DMA((40,)),
            pltpu.SemaphoreType.DMA((40,)),
            pltpu.SemaphoreType.DMA((2,)),
            pltpu.SemaphoreType.DMA((2,)),
            pltpu.SemaphoreType.DMA((COLS,)),
            pltpu.SemaphoreType.DMA((COLS,)),
        ],
        compiler_params=pltpu.CompilerParams(
            collective_id=1, has_side_effects=True, vmem_limit_bytes=32 << 20
        ),
        cost_estimate=pl.CostEstimate(flops=10_000_000, bytes_accessed=16_000_000, transcendentals=0),
        name="gather_records",
    )(records, index, travel, amp)


def image_kernel(uses, index, records, travel, amp, out, acc):
    acc[...] = jnp.zeros_like(acc)

    def step(i, carry):
        picked = []
        for d in range(GROUP):
            u = i * GROUP + d
            picked.append((uses[0, u], uses[1, u], uses[2, u]))
        totals = [jnp.zeros((8, NS), jnp.float32) for _ in picked]
        squares = [jnp.zeros((8, NS), jnp.float32) for _ in picked]
        for q in range(NP // 8):
            rows = pl.ds(8 * q, 8)
            for d, (block, rec, _) in enumerate(picked):
                t = travel[block, rows, :]
                a = amp[block, rows, :]
                pair = records[rec, pl.ds(16 * (q // 2), 16), :].astype(jnp.float32)
                r = pair[8 * (q % 2) : 8 * (q % 2) + 8]
                k = t.astype(jnp.int32)
                f = t - k.astype(jnp.float32)
                w0 = (1.0 - f).astype(jnp.bfloat16).astype(jnp.float32)
                w1 = f.astype(jnp.bfloat16).astype(jnp.float32)
                v0 = jnp.take_along_axis(r, k, axis=1, mode="promise_in_bounds")
                v1 = jnp.take_along_axis(r, k + 1, axis=1, mode="promise_in_bounds")
                totals[d] += a * (v0 * w0 + v1 * w1)
                squares[d] += a * a
        for d, (_, rec, target) in enumerate(picked):
            energy = index[rec // RECS, ENERGY + lax.rem(rec, RECS)]
            acc[target, 0] += totals[d]
            acc[target, 1] += squares[d] * energy
        return carry

    lax.fori_loop(0, (uses[3, 0] + GROUP - 1) // GROUP, step, 0)
    out[...] = jnp.sum(acc[pl.ds(0, TARGETS)], axis=2)


def image(uses, index, records, travel, amp):
    vmem = pl.BlockSpec(memory_space=pltpu.VMEM)
    smem = pl.BlockSpec(memory_space=pltpu.SMEM)
    return pl.pallas_call(
        image_kernel,
        out_shape=pltpu.VMEM((TARGETS, 2, NS), jnp.float32),
        in_specs=[smem, smem, vmem, vmem, vmem],
        out_specs=vmem,
        scratch_shapes=[pltpu.VMEM((TARGETS + 1, 2, 8, NS), jnp.float32)],
        compiler_params=pltpu.CompilerParams(vmem_limit_bytes=32 << 20),
        cost_estimate=pl.CostEstimate(flops=10_000_000, bytes_accessed=8_000_000, transcendentals=0),
        name="image_uses",
    )(uses, index, records, travel, amp)


def exchange_kernel(sums, out, near, total, parts, near_send, near_recv, part_send, part_recv):
    row, col = lax.axis_index("inline"), lax.axis_index("xline")
    greet(row, col)
    up = pltpu.make_async_remote_copy(
        sums.at[2], near.at[0], near_send.at[0], near_recv.at[0], device_id=(row + 1, col), device_id_type=MESH
    )
    down = pltpu.make_async_remote_copy(
        sums.at[0], near.at[1], near_send.at[1], near_recv.at[1], device_id=(row - 1, col), device_id_type=MESH
    )

    @pl.when(row < ROWS - 1)
    def _():
        up.start()

    @pl.when(row > 0)
    def _():
        down.start()

    total[...] = sums[1]

    @pl.when(row > 0)
    def _():
        up.wait_recv()
        total[...] += near[0]

    @pl.when(row < ROWS - 1)
    def _():
        down.wait_recv()
        total[...] += near[1]

    copies = []
    for other in range(1, COLS):
        there = lax.rem(col + other, COLS)
        copy = pltpu.make_async_remote_copy(
            total.at[there],
            parts.at[other],
            part_send.at[other],
            part_recv.at[other],
            device_id=(row, there),
            device_id_type=MESH,
        )
        copy.start()
        copies.append(copy)
    mine = total[col]
    for copy, other in zip(copies, range(1, COLS)):
        copy.wait_recv()
        mine += parts[other]
    out[0] = mine[0:1] / jnp.sqrt(1.0 + mine[1:2])
    for copy in copies:
        copy.wait_send()

    @pl.when(row < ROWS - 1)
    def _():
        up.wait_send()

    @pl.when(row > 0)
    def _():
        down.wait_send()


def exchange(sums):
    vmem = pl.BlockSpec(memory_space=pltpu.VMEM)
    return pl.pallas_call(
        exchange_kernel,
        out_shape=jax.ShapeDtypeStruct((1, 1, NS), jnp.float32),
        in_specs=[vmem],
        out_specs=vmem,
        scratch_shapes=[
            pltpu.VMEM((2, COLS, 2, NS), jnp.float32),
            pltpu.VMEM((COLS, 2, NS), jnp.float32),
            pltpu.VMEM((COLS, 2, NS), jnp.float32),
            pltpu.SemaphoreType.DMA((2,)),
            pltpu.SemaphoreType.DMA((2,)),
            pltpu.SemaphoreType.DMA((COLS,)),
            pltpu.SemaphoreType.DMA((COLS,)),
        ],
        compiler_params=pltpu.CompilerParams(collective_id=2, has_side_effects=True),
        cost_estimate=pl.CostEstimate(flops=10_000, bytes_accessed=100_000, transcendentals=0),
        name="exchange_sums",
    )(sums)


def imaged_by_any_count(records, beam_count, owner_list, block_list, travel_table, amp_table):
    records = records.reshape(RECS, NP, NS)
    named = (owner_list * 128 + block_list)[:, 0].astype(jnp.float32)
    named = named.reshape(SHOTS, 5, BEAMS).transpose(1, 0, 2).reshape(USES)
    energy = jnp.mean(jnp.square(records.astype(jnp.float32)), axis=(1, 2))
    count = jnp.broadcast_to(beam_count[0].astype(jnp.float32), (NS - COUNT,))
    index = jnp.broadcast_to(jnp.concatenate([named, energy, count]), (8, NS))
    gathered, travel, amp, uses, index = gather(records, index, travel_table, amp_table)
    sums = image(uses, index, gathered, travel, amp)
    return exchange(sums.reshape(3, COLS, 2, NS))


CLASSES = (
    (((0, 0), (1, 0), (-1, 0), (2, 0)), 56, 0, 64),
    (((0, 1), (0, -1), (1, 1), (1, -1), (-1, 1), (-1, -1)), 80, 64, 128),
    (((2, 1), (2, -1), (0, 2)), 40, 144, 64),
    (((1, 2), (-1, 2)), 32, 184, 32),
    (((2, 2),), 24, 216, 16),
)
WHERE = {tile: (c, n) for c, (tiles, _, _, _) in enumerate(CLASSES) for n, tile in enumerate(tiles)}
SLOTS = 256
NBLOCKS = 128
COPIES = 40


def wrap(steps):
    return (steps + 1) % SIDE - 1


def fused_kernel(
    records, owner, block, count, travel, amp,
    out, flag_out,
    wide, buf0, buf1, buf2, buf3, buf4, travel_v, amp_v,
    mine, near, mixed, lines, uses_v, uses_s,
    con0, con1, con2, con3, con4, lit0, lit1, lit2, lit3, lit4,
    flag_mine, flags, sums, parts, edge, edges, records_v, owner_v, block_v, met,
    local_sems, send_sems, recv_sems, near_send, near_recv, line_send, line_recv,
    flag_send, flag_recv, part_send, part_recv, edge_send, edge_recv,
):
    row, col = lax.axis_index("inline"), lax.axis_index("xline")
    z, x = col // SIDE, lax.rem(col, SIDE)
    bufs = (buf0, buf1, buf2, buf3, buf4)
    cons, lits = (con0, con1, con2, con3, con4), (lit0, lit1, lit2, lit3, lit4)
    near[...] = jnp.zeros_like(near)
    edges[...] = jnp.zeros_like(edges)

    def at(dz, dx):
        return lax.rem(z + dz + SIDE, SIDE) * SIDE + lax.rem(x + dx + SIDE, SIDE)

    beside = [(row, at(dz, dx)) for dz, dx in ((0, 1), (0, -1), (1, 0), (-1, 0))]
    beside += [(lax.rem(row + 1, ROWS), col), (lax.rem(row + ROWS - 1, ROWS), col)]
    barrier = pltpu.get_barrier_semaphore()
    for there in beside:
        pl.semaphore_signal(barrier, inc=1, device_id=there, device_id_type=MESH)
    inputs = [
        pltpu.make_async_copy(records, records_v, local_sems.at[3]),
        pltpu.make_async_copy(owner, owner_v, local_sems.at[4]),
        pltpu.make_async_copy(block, block_v, local_sems.at[5]),
    ]
    for copy in inputs:
        copy.start()
    loads = [
        pltpu.make_async_copy(travel, travel_v, local_sems.at[0]),
        pltpu.make_async_copy(amp, amp_v, local_sems.at[1]),
    ]
    for copy in loads:
        copy.start()

    for copy in inputs:
        copy.wait()

    wide[pl.ds(0, SHOTS * NP * BEAMS), :] = records_v[...].astype(jnp.float32).reshape(SHOTS * NP * BEAMS, NS)
    energies = jnp.zeros((8, NS), jnp.float32)
    lane8 = lax.broadcasted_iota(jnp.int32, (8, NS), 1)
    for s in range(SHOTS):
        for b in range(BEAMS):
            rec = wide[pl.ds(s * NP * BEAMS + b, NP, stride=BEAMS), :]
            bufs[0][row_of(s, 0, 0) + b] = rec.astype(jnp.bfloat16)
            energy = jnp.sum(rec * rec, keepdims=True) * (1.0 / (NP * NS))
            energies = jnp.where(lane8 == ENERGY + s * BEAMS + b, jnp.broadcast_to(energy, (8, NS)), energies)
    named = (owner_v[...] * 128 + block_v[...]).astype(jnp.float32)
    mine[...] = jnp.where(lane8 >= COUNT, count[0, 0].astype(jnp.float32), energies)
    mine[:, 0:USES] = jnp.broadcast_to(named, (8, USES))
    pl.semaphore_wait(barrier, len(beside))

    started = {}

    def send(kind, route, axis, step, first, second, lo, size):
        seen = (wrap(first - step), second) if axis == 0 else (first, wrap(second - step))
        here, there = WHERE[first, second][0], WHERE[seen][0]
        along_x = (axis == 0) == (route == 0)
        n = len(started)
        copy = pltpu.make_async_remote_copy(
            src_ref=bufs[here].at[pl.ds(row_of(route, first, second) + lo, size)],
            dst_ref=bufs[there].at[pl.ds(row_of(route, *seen) + lo, size)],
            send_sem=send_sems.at[n],
            recv_sem=recv_sems.at[n],
            device_id=(row, at(0, step) if along_x else at(step, 0)),
            device_id_type=MESH,
        )
        copy.start()
        key = (kind, route, step) if axis == 0 else (kind, route, first, step)
        started[key] = copy

    both, ways = (0, 1), (1, -1)
    half = BEAMS // 2

    def along_second(first):
        for way in ways:
            for route in both:
                send("c", route, 1, way, first, 0, 0, BEAMS)

    def pass_on(first):
        for way in ways:
            for route in both:
                started["c", route, first, way].wait_recv()
                send("d", route, 1, way, first, -way, 0 if way > 0 else half, half)

    def arrived(first):
        for route in both:
            for way in ways:
                started["d", route, first, way].wait_recv()

    def image_some(p, begin, end):
        _, slots, base, held = CLASSES[p]
        buf, con, lit = bufs[p], cons[p], lits[p]

        def step(i, carry):
            places = [base + i * GROUP + d for d in range(GROUP)]
            picked = [(uses_s[0, u] & (NBLOCKS - 1), uses_s[1, u] & (held - 1)) for u in places]
            totals = [jnp.zeros((8, NS), jnp.float32) for _ in picked]
            squares = [jnp.zeros((8, NS), jnp.float32) for _ in picked]
            for q in range(NP // 8):
                rows = pl.ds(8 * q, 8)
                for d, (number, rec) in enumerate(picked):
                    t = travel_v[number, rows, :]
                    a = amp_v[number, rows, :]
                    pair = buf[rec, pl.ds(16 * (q // 2), 16), :].astype(jnp.float32)
                    r = pair[8 * (q % 2) : 8 * (q % 2) + 8]
                    k = t.astype(jnp.int32)
                    f = t - k.astype(jnp.float32)
                    w0 = (1.0 - f).astype(jnp.bfloat16).astype(jnp.float32)
                    w1 = f.astype(jnp.bfloat16).astype(jnp.float32)
                    v0 = jnp.take_along_axis(r, k, axis=1, mode="promise_in_bounds")
                    v1 = jnp.take_along_axis(r, k + 1, axis=1, mode="promise_in_bounds")
                    totals[d] += a * (v0 * w0 + v1 * w1)
                    squares[d] += a * a
            for d in range(GROUP):
                con[pl.ds(i * GROUP + d, 8, stride=slots), :] = totals[d]
                lit[pl.ds(i * GROUP + d, 8, stride=slots), :] = squares[d]
            return carry

        lax.fori_loop(begin // GROUP, end // GROUP, step, 0)

    def total_of(p, listed, energy):
        _, slots, base, _ = CLASSES[p]
        con = sum(cons[p][pl.ds(s * slots, slots), :] for s in range(8))
        lit = sum(lits[p][pl.ds(s * slots, slots), :] for s in range(8))
        target = jnp.broadcast_to(listed[2:3, base : base + slots], (NS, slots))
        weight = jnp.broadcast_to(energy[:, base : base + slots], (NS, slots))
        line = (lax.broadcasted_iota(jnp.int32, (NS, slots), 0) + 1).astype(jnp.float32)
        to_con = jnp.where(target == line, 1.0, 0.0)
        to_lit = jnp.where((target + 4.0 == line) & (target > 0.0), weight, 0.0)
        dot = lambda m, v: jnp.dot(m, v, precision=lax.Precision.HIGHEST, preferred_element_type=jnp.float32)
        return dot(to_con, con) + dot(to_lit, lit)

    for step in ways:
        for route in both:
            send("a", route, 0, step, 0, 0, 0, BEAMS)
    along_second(0)

    up = pltpu.make_async_remote_copy(
        mine, near.at[0], near_send.at[0], near_recv.at[0], device_id=(row + 1, col), device_id_type=MESH
    )
    down = pltpu.make_async_remote_copy(
        mine, near.at[1], near_send.at[1], near_recv.at[1], device_id=(row - 1, col), device_id_type=MESH
    )
    upward, downward = pl.when(row < ROWS - 1), pl.when(row > 0)
    upward(up.start)
    downward(down.start)
    for turn in range(3):
        for there in beside:
            pl.semaphore_signal(met.at[turn], inc=1, device_id=there, device_id_type=MESH)
        pl.semaphore_wait(met.at[turn], len(beside))
    downward(up.wait_recv)
    upward(down.wait_recv)
    kind8 = lax.rem(lane8, 5 * BEAMS) // BEAMS
    kind8 = jnp.where(lane8 < USES, kind8, 0)
    mixed[...] = jnp.where(kind8 == 1, near[1], jnp.where(kind8 == 2, near[0], mine[...]))
    shares = []
    for other in range(1, COLS):
        share = pltpu.make_async_remote_copy(
            mixed, lines.at[other], line_send.at[other], line_recv.at[other],
            device_id=(row, lax.rem(col + other, COLS)), device_id_type=MESH,
        )
        share.start()
        shares.append(share)
    lines[0] = mixed[...]

    for step in ways:
        for route in both:
            started["a", route, step].wait_recv()
            send("b", route, 0, step, -step, 0, 0 if step > 0 else half, half)
        along_second(-step)

    for share in shares:
        share.wait_recv()
    listed, energy, over = list_uses(row, col, lines)
    uses_v[...] = listed.astype(jnp.int32)
    to_smem = pltpu.make_async_copy(uses_v, uses_s, local_sems.at[2])
    to_smem.start()
    flag_mine[...] = over
    alarms = []
    for other in range(1, ROWS):
        alarm = pltpu.make_async_remote_copy(
            flag_mine, flags.at[other], flag_send.at[other], flag_recv.at[other],
            device_id=(lax.rem(row + other, ROWS), col), device_id_type=MESH,
        )
        alarm.start()
        alarms.append(alarm)

    for route in both:
        for step in ways:
            started["b", route, step].wait_recv()
    along_second(2)
    pass_on(0)
    to_smem.wait()
    for copy in loads:
        copy.wait()
    image_some(0, 0, 56)
    pass_on(1)
    pass_on(-1)
    image_some(1, 0, 80)
    pass_on(2)
    arrived(0)
    image_some(2, 0, 40)
    early = total_of(0, listed, energy) + total_of(1, listed, energy) + total_of(2, listed, energy)
    raised = flag_mine[...]
    for alarm, other in zip(alarms, range(1, ROWS)):
        alarm.wait_recv()
        raised = jnp.maximum(raised, flags[other])
    flag_out[0] = jnp.max(raised).astype(jnp.int32)
    arrived(1)
    arrived(-1)
    image_some(3, 0, 32)
    early += total_of(3, listed, energy)
    arrived(2)
    image_some(4, 0, 24)
    sums[...] = (early + total_of(4, listed, energy)).reshape(COLS, 8, NS)

    pieces = []
    for other in range(1, COLS):
        there = lax.rem(col + other, COLS)
        piece = pltpu.make_async_remote_copy(
            sums.at[there], parts.at[other], part_send.at[other], part_recv.at[other],
            device_id=(row, there), device_id_type=MESH,
        )
        piece.start()
        pieces.append(piece)
    whole = sums[col]
    for piece, other in zip(pieces, range(1, COLS)):
        piece.wait_recv()
        whole += parts[other]
    edge[...] = whole
    to_next = pltpu.make_async_remote_copy(
        edge, edges.at[0], edge_send.at[0], edge_recv.at[0], device_id=(row + 1, col), device_id_type=MESH
    )
    to_prev = pltpu.make_async_remote_copy(
        edge, edges.at[1], edge_send.at[1], edge_recv.at[1], device_id=(row - 1, col), device_id_type=MESH
    )
    upward(to_next.start)
    downward(to_prev.start)
    for copy in started.values():
        copy.wait_send()
    for copy in shares + alarms + pieces:
        copy.wait_send()
    upward(up.wait_send)
    downward(down.wait_send)
    downward(to_next.wait_recv)
    upward(to_prev.wait_recv)
    contrib = whole[1:2] + edges[0][2:3] + edges[1][0:1]
    lighting = whole[5:6] + edges[0][6:7] + edges[1][4:5]
    out[0] = contrib / jnp.sqrt(1.0 + lighting)
    upward(to_next.wait_send)
    downward(to_prev.wait_send)


def row_of(route, first, second):
    c, n = WHERE[first, second]
    return (route * len(CLASSES[c][0]) + n) * BEAMS


def list_uses(row, col, lines):
    table = jnp.concatenate([lines[lax.rem(col - tile + COLS, COLS)][0:1, :] for tile in range(COLS)], axis=0)
    shape = (COLS, NS)
    lane = lax.broadcasted_iota(jnp.int32, shape, 1)
    tile = lax.broadcasted_iota(jnp.int32, shape, 0)
    shot, kind, beam = lane // (5 * BEAMS), lax.rem(lane, 5 * BEAMS) // BEAMS, lax.rem(lane, BEAMS)
    names = table.astype(jnp.int32)

    def of_source(own):
        before, after = pltpu.roll(own, 1, 0), pltpu.roll(own, COLS - 1, 0)
        return jnp.where(kind == 3, before, jnp.where(kind == 4, after, own))

    last, first = (row == ROWS - 1).astype(jnp.int32), (row == 0).astype(jnp.int32)
    missing = (
        ((kind == 1) & (last == 1))
        | ((kind == 2) & (first == 1))
        | ((kind == 3) & (tile == 0))
        | ((kind == 4) & (tile == COLS - 1))
    )
    counts = of_source(jnp.broadcast_to(names[:, COUNT : COUNT + 1], shape))
    energy = of_source(
        jnp.take_along_axis(
            table, jnp.where(lane < USES, ENERGY + shot * BEAMS + beam, lane), axis=1, mode="promise_in_bounds"
        )
    )
    live = (lane < USES) & (beam < counts) & jnp.logical_not(missing)
    owners = names // 128

    source = tile + (kind == 4).astype(jnp.int32) - (kind == 3).astype(jnp.int32)
    along_z = (source // SIDE - owners // SIDE) & (SIDE - 1)
    along_x = (source - owners) & (SIDE - 1)
    code = jnp.where(shot == 0, along_x * SIDE + along_z, along_z * SIDE + along_x)
    group, record = jnp.zeros(shape, jnp.int32), jnp.zeros(shape, jnp.int32)
    for (first_step, second_step), (c, _) in WHERE.items():
        same = code == first_step % SIDE * SIDE + second_step % SIDE
        group = jnp.where(same, c, group)
        begin = [row_of(route, first_step, second_step) for route in (0, 1)]
        record = jnp.where(same, jnp.where(shot == 0, begin[0], begin[1]) + beam, record)

    column = lax.broadcasted_iota(jnp.int32, (NS, NS), 1)
    owned = jnp.where(live, owners * 8 + group, -1)
    over = jnp.zeros((1, 1), jnp.float32)
    for c, (_, slots, _, _) in enumerate(CLASSES):
        per_owner = jnp.concatenate(
            [jnp.sum((owned == o * 8 + c).astype(jnp.float32), axis=0, keepdims=True) for o in range(COLS)], axis=0
        )
        held = jnp.sum(per_owner, axis=1, keepdims=True)
        over = jnp.maximum(over, jnp.max((held > float(slots)).astype(jnp.float32), keepdims=True))

    earlier = lax.broadcasted_iota(jnp.int32, (NS, NS), 0) <= column
    above = lax.broadcasted_iota(jnp.int32, (COLS, COLS), 1) < lax.broadcasted_iota(jnp.int32, (COLS, COLS), 0)
    shift = 1 + (kind == 1).astype(jnp.int32) - (kind == 2).astype(jnp.int32)
    place = jnp.full(shape, -1.0)
    for c, (_, slots, base, _) in enumerate(CLASSES):
        marks = live & (owners == col) & (group == c)
        ones = marks.astype(jnp.float32)
        within = jnp.dot(ones, earlier.astype(jnp.float32), preferred_element_type=jnp.float32)
        totals = jnp.broadcast_to(jnp.sum(ones, axis=1, keepdims=True), shape)
        ahead = jnp.dot(above.astype(jnp.float32), totals, preferred_element_type=jnp.float32)
        rank = within + ahead - 1.0
        place = jnp.where(marks & (rank < float(slots)), rank + float(base), place)
    high = energy.astype(jnp.bfloat16).astype(jnp.float32)
    middle = (energy - high).astype(jnp.bfloat16).astype(jnp.float32)
    low = energy - high - middle
    fields = (
        lax.rem(names, 128).astype(jnp.float32),
        record.astype(jnp.float32),
        (tile * 8 + shift + 1).astype(jnp.float32),
        high,
        middle,
        low,
    )
    upright = jnp.transpose(place)
    slot = lax.broadcasted_iota(jnp.int32, (NS, SLOTS), 1).astype(jnp.float32)
    line = lax.broadcasted_iota(jnp.int32, (8, NS), 0)
    listed = jnp.zeros((8, SLOTS), jnp.float32)
    for t in range(COLS):
        here = (jnp.broadcast_to(upright[:, t : t + 1], (NS, SLOTS)) == slot).astype(jnp.bfloat16)
        rows = jnp.zeros((8, NS), jnp.float32)
        for f, field in enumerate(fields):
            rows = jnp.where(line == f, jnp.broadcast_to(field[t : t + 1, :], (8, NS)), rows)
        listed += jnp.dot(rows.astype(jnp.bfloat16), here, preferred_element_type=jnp.float32)
    return listed, listed[3:4] + listed[4:5] + listed[5:6], jnp.broadcast_to(over, (8, NS))


def fused(records, owner, block, count, travel, amp):
    vmem = pl.BlockSpec(memory_space=pltpu.VMEM)
    smem = pl.BlockSpec(memory_space=pltpu.SMEM)
    hbm = pl.BlockSpec(memory_space=pl.ANY)
    dma = pltpu.SemaphoreType.DMA
    f32 = jnp.float32
    return pl.pallas_call(
        fused_kernel,
        out_shape=(jax.ShapeDtypeStruct((1, 1, NS), f32), jax.ShapeDtypeStruct((1,), jnp.int32)),
        in_specs=[hbm, hbm, hbm, smem, hbm, hbm],
        out_specs=(vmem, smem),
        scratch_shapes=[
            pltpu.VMEM(((SHOTS * NP + 1) * BEAMS, NS), f32),
            *[pltpu.VMEM((held, NP, NS), jnp.bfloat16) for _, _, _, held in CLASSES],
            pltpu.VMEM(travel.shape, f32),
            pltpu.VMEM(amp.shape, f32),
            pltpu.VMEM((8, NS), f32),
            pltpu.VMEM((2, 8, NS), f32),
            pltpu.VMEM((8, NS), f32),
            pltpu.VMEM((COLS, 8, NS), f32),
            pltpu.VMEM((8, SLOTS), jnp.int32),
            pltpu.SMEM((8, SLOTS), jnp.int32),
            *[pltpu.VMEM((9 * slots, NS), f32) for _, slots, _, _ in CLASSES],
            *[pltpu.VMEM((9 * slots, NS), f32) for _, slots, _, _ in CLASSES],
            pltpu.VMEM((8, NS), f32),
            pltpu.VMEM((ROWS, 8, NS), f32),
            pltpu.VMEM((COLS, 8, NS), f32),
            pltpu.VMEM((COLS, 8, NS), f32),
            pltpu.VMEM((8, NS), f32),
            pltpu.VMEM((2, 8, NS), f32),
            pltpu.VMEM(records.shape, records.dtype),
            pltpu.VMEM(owner.shape, jnp.int32),
            pltpu.VMEM(block.shape, jnp.int32),
            pltpu.SemaphoreType.REGULAR((3,)),
            dma((6,)),
            dma((COPIES,)),
            dma((COPIES,)),
            dma((2,)),
            dma((2,)),
            dma((COLS,)),
            dma((COLS,)),
            dma((ROWS,)),
            dma((ROWS,)),
            dma((COLS,)),
            dma((COLS,)),
            dma((2,)),
            dma((2,)),
        ],
        compiler_params=pltpu.CompilerParams(
            collective_id=0, has_side_effects=True, vmem_limit_bytes=40 << 20
        ),
        cost_estimate=pl.CostEstimate(flops=10_000_000, bytes_accessed=16_000_000, transcendentals=0),
        name="migrate",
    )(records, owner, block, count, travel, amp)


def per_device(records, beam_count, owner_list, block_list, travel_table, amp_table):
    travel_table = pltpu.with_memory_space_constraint(travel_table, pltpu.HBM)
    amp_table = pltpu.with_memory_space_constraint(amp_table, pltpu.HBM)
    by_slowness = records.reshape(SHOTS, BEAMS, NP, NS).transpose(0, 2, 1, 3)
    owner, block = owner_list.reshape(1, USES), block_list.reshape(1, USES)
    quick, flag = fused(by_slowness, owner, block, beam_count, travel_table, amp_table)
    return lax.cond(
        flag[0] > 0,
        lambda: imaged_by_any_count(records, beam_count, owner_list, block_list, travel_table, amp_table),
        lambda: quick,
    )


def solution(mesh):
    placed = (
        P(None, "inline", "xline", None, None),
        P("inline", "xline"),
        P(("inline", "xline"), None),
        P(("inline", "xline"), None),
        P("xline", None, None),
        P("xline", None, None),
    )
    return jax.shard_map(
        per_device,
        mesh=mesh,
        in_specs=placed,
        out_specs=P("inline", "xline", None),
        check_vma=False,
    )
```

```python
import jax
import jax.numpy as jnp
from jax import lax
from jax.experimental import pallas as pl
from jax.experimental.pallas import tpu as pltpu
from jax.sharding import PartitionSpec as P

NS = 128
NP = 64
BEAMS = 8
SHOTS = 2
RECS = SHOTS * BEAMS
SIDE = 4
COLS = SIDE * SIDE
ROWS = 8
USES = 5 * RECS
LIST = 512
TARGETS = 3 * COLS
GROUP = 8
MESH = pl.DeviceIdType.MESH

ENERGY = USES
COUNT = USES + RECS


def greet(row, col):
    barrier = pltpu.get_barrier_semaphore()
    for other in range(1, COLS):
        pl.semaphore_signal(
            barrier, inc=1, device_id=(row, lax.rem(col + other, COLS)), device_id_type=MESH
        )

    @pl.when(row > 0)
    def _():
        pl.semaphore_signal(barrier, inc=1, device_id=(row - 1, col), device_id_type=MESH)

    @pl.when(row < ROWS - 1)
    def _():
        pl.semaphore_signal(barrier, inc=1, device_id=(row + 1, col), device_id_type=MESH)

    edges = (row > 0).astype(jnp.int32) + (row < ROWS - 1).astype(jnp.int32)
    pl.semaphore_wait(barrier, COLS - 1 + edges)


def gather_kernel(
    records, index, travel, amp,
    held, travel_out, amp_out, uses_out, index_out,
    near, mixed, lines, uses_vmem, index_vmem,
    local_sems, send_sems, recv_sems, near_send, near_recv, line_send, line_recv,
):
    row, col = lax.axis_index("inline"), lax.axis_index("xline")
    z, x = col // SIDE, lax.rem(col, SIDE)
    loads = [
        pltpu.make_async_copy(travel, travel_out, local_sems.at[0]),
        pltpu.make_async_copy(amp, amp_out, local_sems.at[1]),
        pltpu.make_async_copy(records, held.at[pl.ds(col * RECS, RECS)], local_sems.at[2]),
    ]
    near[...] = jnp.zeros_like(near)
    greet(row, col)

    def at(dz, dx):
        return lax.rem(z + dz + SIDE, SIDE) * SIDE + lax.rem(x + dx + SIDE, SIDE)

    started = {}

    def block(route, first, second, lo, size):
        tile = at(second, first) if route == 0 else at(first, second)
        return pl.ds(tile * RECS + route * BEAMS + lo, size)

    def toward(route, axis, step):
        along_x = (axis == 0) == (route == 0)
        return (row, at(0, step) if along_x else at(step, 0))

    def send(key, route, axis, step, first, second, lo, size):
        here = block(route, first, second, lo, size)
        n = len(started)
        if first == 0 and second == 0:
            source = records.at[pl.ds(route * BEAMS + lo, size)]
        else:
            source = held.at[here]
        copy = pltpu.make_async_remote_copy(
            src_ref=source,
            dst_ref=held.at[here],
            send_sem=send_sems.at[n],
            recv_sem=recv_sems.at[n],
            device_id=toward(route, axis, step),
            device_id_type=MESH,
        )
        copy.start()
        started[key] = copy

    half = BEAMS // 2
    both = (0, 1)
    for route in both:
        for step in (1, -1):
            send(("a", route, step), route, 0, step, 0, 0, 0, BEAMS)
    for route in both:
        for step in (1, -1):
            send(("c", route, 0, step), route, 1, step, 0, 0, 0, BEAMS)
    for copy in loads:
        copy.start()

    up = pltpu.make_async_remote_copy(
        index, near.at[0], near_send.at[0], near_recv.at[0], device_id=(row + 1, col), device_id_type=MESH
    )
    down = pltpu.make_async_remote_copy(
        index, near.at[1], near_send.at[1], near_recv.at[1], device_id=(row - 1, col), device_id_type=MESH
    )
    @pl.when(row < ROWS - 1)
    def _():
        up.start()

    @pl.when(row > 0)
    def _():
        down.start()

    @pl.when(row > 0)
    def _():
        up.wait_recv()

    @pl.when(row < ROWS - 1)
    def _():
        down.wait_recv()

    @pl.when(row < ROWS - 1)
    def _():
        up.wait_send()

    @pl.when(row > 0)
    def _():
        down.wait_send()

    kind = lax.broadcasted_iota(jnp.int32, (8, NS), 1) // RECS
    mixed[...] = jnp.where(kind == 1, near[1], jnp.where(kind == 2, near[0], index[...]))
    shares = []
    for other in range(1, COLS):
        share = pltpu.make_async_remote_copy(
            mixed,
            lines.at[other],
            line_send.at[other],
            line_recv.at[other],
            device_id=(row, lax.rem(col + other, COLS)),
            device_id_type=MESH,
        )
        share.start()
        shares.append(share)
    lines[0] = mixed[...]

    for route in both:
        for step in (1, -1):
            started["a", route, step].wait_recv()
            lo = 0 if step > 0 else half
            send(("b", route, step), route, 0, step, -step, 0, lo, half)
            for way in (1, -1):
                send(("c", route, -step, way), route, 1, way, -step, 0, 0, BEAMS)
    for route in both:
        for way in (1, -1):
            started["c", route, 0, way].wait_recv()
            lo = 0 if way > 0 else half
            send(("d", route, 0, way), route, 1, way, 0, -way, lo, half)

    build_list(row, col, shares, lines, index_vmem, uses_vmem)

    for route in both:
        for step in (1, -1):
            started["b", route, step].wait_recv()
        for way in (1, -1):
            send(("c", route, 2, way), route, 1, way, 2, 0, 0, BEAMS)
    for first in (-1, 1, 2):
        for route in both:
            for way in (1, -1):
                started["c", route, first, way].wait_recv()
                lo = 0 if way > 0 else half
                send(("d", route, first, way), route, 1, way, first, -way, lo, half)
    finish = [
        pltpu.make_async_copy(uses_vmem, uses_out, local_sems.at[3]),
        pltpu.make_async_copy(index_vmem, index_out, local_sems.at[4]),
    ]
    for copy in finish:
        copy.start()
    for first in (0, -1, 1, 2):
        for route in both:
            for way in (1, -1):
                started["d", route, first, way].wait_recv()
    for copy in started.values():
        copy.wait_send()
    for share in shares:
        share.wait_send()
    for copy in loads + finish:
        copy.wait()


def build_list(row, col, shares, lines, index_vmem, uses_vmem):
    for share in shares:
        share.wait_recv()
    for tile in range(COLS):
        index_vmem[pl.ds(tile, 1), :] = lines[lax.rem(col - tile + COLS, COLS)][0:1, :]
    table = index_vmem[...]
    names = table.astype(jnp.int32)
    shape = (COLS, NS)
    lane = lax.broadcasted_iota(jnp.int32, shape, 1)
    tile = lax.broadcasted_iota(jnp.int32, shape, 0)
    kind, beam = lane // RECS, lax.rem(lane, BEAMS)
    counts = jnp.broadcast_to(names[:, COUNT : COUNT + 1], shape)
    before = jnp.where(tile > 0, pltpu.roll(counts, 1, 0), 0)
    after = jnp.where(tile < COLS - 1, pltpu.roll(counts, COLS - 1, 0), 0)
    last, first = (row == ROWS - 1).astype(jnp.int32), (row == 0).astype(jnp.int32)
    live = jnp.where(kind == 3, before, jnp.where(kind == 4, after, counts))
    live = jnp.where(kind == 1, counts * (1 - last), live)
    live = jnp.where(kind == 2, counts * (1 - first), live)
    wanted = (lane < USES) & (beam < live) & (names // 128 == col)
    marks = wanted.astype(jnp.float32)
    earlier = lax.broadcasted_iota(jnp.int32, (NS, NS), 0) <= lax.broadcasted_iota(jnp.int32, (NS, NS), 1)
    within = jnp.dot(marks, earlier.astype(jnp.float32), preferred_element_type=jnp.float32)
    above = lax.broadcasted_iota(jnp.int32, (COLS, COLS), 1) < lax.broadcasted_iota(jnp.int32, (COLS, COLS), 0)
    totals = jnp.broadcast_to(jnp.sum(marks, axis=1, keepdims=True), shape)
    ahead = jnp.dot(above.astype(jnp.float32), totals, preferred_element_type=jnp.float32)
    place = jnp.where(wanted, within + ahead - 1.0, -1.0)
    number = jnp.sum(marks)

    source = tile + (kind == 4).astype(jnp.int32) - (kind == 3).astype(jnp.int32)
    shift = 1 + (kind == 1).astype(jnp.int32) - (kind == 2).astype(jnp.int32)
    fields = (
        lax.rem(names, 128).astype(jnp.float32),
        (source * RECS + lax.rem(lane, RECS)).astype(jnp.float32),
        (shift * COLS + tile).astype(jnp.float32),
    )
    upright = jnp.transpose(place)
    slot = lax.broadcasted_iota(jnp.int32, (NS, LIST), 1).astype(jnp.float32)
    line = lax.broadcasted_iota(jnp.int32, (8, NS), 0)
    listed = jnp.zeros((8, LIST), jnp.float32)
    for t in range(COLS):
        here = (jnp.broadcast_to(upright[:, t : t + 1], (NS, LIST)) == slot).astype(jnp.bfloat16)
        rows = jnp.zeros((8, NS), jnp.float32)
        for f, field in enumerate(fields):
            rows = jnp.where(line == f, jnp.broadcast_to(field[t : t + 1, :], (8, NS)), rows)
        listed += jnp.dot(rows.astype(jnp.bfloat16), here, preferred_element_type=jnp.float32)
    place_in = lax.broadcasted_iota(jnp.int32, (8, LIST), 1).astype(jnp.float32)
    part = lax.broadcasted_iota(jnp.int32, (8, LIST), 0)
    listed = jnp.where((part == 2) & (place_in >= number), float(TARGETS), listed)
    listed = jnp.where(part == 3, number, listed)
    uses_vmem[...] = listed.astype(jnp.int32)


def gather(records, index, travel, amp):
    hbm = pl.BlockSpec(memory_space=pl.ANY)
    vmem = pl.BlockSpec(memory_space=pltpu.VMEM)
    smem = pl.BlockSpec(memory_space=pltpu.SMEM)
    return pl.pallas_call(
        gather_kernel,
        out_shape=(
            pltpu.VMEM((COLS * RECS, NP, NS), jnp.bfloat16),
            pltpu.VMEM(travel.shape, jnp.float32),
            pltpu.VMEM(amp.shape, jnp.float32),
            jax.ShapeDtypeStruct((8, LIST), jnp.int32),
            jax.ShapeDtypeStruct((COLS, NS), jnp.float32),
        ),
        in_specs=[hbm, vmem, hbm, hbm],
        out_specs=(vmem, vmem, vmem, hbm, hbm),
        scratch_shapes=[
            pltpu.VMEM((2, 8, NS), jnp.float32),
            pltpu.VMEM((8, NS), jnp.float32),
            pltpu.VMEM((COLS, 8, NS), jnp.float32),
            pltpu.VMEM((8, LIST), jnp.int32),
            pltpu.VMEM((COLS, NS), jnp.float32),
            pltpu.SemaphoreType.DMA((5,)),
            pltpu.SemaphoreType.DMA((40,)),
            pltpu.SemaphoreType.DMA((40,)),
            pltpu.SemaphoreType.DMA((2,)),
            pltpu.SemaphoreType.DMA((2,)),
            pltpu.SemaphoreType.DMA((COLS,)),
            pltpu.SemaphoreType.DMA((COLS,)),
        ],
        compiler_params=pltpu.CompilerParams(
            collective_id=1, has_side_effects=True, vmem_limit_bytes=32 << 20
        ),
        cost_estimate=pl.CostEstimate(flops=10_000_000, bytes_accessed=16_000_000, transcendentals=0),
        name="gather_records",
    )(records, index, travel, amp)


def image_kernel(uses, index, records, travel, amp, out, acc):
    acc[...] = jnp.zeros_like(acc)

    def step(i, carry):
        picked = []
        for d in range(GROUP):
            u = i * GROUP + d
            picked.append((uses[0, u], uses[1, u], uses[2, u]))
        totals = [jnp.zeros((8, NS), jnp.float32) for _ in picked]
        squares = [jnp.zeros((8, NS), jnp.float32) for _ in picked]
        for q in range(NP // 8):
            rows = pl.ds(8 * q, 8)
            for d, (block, rec, _) in enumerate(picked):
                t = travel[block, rows, :]
                a = amp[block, rows, :]
                pair = records[rec, pl.ds(16 * (q // 2), 16), :].astype(jnp.float32)
                r = pair[8 * (q % 2) : 8 * (q % 2) + 8]
                k = t.astype(jnp.int32)
                f = t - k.astype(jnp.float32)
                w0 = (1.0 - f).astype(jnp.bfloat16).astype(jnp.float32)
                w1 = f.astype(jnp.bfloat16).astype(jnp.float32)
                v0 = jnp.take_along_axis(r, k, axis=1, mode="promise_in_bounds")
                v1 = jnp.take_along_axis(r, k + 1, axis=1, mode="promise_in_bounds")
                totals[d] += a * (v0 * w0 + v1 * w1)
                squares[d] += a * a
        for d, (_, rec, target) in enumerate(picked):
            energy = index[rec // RECS, ENERGY + lax.rem(rec, RECS)]
            acc[target, 0] += totals[d]
            acc[target, 1] += squares[d] * energy
        return carry

    lax.fori_loop(0, (uses[3, 0] + GROUP - 1) // GROUP, step, 0)
    out[...] = jnp.sum(acc[pl.ds(0, TARGETS)], axis=2)


def image(uses, index, records, travel, amp):
    vmem = pl.BlockSpec(memory_space=pltpu.VMEM)
    smem = pl.BlockSpec(memory_space=pltpu.SMEM)
    return pl.pallas_call(
        image_kernel,
        out_shape=pltpu.VMEM((TARGETS, 2, NS), jnp.float32),
        in_specs=[smem, smem, vmem, vmem, vmem],
        out_specs=vmem,
        scratch_shapes=[pltpu.VMEM((TARGETS + 1, 2, 8, NS), jnp.float32)],
        compiler_params=pltpu.CompilerParams(vmem_limit_bytes=32 << 20),
        cost_estimate=pl.CostEstimate(flops=10_000_000, bytes_accessed=8_000_000, transcendentals=0),
        name="image_uses",
    )(uses, index, records, travel, amp)


def exchange_kernel(sums, out, near, total, parts, near_send, near_recv, part_send, part_recv):
    row, col = lax.axis_index("inline"), lax.axis_index("xline")
    greet(row, col)
    up = pltpu.make_async_remote_copy(
        sums.at[2], near.at[0], near_send.at[0], near_recv.at[0], device_id=(row + 1, col), device_id_type=MESH
    )
    down = pltpu.make_async_remote_copy(
        sums.at[0], near.at[1], near_send.at[1], near_recv.at[1], device_id=(row - 1, col), device_id_type=MESH
    )

    @pl.when(row < ROWS - 1)
    def _():
        up.start()

    @pl.when(row > 0)
    def _():
        down.start()

    total[...] = sums[1]

    @pl.when(row > 0)
    def _():
        up.wait_recv()
        total[...] += near[0]

    @pl.when(row < ROWS - 1)
    def _():
        down.wait_recv()
        total[...] += near[1]

    copies = []
    for other in range(1, COLS):
        there = lax.rem(col + other, COLS)
        copy = pltpu.make_async_remote_copy(
            total.at[there],
            parts.at[other],
            part_send.at[other],
            part_recv.at[other],
            device_id=(row, there),
            device_id_type=MESH,
        )
        copy.start()
        copies.append(copy)
    mine = total[col]
    for copy, other in zip(copies, range(1, COLS)):
        copy.wait_recv()
        mine += parts[other]
    out[0] = mine[0:1] / jnp.sqrt(1.0 + mine[1:2])
    for copy in copies:
        copy.wait_send()

    @pl.when(row < ROWS - 1)
    def _():
        up.wait_send()

    @pl.when(row > 0)
    def _():
        down.wait_send()


def exchange(sums):
    vmem = pl.BlockSpec(memory_space=pltpu.VMEM)
    return pl.pallas_call(
        exchange_kernel,
        out_shape=jax.ShapeDtypeStruct((1, 1, NS), jnp.float32),
        in_specs=[vmem],
        out_specs=vmem,
        scratch_shapes=[
            pltpu.VMEM((2, COLS, 2, NS), jnp.float32),
            pltpu.VMEM((COLS, 2, NS), jnp.float32),
            pltpu.VMEM((COLS, 2, NS), jnp.float32),
            pltpu.SemaphoreType.DMA((2,)),
            pltpu.SemaphoreType.DMA((2,)),
            pltpu.SemaphoreType.DMA((COLS,)),
            pltpu.SemaphoreType.DMA((COLS,)),
        ],
        compiler_params=pltpu.CompilerParams(collective_id=2, has_side_effects=True),
        cost_estimate=pl.CostEstimate(flops=10_000, bytes_accessed=100_000, transcendentals=0),
        name="exchange_sums",
    )(sums)


def imaged_by_any_count(records, beam_count, owner_list, block_list, travel_table, amp_table):
    records = records.reshape(RECS, NP, NS)
    named = (owner_list * 128 + block_list)[:, 0].astype(jnp.float32)
    named = named.reshape(SHOTS, 5, BEAMS).transpose(1, 0, 2).reshape(USES)
    energy = jnp.mean(jnp.square(records.astype(jnp.float32)), axis=(1, 2))
    count = jnp.broadcast_to(beam_count[0].astype(jnp.float32), (NS - COUNT,))
    index = jnp.broadcast_to(jnp.concatenate([named, energy, count]), (8, NS))
    gathered, travel, amp, uses, index = gather(records, index, travel_table, amp_table)
    sums = image(uses, index, gathered, travel, amp)
    return exchange(sums.reshape(3, COLS, 2, NS))


CLASSES = (
    (((0, 0), (1, 0), (-1, 0), (2, 0)), 56, 0, 64),
    (((0, 1), (0, -1), (1, 1), (1, -1), (-1, 1), (-1, -1)), 80, 64, 128),
    (((2, 1), (2, -1), (0, 2)), 40, 144, 64),
    (((1, 2), (-1, 2)), 32, 184, 32),
    (((2, 2),), 24, 216, 16),
)
WHERE = {tile: (c, n) for c, (tiles, _, _, _) in enumerate(CLASSES) for n, tile in enumerate(tiles)}
FAR_FIRST = sorted(
    ((dz, dx) for dz in (0, 1, -1, 2) for dx in (0, 1, -1, 2) if (dz, dx) != (0, 0)),
    key=lambda step: -abs(step[0]) - abs(step[1]),
)
SLOTS = 256
NBLOCKS = 128
COPIES = 40


def wrap(steps):
    return (steps + 1) % SIDE - 1


def fused_kernel(
    records, owner, block, count, travel, amp,
    out, flag_out,
    wide, buf0, buf1, buf2, buf3, buf4, travel_v, amp_v,
    mine, near, mixed, lines, uses_v, uses_s,
    con0, con1, con2, con3, con4, lit0, lit1, lit2, lit3, lit4,
    flag_mine, flags, sums, parts, edge, edges, records_v, owner_v, block_v, met,
    local_sems, send_sems, recv_sems, near_send, near_recv, line_send, line_recv,
    flag_send, flag_recv, part_send, part_recv, edge_send, edge_recv, late, late_in, late_send, late_recv,
):
    row, col = lax.axis_index("inline"), lax.axis_index("xline")
    z, x = col // SIDE, lax.rem(col, SIDE)
    bufs = (buf0, buf1, buf2, buf3, buf4)
    cons, lits = (con0, con1, con2, con3, con4), (lit0, lit1, lit2, lit3, lit4)
    near[...] = jnp.zeros_like(near)
    edges[...] = jnp.zeros_like(edges)

    def at(dz, dx):
        return lax.rem(z + dz + SIDE, SIDE) * SIDE + lax.rem(x + dx + SIDE, SIDE)

    beside = [(row, at(dz, dx)) for dz, dx in ((0, 1), (0, -1), (1, 0), (-1, 0))]
    beside += [(lax.rem(row + 1, ROWS), col), (lax.rem(row + ROWS - 1, ROWS), col)]
    barrier = pltpu.get_barrier_semaphore()
    for there in beside:
        pl.semaphore_signal(barrier, inc=1, device_id=there, device_id_type=MESH)
    inputs = [
        pltpu.make_async_copy(records, records_v, local_sems.at[3]),
        pltpu.make_async_copy(owner, owner_v, local_sems.at[4]),
        pltpu.make_async_copy(block, block_v, local_sems.at[5]),
    ]
    for copy in inputs:
        copy.start()
    loads = [
        pltpu.make_async_copy(travel, travel_v, local_sems.at[0]),
        pltpu.make_async_copy(amp, amp_v, local_sems.at[1]),
    ]
    for copy in loads:
        copy.start()

    for copy in inputs:
        copy.wait()

    wide[pl.ds(0, SHOTS * NP * BEAMS), :] = records_v[...].astype(jnp.float32).reshape(SHOTS * NP * BEAMS, NS)
    energies = jnp.zeros((8, NS), jnp.float32)
    lane8 = lax.broadcasted_iota(jnp.int32, (8, NS), 1)
    for s in range(SHOTS):
        for b in range(BEAMS):
            rec = wide[pl.ds(s * NP * BEAMS + b, NP, stride=BEAMS), :]
            bufs[0][row_of(s, 0, 0) + b] = rec.astype(jnp.bfloat16)
            energy = jnp.sum(rec * rec, keepdims=True) * (1.0 / (NP * NS))
            energies = jnp.where(lane8 == ENERGY + s * BEAMS + b, jnp.broadcast_to(energy, (8, NS)), energies)
    named = (owner_v[...] * 128 + block_v[...]).astype(jnp.float32)
    mine[...] = jnp.where(lane8 >= COUNT, count[0, 0].astype(jnp.float32), energies)
    mine[:, 0:USES] = jnp.broadcast_to(named, (8, USES))
    pl.semaphore_wait(barrier, len(beside))

    started = {}

    def send(kind, route, axis, step, first, second, lo, size):
        seen = (wrap(first - step), second) if axis == 0 else (first, wrap(second - step))
        here, there = WHERE[first, second][0], WHERE[seen][0]
        along_x = (axis == 0) == (route == 0)
        n = len(started)
        copy = pltpu.make_async_remote_copy(
            src_ref=bufs[here].at[pl.ds(row_of(route, first, second) + lo, size)],
            dst_ref=bufs[there].at[pl.ds(row_of(route, *seen) + lo, size)],
            send_sem=send_sems.at[n],
            recv_sem=recv_sems.at[n],
            device_id=(row, at(0, step) if along_x else at(step, 0)),
            device_id_type=MESH,
        )
        copy.start()
        key = (kind, route, step) if axis == 0 else (kind, route, first, step)
        started[key] = copy

    both, ways = (0, 1), (1, -1)
    half = BEAMS // 2

    def along_second(first):
        for way in ways:
            for route in both:
                send("c", route, 1, way, first, 0, 0, BEAMS)

    def pass_on(first):
        for way in ways:
            for route in both:
                started["c", route, first, way].wait_recv()
                send("d", route, 1, way, first, -way, 0 if way > 0 else half, half)

    def arrived(first):
        for route in both:
            for way in ways:
                started["d", route, first, way].wait_recv()

    def image_some(p, begin, end):
        _, slots, base, held = CLASSES[p]
        buf, con, lit = bufs[p], cons[p], lits[p]

        def step(i, carry):
            places = [base + i * GROUP + d for d in range(GROUP)]
            picked = [(uses_s[0, u] & (NBLOCKS - 1), uses_s[1, u] & (held - 1)) for u in places]
            totals = [jnp.zeros((8, NS), jnp.float32) for _ in picked]
            squares = [jnp.zeros((8, NS), jnp.float32) for _ in picked]
            for q in range(NP // 8):
                rows = pl.ds(8 * q, 8)
                for d, (number, rec) in enumerate(picked):
                    t = travel_v[number, rows, :]
                    a = amp_v[number, rows, :]
                    pair = buf[rec, pl.ds(16 * (q // 2), 16), :].astype(jnp.float32)
                    r = pair[8 * (q % 2) : 8 * (q % 2) + 8]
                    k = t.astype(jnp.int32)
                    f = t - k.astype(jnp.float32)
                    w0 = (1.0 - f).astype(jnp.bfloat16).astype(jnp.float32)
                    w1 = f.astype(jnp.bfloat16).astype(jnp.float32)
                    v0 = jnp.take_along_axis(r, k, axis=1, mode="promise_in_bounds")
                    v1 = jnp.take_along_axis(r, k + 1, axis=1, mode="promise_in_bounds")
                    totals[d] += a * (v0 * w0 + v1 * w1)
                    squares[d] += a * a
            for d in range(GROUP):
                con[pl.ds(i * GROUP + d, 8, stride=slots), :] = totals[d]
                lit[pl.ds(i * GROUP + d, 8, stride=slots), :] = squares[d]
            return carry

        lax.fori_loop(begin // GROUP, end // GROUP, step, 0)

    def total_of(p, listed, energy):
        _, slots, base, _ = CLASSES[p]
        con = sum(cons[p][pl.ds(s * slots, slots), :] for s in range(8))
        lit = sum(lits[p][pl.ds(s * slots, slots), :] for s in range(8))
        target = jnp.broadcast_to(listed[2:3, base : base + slots], (NS, slots))
        weight = jnp.broadcast_to(energy[:, base : base + slots], (NS, slots))
        line = (lax.broadcasted_iota(jnp.int32, (NS, slots), 0) + 1).astype(jnp.float32)
        to_con = jnp.where(target == line, 1.0, 0.0)
        to_lit = jnp.where((target + 4.0 == line) & (target > 0.0), weight, 0.0)
        dot = lambda m, v: jnp.dot(m, v, precision=lax.Precision.HIGHEST, preferred_element_type=jnp.float32)
        return dot(to_con, con) + dot(to_lit, lit)

    for step in ways:
        for route in both:
            send("a", route, 0, step, 0, 0, 0, BEAMS)
    along_second(0)

    up = pltpu.make_async_remote_copy(
        mine, near.at[0], near_send.at[0], near_recv.at[0], device_id=(row + 1, col), device_id_type=MESH
    )
    down = pltpu.make_async_remote_copy(
        mine, near.at[1], near_send.at[1], near_recv.at[1], device_id=(row - 1, col), device_id_type=MESH
    )
    upward, downward = pl.when(row < ROWS - 1), pl.when(row > 0)
    upward(up.start)
    downward(down.start)
    for turn in range(3):
        for there in beside:
            pl.semaphore_signal(met.at[turn], inc=1, device_id=there, device_id_type=MESH)
        pl.semaphore_wait(met.at[turn], len(beside))
    downward(up.wait_recv)
    upward(down.wait_recv)
    kind8 = lax.rem(lane8, 5 * BEAMS) // BEAMS
    kind8 = jnp.where(lane8 < USES, kind8, 0)
    mixed[...] = jnp.where(kind8 == 1, near[1], jnp.where(kind8 == 2, near[0], mine[...]))
    shares = []
    for other in range(1, COLS):
        share = pltpu.make_async_remote_copy(
            mixed, lines.at[other], line_send.at[other], line_recv.at[other],
            device_id=(row, lax.rem(col + other, COLS)), device_id_type=MESH,
        )
        share.start()
        shares.append(share)
    lines[0] = mixed[...]

    for step in ways:
        for route in both:
            started["a", route, step].wait_recv()
            send("b", route, 0, step, -step, 0, 0 if step > 0 else half, half)
        along_second(-step)

    for share in shares:
        share.wait_recv()
    listed, energy, over = list_uses(row, col, lines)
    uses_v[...] = listed.astype(jnp.int32)
    to_smem = pltpu.make_async_copy(uses_v, uses_s, local_sems.at[2])
    to_smem.start()
    flag_mine[...] = over
    alarms = []
    for other in range(1, ROWS):
        alarm = pltpu.make_async_remote_copy(
            flag_mine, flags.at[other], flag_send.at[other], flag_recv.at[other],
            device_id=(lax.rem(row + other, ROWS), col), device_id_type=MESH,
        )
        alarm.start()
        alarms.append(alarm)

    for route in both:
        for step in ways:
            started["b", route, step].wait_recv()
    along_second(2)
    pass_on(0)
    to_smem.wait()
    for copy in loads:
        copy.wait()
    image_some(0, 0, 56)
    pass_on(1)
    pass_on(-1)
    image_some(1, 0, 80)
    pass_on(2)
    arrived(0)
    image_some(2, 0, 40)
    early = total_of(0, listed, energy) + total_of(1, listed, energy) + total_of(2, listed, energy)
    raised = flag_mine[...]
    for alarm, other in zip(alarms, range(1, ROWS)):
        alarm.wait_recv()
        raised = jnp.maximum(raised, flags[other])
    flag_out[0] = jnp.max(raised).astype(jnp.int32)
    arrived(1)
    arrived(-1)
    image_some(3, 0, 32)
    sums[...] = (early + total_of(3, listed, energy)).reshape(COLS, 8, NS)

    pieces = []
    for n, (dz, dx) in enumerate(FAR_FIRST):
        there = at(dz, dx)
        piece = pltpu.make_async_remote_copy(
            sums.at[there], parts.at[n], part_send.at[n], part_recv.at[n],
            device_id=(row, there), device_id_type=MESH,
        )
        piece.start()
        pieces.append(piece)

    arrived(2)
    image_some(4, 0, 24)
    late[...] = total_of(4, listed, energy).reshape(COLS, 8, NS)
    across = at(2, 2)
    next_col, prev_col = lax.rem(across + 1, COLS), lax.rem(across + COLS - 1, COLS)
    next_row, prev_row = lax.rem(row + 1, ROWS), lax.rem(row + ROWS - 1, ROWS)
    direct = []
    for n, (there_row, there_col) in enumerate(
        ((row, across), (row, next_col), (row, prev_col), (next_row, across), (prev_row, across))
    ):
        copy = pltpu.make_async_remote_copy(
            late.at[there_col], late_in.at[n], late_send.at[n], late_recv.at[n],
            device_id=(there_row, there_col), device_id_type=MESH,
        )
        copy.start()
        direct.append(copy)
    whole = sums[col]
    for n, piece in enumerate(pieces):
        piece.wait_recv()
        whole += parts[n]
    edge[...] = whole
    to_next = pltpu.make_async_remote_copy(
        edge, edges.at[0], edge_send.at[0], edge_recv.at[0], device_id=(row + 1, col), device_id_type=MESH
    )
    to_prev = pltpu.make_async_remote_copy(
        edge, edges.at[1], edge_send.at[1], edge_recv.at[1], device_id=(row - 1, col), device_id_type=MESH
    )
    upward(to_next.start)
    downward(to_prev.start)
    for copy in started.values():
        copy.wait_send()
    for copy in shares + alarms + pieces + direct:
        copy.wait_send()
    for copy in direct:
        copy.wait_recv()
    straight = late_in[0] + late_in[1] + late_in[2]
    contrib = whole[1:2] + straight[1:2] + late_in[3][2:3] + late_in[4][0:1]
    lighting = whole[5:6] + straight[5:6] + late_in[3][6:7] + late_in[4][4:5]
    upward(up.wait_send)
    downward(down.wait_send)
    downward(to_next.wait_recv)
    upward(to_prev.wait_recv)
    contrib += edges[0][2:3] + edges[1][0:1]
    lighting += edges[0][6:7] + edges[1][4:5]
    out[0] = contrib / jnp.sqrt(1.0 + lighting)
    upward(to_next.wait_send)
    downward(to_prev.wait_send)


def row_of(route, first, second):
    c, n = WHERE[first, second]
    return (route * len(CLASSES[c][0]) + n) * BEAMS


def list_uses(row, col, lines):
    table = jnp.concatenate([lines[lax.rem(col - tile + COLS, COLS)][0:1, :] for tile in range(COLS)], axis=0)
    shape = (COLS, NS)
    lane = lax.broadcasted_iota(jnp.int32, shape, 1)
    tile = lax.broadcasted_iota(jnp.int32, shape, 0)
    shot, kind, beam = lane // (5 * BEAMS), lax.rem(lane, 5 * BEAMS) // BEAMS, lax.rem(lane, BEAMS)
    names = table.astype(jnp.int32)

    def of_source(own):
        before, after = pltpu.roll(own, 1, 0), pltpu.roll(own, COLS - 1, 0)
        return jnp.where(kind == 3, before, jnp.where(kind == 4, after, own))

    last, first = (row == ROWS - 1).astype(jnp.int32), (row == 0).astype(jnp.int32)
    missing = (
        ((kind == 1) & (last == 1))
        | ((kind == 2) & (first == 1))
        | ((kind == 3) & (tile == 0))
        | ((kind == 4) & (tile == COLS - 1))
    )
    counts = of_source(jnp.broadcast_to(names[:, COUNT : COUNT + 1], shape))
    energy = of_source(
        jnp.take_along_axis(
            table, jnp.where(lane < USES, ENERGY + shot * BEAMS + beam, lane), axis=1, mode="promise_in_bounds"
        )
    )
    live = (lane < USES) & (beam < counts) & jnp.logical_not(missing)
    owners = names // 128

    source = tile + (kind == 4).astype(jnp.int32) - (kind == 3).astype(jnp.int32)
    along_z = (source // SIDE - owners // SIDE) & (SIDE - 1)
    along_x = (source - owners) & (SIDE - 1)
    code = jnp.where(shot == 0, along_x * SIDE + along_z, along_z * SIDE + along_x)
    group, record = jnp.zeros(shape, jnp.int32), jnp.zeros(shape, jnp.int32)
    for (first_step, second_step), (c, _) in WHERE.items():
        same = code == first_step % SIDE * SIDE + second_step % SIDE
        group = jnp.where(same, c, group)
        begin = [row_of(route, first_step, second_step) for route in (0, 1)]
        record = jnp.where(same, jnp.where(shot == 0, begin[0], begin[1]) + beam, record)

    column = lax.broadcasted_iota(jnp.int32, (NS, NS), 1)
    owned = jnp.where(live, owners * 8 + group, -1)
    over = jnp.zeros((1, 1), jnp.float32)
    for c, (_, slots, _, _) in enumerate(CLASSES):
        per_owner = jnp.concatenate(
            [jnp.sum((owned == o * 8 + c).astype(jnp.float32), axis=0, keepdims=True) for o in range(COLS)], axis=0
        )
        held = jnp.sum(per_owner, axis=1, keepdims=True)
        over = jnp.maximum(over, jnp.max((held > float(slots)).astype(jnp.float32), keepdims=True))

    earlier = lax.broadcasted_iota(jnp.int32, (NS, NS), 0) <= column
    above = lax.broadcasted_iota(jnp.int32, (COLS, COLS), 1) < lax.broadcasted_iota(jnp.int32, (COLS, COLS), 0)
    shift = 1 + (kind == 1).astype(jnp.int32) - (kind == 2).astype(jnp.int32)
    place = jnp.full(shape, -1.0)
    for c, (_, slots, base, _) in enumerate(CLASSES):
        marks = live & (owners == col) & (group == c)
        ones = marks.astype(jnp.float32)
        within = jnp.dot(ones, earlier.astype(jnp.float32), preferred_element_type=jnp.float32)
        totals = jnp.broadcast_to(jnp.sum(ones, axis=1, keepdims=True), shape)
        ahead = jnp.dot(above.astype(jnp.float32), totals, preferred_element_type=jnp.float32)
        rank = within + ahead - 1.0
        place = jnp.where(marks & (rank < float(slots)), rank + float(base), place)
    high = energy.astype(jnp.bfloat16).astype(jnp.float32)
    middle = (energy - high).astype(jnp.bfloat16).astype(jnp.float32)
    low = energy - high - middle
    fields = (
        lax.rem(names, 128).astype(jnp.float32),
        record.astype(jnp.float32),
        (tile * 8 + shift + 1).astype(jnp.float32),
        high,
        middle,
        low,
    )
    upright = jnp.transpose(place)
    slot = lax.broadcasted_iota(jnp.int32, (NS, SLOTS), 1).astype(jnp.float32)
    line = lax.broadcasted_iota(jnp.int32, (8, NS), 0)
    listed = jnp.zeros((8, SLOTS), jnp.float32)
    for t in range(COLS):
        here = (jnp.broadcast_to(upright[:, t : t + 1], (NS, SLOTS)) == slot).astype(jnp.bfloat16)
        rows = jnp.zeros((8, NS), jnp.float32)
        for f, field in enumerate(fields):
            rows = jnp.where(line == f, jnp.broadcast_to(field[t : t + 1, :], (8, NS)), rows)
        listed += jnp.dot(rows.astype(jnp.bfloat16), here, preferred_element_type=jnp.float32)
    return listed, listed[3:4] + listed[4:5] + listed[5:6], jnp.broadcast_to(over, (8, NS))


def fused(records, owner, block, count, travel, amp):
    vmem = pl.BlockSpec(memory_space=pltpu.VMEM)
    smem = pl.BlockSpec(memory_space=pltpu.SMEM)
    hbm = pl.BlockSpec(memory_space=pl.ANY)
    dma = pltpu.SemaphoreType.DMA
    f32 = jnp.float32
    return pl.pallas_call(
        fused_kernel,
        out_shape=(jax.ShapeDtypeStruct((1, 1, NS), f32), jax.ShapeDtypeStruct((1,), jnp.int32)),
        in_specs=[hbm, hbm, hbm, smem, hbm, hbm],
        out_specs=(vmem, smem),
        scratch_shapes=[
            pltpu.VMEM(((SHOTS * NP + 1) * BEAMS, NS), f32),
            *[pltpu.VMEM((held, NP, NS), jnp.bfloat16) for _, _, _, held in CLASSES],
            pltpu.VMEM(travel.shape, f32),
            pltpu.VMEM(amp.shape, f32),
            pltpu.VMEM((8, NS), f32),
            pltpu.VMEM((2, 8, NS), f32),
            pltpu.VMEM((8, NS), f32),
            pltpu.VMEM((COLS, 8, NS), f32),
            pltpu.VMEM((8, SLOTS), jnp.int32),
            pltpu.SMEM((8, SLOTS), jnp.int32),
            *[pltpu.VMEM((9 * slots, NS), f32) for _, slots, _, _ in CLASSES],
            *[pltpu.VMEM((9 * slots, NS), f32) for _, slots, _, _ in CLASSES],
            pltpu.VMEM((8, NS), f32),
            pltpu.VMEM((ROWS, 8, NS), f32),
            pltpu.VMEM((COLS, 8, NS), f32),
            pltpu.VMEM((COLS, 8, NS), f32),
            pltpu.VMEM((8, NS), f32),
            pltpu.VMEM((2, 8, NS), f32),
            pltpu.VMEM(records.shape, records.dtype),
            pltpu.VMEM(owner.shape, jnp.int32),
            pltpu.VMEM(block.shape, jnp.int32),
            pltpu.SemaphoreType.REGULAR((3,)),
            dma((6,)),
            dma((COPIES,)),
            dma((COPIES,)),
            dma((2,)),
            dma((2,)),
            dma((COLS,)),
            dma((COLS,)),
            dma((ROWS,)),
            dma((ROWS,)),
            dma((COLS,)),
            dma((COLS,)),
            dma((2,)),
            dma((2,)),
            pltpu.VMEM((COLS, 8, NS), f32),
            pltpu.VMEM((5, 8, NS), f32),
            dma((5,)),
            dma((5,)),
        ],
        compiler_params=pltpu.CompilerParams(
            collective_id=0, has_side_effects=True, vmem_limit_bytes=40 << 20
        ),
        cost_estimate=pl.CostEstimate(flops=10_000_000, bytes_accessed=16_000_000, transcendentals=0),
        name="migrate",
    )(records, owner, block, count, travel, amp)


def per_device(records, beam_count, owner_list, block_list, travel_table, amp_table):
    travel_table = pltpu.with_memory_space_constraint(travel_table, pltpu.HBM)
    amp_table = pltpu.with_memory_space_constraint(amp_table, pltpu.HBM)
    by_slowness = records.reshape(SHOTS, BEAMS, NP, NS).transpose(0, 2, 1, 3)
    owner, block = owner_list.reshape(1, USES), block_list.reshape(1, USES)
    quick, flag = fused(by_slowness, owner, block, beam_count, travel_table, amp_table)
    return lax.cond(
        flag[0] > 0,
        lambda: imaged_by_any_count(records, beam_count, owner_list, block_list, travel_table, amp_table),
        lambda: quick,
    )


def solution(mesh):
    placed = (
        P(None, "inline", "xline", None, None),
        P("inline", "xline"),
        P(("inline", "xline"), None),
        P(("inline", "xline"), None),
        P("xline", None, None),
        P("xline", None, None),
    )
    return jax.shard_map(
        per_device,
        mesh=mesh,
        in_specs=placed,
        out_specs=P("inline", "xline", None),
        check_vma=False,
    )
```

```python
import jax
import jax.numpy as jnp
from jax import lax
from jax.experimental import pallas as pl
from jax.experimental.pallas import tpu as pltpu
from jax.sharding import PartitionSpec as P

NS = 128
NP = 64
BEAMS = 8
SHOTS = 2
RECS = SHOTS * BEAMS
SIDE = 4
COLS = SIDE * SIDE
ROWS = 8
USES = 5 * RECS
LIST = 512
TARGETS = 3 * COLS
GROUP = 8
MESH = pl.DeviceIdType.MESH

ENERGY = USES
COUNT = USES + RECS


def greet(row, col):
    barrier = pltpu.get_barrier_semaphore()
    for other in range(1, COLS):
        pl.semaphore_signal(
            barrier, inc=1, device_id=(row, lax.rem(col + other, COLS)), device_id_type=MESH
        )

    @pl.when(row > 0)
    def _():
        pl.semaphore_signal(barrier, inc=1, device_id=(row - 1, col), device_id_type=MESH)

    @pl.when(row < ROWS - 1)
    def _():
        pl.semaphore_signal(barrier, inc=1, device_id=(row + 1, col), device_id_type=MESH)

    edges = (row > 0).astype(jnp.int32) + (row < ROWS - 1).astype(jnp.int32)
    pl.semaphore_wait(barrier, COLS - 1 + edges)


def gather_kernel(
    records, index, travel, amp,
    held, travel_out, amp_out, uses_out, index_out,
    near, mixed, lines, uses_vmem, index_vmem,
    local_sems, send_sems, recv_sems, near_send, near_recv, line_send, line_recv,
):
    row, col = lax.axis_index("inline"), lax.axis_index("xline")
    z, x = col // SIDE, lax.rem(col, SIDE)
    loads = [
        pltpu.make_async_copy(travel, travel_out, local_sems.at[0]),
        pltpu.make_async_copy(amp, amp_out, local_sems.at[1]),
        pltpu.make_async_copy(records, held.at[pl.ds(col * RECS, RECS)], local_sems.at[2]),
    ]
    near[...] = jnp.zeros_like(near)
    greet(row, col)

    def at(dz, dx):
        return lax.rem(z + dz + SIDE, SIDE) * SIDE + lax.rem(x + dx + SIDE, SIDE)

    started = {}

    def block(route, first, second, lo, size):
        tile = at(second, first) if route == 0 else at(first, second)
        return pl.ds(tile * RECS + route * BEAMS + lo, size)

    def toward(route, axis, step):
        along_x = (axis == 0) == (route == 0)
        return (row, at(0, step) if along_x else at(step, 0))

    def send(key, route, axis, step, first, second, lo, size):
        here = block(route, first, second, lo, size)
        n = len(started)
        if first == 0 and second == 0:
            source = records.at[pl.ds(route * BEAMS + lo, size)]
        else:
            source = held.at[here]
        copy = pltpu.make_async_remote_copy(
            src_ref=source,
            dst_ref=held.at[here],
            send_sem=send_sems.at[n],
            recv_sem=recv_sems.at[n],
            device_id=toward(route, axis, step),
            device_id_type=MESH,
        )
        copy.start()
        started[key] = copy

    half = BEAMS // 2
    both = (0, 1)
    for route in both:
        for step in (1, -1):
            send(("a", route, step), route, 0, step, 0, 0, 0, BEAMS)
    for route in both:
        for step in (1, -1):
            send(("c", route, 0, step), route, 1, step, 0, 0, 0, BEAMS)
    for copy in loads:
        copy.start()

    up = pltpu.make_async_remote_copy(
        index, near.at[0], near_send.at[0], near_recv.at[0], device_id=(row + 1, col), device_id_type=MESH
    )
    down = pltpu.make_async_remote_copy(
        index, near.at[1], near_send.at[1], near_recv.at[1], device_id=(row - 1, col), device_id_type=MESH
    )
    @pl.when(row < ROWS - 1)
    def _():
        up.start()

    @pl.when(row > 0)
    def _():
        down.start()

    @pl.when(row > 0)
    def _():
        up.wait_recv()

    @pl.when(row < ROWS - 1)
    def _():
        down.wait_recv()

    @pl.when(row < ROWS - 1)
    def _():
        up.wait_send()

    @pl.when(row > 0)
    def _():
        down.wait_send()

    kind = lax.broadcasted_iota(jnp.int32, (8, NS), 1) // RECS
    mixed[...] = jnp.where(kind == 1, near[1], jnp.where(kind == 2, near[0], index[...]))
    shares = []
    for other in range(1, COLS):
        share = pltpu.make_async_remote_copy(
            mixed,
            lines.at[other],
            line_send.at[other],
            line_recv.at[other],
            device_id=(row, lax.rem(col + other, COLS)),
            device_id_type=MESH,
        )
        share.start()
        shares.append(share)
    lines[0] = mixed[...]

    for route in both:
        for step in (1, -1):
            started["a", route, step].wait_recv()
            lo = 0 if step > 0 else half
            send(("b", route, step), route, 0, step, -step, 0, lo, half)
            for way in (1, -1):
                send(("c", route, -step, way), route, 1, way, -step, 0, 0, BEAMS)
    for route in both:
        for way in (1, -1):
            started["c", route, 0, way].wait_recv()
            lo = 0 if way > 0 else half
            send(("d", route, 0, way), route, 1, way, 0, -way, lo, half)

    build_list(row, col, shares, lines, index_vmem, uses_vmem)

    for route in both:
        for step in (1, -1):
            started["b", route, step].wait_recv()
        for way in (1, -1):
            send(("c", route, 2, way), route, 1, way, 2, 0, 0, BEAMS)
    for first in (-1, 1, 2):
        for route in both:
            for way in (1, -1):
                started["c", route, first, way].wait_recv()
                lo = 0 if way > 0 else half
                send(("d", route, first, way), route, 1, way, first, -way, lo, half)
    finish = [
        pltpu.make_async_copy(uses_vmem, uses_out, local_sems.at[3]),
        pltpu.make_async_copy(index_vmem, index_out, local_sems.at[4]),
    ]
    for copy in finish:
        copy.start()
    for first in (0, -1, 1, 2):
        for route in both:
            for way in (1, -1):
                started["d", route, first, way].wait_recv()
    for copy in started.values():
        copy.wait_send()
    for share in shares:
        share.wait_send()
    for copy in loads + finish:
        copy.wait()


def build_list(row, col, shares, lines, index_vmem, uses_vmem):
    for share in shares:
        share.wait_recv()
    for tile in range(COLS):
        index_vmem[pl.ds(tile, 1), :] = lines[lax.rem(col - tile + COLS, COLS)][0:1, :]
    table = index_vmem[...]
    names = table.astype(jnp.int32)
    shape = (COLS, NS)
    lane = lax.broadcasted_iota(jnp.int32, shape, 1)
    tile = lax.broadcasted_iota(jnp.int32, shape, 0)
    kind, beam = lane // RECS, lax.rem(lane, BEAMS)
    counts = jnp.broadcast_to(names[:, COUNT : COUNT + 1], shape)
    before = jnp.where(tile > 0, pltpu.roll(counts, 1, 0), 0)
    after = jnp.where(tile < COLS - 1, pltpu.roll(counts, COLS - 1, 0), 0)
    last, first = (row == ROWS - 1).astype(jnp.int32), (row == 0).astype(jnp.int32)
    live = jnp.where(kind == 3, before, jnp.where(kind == 4, after, counts))
    live = jnp.where(kind == 1, counts * (1 - last), live)
    live = jnp.where(kind == 2, counts * (1 - first), live)
    wanted = (lane < USES) & (beam < live) & (names // 128 == col)
    marks = wanted.astype(jnp.float32)
    earlier = lax.broadcasted_iota(jnp.int32, (NS, NS), 0) <= lax.broadcasted_iota(jnp.int32, (NS, NS), 1)
    within = jnp.dot(marks, earlier.astype(jnp.float32), preferred_element_type=jnp.float32)
    above = lax.broadcasted_iota(jnp.int32, (COLS, COLS), 1) < lax.broadcasted_iota(jnp.int32, (COLS, COLS), 0)
    totals = jnp.broadcast_to(jnp.sum(marks, axis=1, keepdims=True), shape)
    ahead = jnp.dot(above.astype(jnp.float32), totals, preferred_element_type=jnp.float32)
    place = jnp.where(wanted, within + ahead - 1.0, -1.0)
    number = jnp.sum(marks)

    source = tile + (kind == 4).astype(jnp.int32) - (kind == 3).astype(jnp.int32)
    shift = 1 + (kind == 1).astype(jnp.int32) - (kind == 2).astype(jnp.int32)
    fields = (
        lax.rem(names, 128).astype(jnp.float32),
        (source * RECS + lax.rem(lane, RECS)).astype(jnp.float32),
        (shift * COLS + tile).astype(jnp.float32),
    )
    upright = jnp.transpose(place)
    slot = lax.broadcasted_iota(jnp.int32, (NS, LIST), 1).astype(jnp.float32)
    line = lax.broadcasted_iota(jnp.int32, (8, NS), 0)
    listed = jnp.zeros((8, LIST), jnp.float32)
    for t in range(COLS):
        here = (jnp.broadcast_to(upright[:, t : t + 1], (NS, LIST)) == slot).astype(jnp.bfloat16)
        rows = jnp.zeros((8, NS), jnp.float32)
        for f, field in enumerate(fields):
            rows = jnp.where(line == f, jnp.broadcast_to(field[t : t + 1, :], (8, NS)), rows)
        listed += jnp.dot(rows.astype(jnp.bfloat16), here, preferred_element_type=jnp.float32)
    place_in = lax.broadcasted_iota(jnp.int32, (8, LIST), 1).astype(jnp.float32)
    part = lax.broadcasted_iota(jnp.int32, (8, LIST), 0)
    listed = jnp.where((part == 2) & (place_in >= number), float(TARGETS), listed)
    listed = jnp.where(part == 3, number, listed)
    uses_vmem[...] = listed.astype(jnp.int32)


def gather(records, index, travel, amp):
    hbm = pl.BlockSpec(memory_space=pl.ANY)
    vmem = pl.BlockSpec(memory_space=pltpu.VMEM)
    smem = pl.BlockSpec(memory_space=pltpu.SMEM)
    return pl.pallas_call(
        gather_kernel,
        out_shape=(
            pltpu.VMEM((COLS * RECS, NP, NS), jnp.bfloat16),
            pltpu.VMEM(travel.shape, jnp.float32),
            pltpu.VMEM(amp.shape, jnp.float32),
            jax.ShapeDtypeStruct((8, LIST), jnp.int32),
            jax.ShapeDtypeStruct((COLS, NS), jnp.float32),
        ),
        in_specs=[hbm, vmem, hbm, hbm],
        out_specs=(vmem, vmem, vmem, hbm, hbm),
        scratch_shapes=[
            pltpu.VMEM((2, 8, NS), jnp.float32),
            pltpu.VMEM((8, NS), jnp.float32),
            pltpu.VMEM((COLS, 8, NS), jnp.float32),
            pltpu.VMEM((8, LIST), jnp.int32),
            pltpu.VMEM((COLS, NS), jnp.float32),
            pltpu.SemaphoreType.DMA((5,)),
            pltpu.SemaphoreType.DMA((40,)),
            pltpu.SemaphoreType.DMA((40,)),
            pltpu.SemaphoreType.DMA((2,)),
            pltpu.SemaphoreType.DMA((2,)),
            pltpu.SemaphoreType.DMA((COLS,)),
            pltpu.SemaphoreType.DMA((COLS,)),
        ],
        compiler_params=pltpu.CompilerParams(
            collective_id=1, has_side_effects=True, vmem_limit_bytes=32 << 20
        ),
        cost_estimate=pl.CostEstimate(flops=10_000_000, bytes_accessed=16_000_000, transcendentals=0),
        name="gather_records",
    )(records, index, travel, amp)


def image_kernel(uses, index, records, travel, amp, out, acc):
    acc[...] = jnp.zeros_like(acc)

    def step(i, carry):
        picked = []
        for d in range(GROUP):
            u = i * GROUP + d
            picked.append((uses[0, u], uses[1, u], uses[2, u]))
        totals = [jnp.zeros((8, NS), jnp.float32) for _ in picked]
        squares = [jnp.zeros((8, NS), jnp.float32) for _ in picked]
        for q in range(NP // 8):
            rows = pl.ds(8 * q, 8)
            for d, (block, rec, _) in enumerate(picked):
                t = travel[block, rows, :]
                a = amp[block, rows, :]
                pair = records[rec, pl.ds(16 * (q // 2), 16), :].astype(jnp.float32)
                r = pair[8 * (q % 2) : 8 * (q % 2) + 8]
                k = t.astype(jnp.int32)
                f = t - k.astype(jnp.float32)
                w0 = (1.0 - f).astype(jnp.bfloat16).astype(jnp.float32)
                w1 = f.astype(jnp.bfloat16).astype(jnp.float32)
                v0 = jnp.take_along_axis(r, k, axis=1, mode="promise_in_bounds")
                v1 = jnp.take_along_axis(r, k + 1, axis=1, mode="promise_in_bounds")
                totals[d] += a * (v0 * w0 + v1 * w1)
                squares[d] += a * a
        for d, (_, rec, target) in enumerate(picked):
            energy = index[rec // RECS, ENERGY + lax.rem(rec, RECS)]
            acc[target, 0] += totals[d]
            acc[target, 1] += squares[d] * energy
        return carry

    lax.fori_loop(0, (uses[3, 0] + GROUP - 1) // GROUP, step, 0)
    out[...] = jnp.sum(acc[pl.ds(0, TARGETS)], axis=2)


def image(uses, index, records, travel, amp):
    vmem = pl.BlockSpec(memory_space=pltpu.VMEM)
    smem = pl.BlockSpec(memory_space=pltpu.SMEM)
    return pl.pallas_call(
        image_kernel,
        out_shape=pltpu.VMEM((TARGETS, 2, NS), jnp.float32),
        in_specs=[smem, smem, vmem, vmem, vmem],
        out_specs=vmem,
        scratch_shapes=[pltpu.VMEM((TARGETS + 1, 2, 8, NS), jnp.float32)],
        compiler_params=pltpu.CompilerParams(vmem_limit_bytes=32 << 20),
        cost_estimate=pl.CostEstimate(flops=10_000_000, bytes_accessed=8_000_000, transcendentals=0),
        name="image_uses",
    )(uses, index, records, travel, amp)


def exchange_kernel(sums, out, near, total, parts, near_send, near_recv, part_send, part_recv):
    row, col = lax.axis_index("inline"), lax.axis_index("xline")
    greet(row, col)
    up = pltpu.make_async_remote_copy(
        sums.at[2], near.at[0], near_send.at[0], near_recv.at[0], device_id=(row + 1, col), device_id_type=MESH
    )
    down = pltpu.make_async_remote_copy(
        sums.at[0], near.at[1], near_send.at[1], near_recv.at[1], device_id=(row - 1, col), device_id_type=MESH
    )

    @pl.when(row < ROWS - 1)
    def _():
        up.start()

    @pl.when(row > 0)
    def _():
        down.start()

    total[...] = sums[1]

    @pl.when(row > 0)
    def _():
        up.wait_recv()
        total[...] += near[0]

    @pl.when(row < ROWS - 1)
    def _():
        down.wait_recv()
        total[...] += near[1]

    copies = []
    for other in range(1, COLS):
        there = lax.rem(col + other, COLS)
        copy = pltpu.make_async_remote_copy(
            total.at[there],
            parts.at[other],
            part_send.at[other],
            part_recv.at[other],
            device_id=(row, there),
            device_id_type=MESH,
        )
        copy.start()
        copies.append(copy)
    mine = total[col]
    for copy, other in zip(copies, range(1, COLS)):
        copy.wait_recv()
        mine += parts[other]
    out[0] = mine[0:1] / jnp.sqrt(1.0 + mine[1:2])
    for copy in copies:
        copy.wait_send()

    @pl.when(row < ROWS - 1)
    def _():
        up.wait_send()

    @pl.when(row > 0)
    def _():
        down.wait_send()


def exchange(sums):
    vmem = pl.BlockSpec(memory_space=pltpu.VMEM)
    return pl.pallas_call(
        exchange_kernel,
        out_shape=jax.ShapeDtypeStruct((1, 1, NS), jnp.float32),
        in_specs=[vmem],
        out_specs=vmem,
        scratch_shapes=[
            pltpu.VMEM((2, COLS, 2, NS), jnp.float32),
            pltpu.VMEM((COLS, 2, NS), jnp.float32),
            pltpu.VMEM((COLS, 2, NS), jnp.float32),
            pltpu.SemaphoreType.DMA((2,)),
            pltpu.SemaphoreType.DMA((2,)),
            pltpu.SemaphoreType.DMA((COLS,)),
            pltpu.SemaphoreType.DMA((COLS,)),
        ],
        compiler_params=pltpu.CompilerParams(collective_id=2, has_side_effects=True),
        cost_estimate=pl.CostEstimate(flops=10_000, bytes_accessed=100_000, transcendentals=0),
        name="exchange_sums",
    )(sums)


def imaged_by_any_count(records, beam_count, owner_list, block_list, travel_table, amp_table):
    records = records.reshape(RECS, NP, NS)
    named = (owner_list * 128 + block_list)[:, 0].astype(jnp.float32)
    named = named.reshape(SHOTS, 5, BEAMS).transpose(1, 0, 2).reshape(USES)
    energy = jnp.mean(jnp.square(records.astype(jnp.float32)), axis=(1, 2))
    count = jnp.broadcast_to(beam_count[0].astype(jnp.float32), (NS - COUNT,))
    index = jnp.broadcast_to(jnp.concatenate([named, energy, count]), (8, NS))
    gathered, travel, amp, uses, index = gather(records, index, travel_table, amp_table)
    sums = image(uses, index, gathered, travel, amp)
    return exchange(sums.reshape(3, COLS, 2, NS))


CLASSES = (
    (((0, 0), (1, 0), (-1, 0), (2, 0)), 48, 0, 64),
    (((0, 1), (0, -1), (1, 1), (1, -1), (-1, 1), (-1, -1)), 64, 64, 128),
    (((2, 1), (2, -1), (0, 2)), 40, 144, 64),
    (((1, 2), (-1, 2)), 32, 184, 32),
    (((2, 2),), 24, 216, 16),
)
WHERE = {tile: (c, n) for c, (tiles, _, _, _) in enumerate(CLASSES) for n, tile in enumerate(tiles)}
FAR_FIRST = sorted(
    ((dz, dx) for dz in (0, 1, -1, 2) for dx in (0, 1, -1, 2) if (dz, dx) != (0, 0)),
    key=lambda step: -abs(step[0]) - abs(step[1]),
)
SLOTS = 256
NBLOCKS = 128
COPIES = 40


def wrap(steps):
    return (steps + 1) % SIDE - 1


def fused_kernel(
    records, owner, block, count, travel, amp,
    out, flag_out,
    wide, buf0, buf1, buf2, buf3, buf4, travel_v, amp_v,
    mine, near, mixed, lines, uses_v, uses_s,
    con0, con1, con2, con3, con4, lit0, lit1, lit2, lit3, lit4,
    flag_mine, flags, sums, parts, edges, records_v, owner_v, block_v, met,
    local_sems, send_sems, recv_sems, near_send, near_recv, line_send, line_recv,
    flag_send, flag_recv, part_send, part_recv, edge_send, edge_recv,
    early_v, late_v, last_v, late_in, late_send, late_recv,
):
    row, col = lax.axis_index("inline"), lax.axis_index("xline")
    z, x = col // SIDE, lax.rem(col, SIDE)
    bufs = (buf0, buf1, buf2, buf3, buf4)
    cons, lits = (con0, con1, con2, con3, con4), (lit0, lit1, lit2, lit3, lit4)
    near[...] = jnp.zeros_like(near)
    edges[...] = jnp.zeros_like(edges)

    def at(dz, dx):
        return lax.rem(z + dz + SIDE, SIDE) * SIDE + lax.rem(x + dx + SIDE, SIDE)

    beside = [(row, at(dz, dx)) for dz, dx in ((0, 1), (0, -1), (1, 0), (-1, 0))]
    beside += [(lax.rem(row + 1, ROWS), col), (lax.rem(row + ROWS - 1, ROWS), col)]
    barrier = pltpu.get_barrier_semaphore()
    for there in beside:
        pl.semaphore_signal(barrier, inc=1, device_id=there, device_id_type=MESH)
    inputs = [
        pltpu.make_async_copy(records, records_v, local_sems.at[3]),
        pltpu.make_async_copy(owner, owner_v, local_sems.at[4]),
        pltpu.make_async_copy(block, block_v, local_sems.at[5]),
    ]
    for copy in inputs:
        copy.start()
    loads = [
        pltpu.make_async_copy(travel, travel_v, local_sems.at[0]),
        pltpu.make_async_copy(amp, amp_v, local_sems.at[1]),
    ]
    for copy in loads:
        copy.start()

    for copy in inputs:
        copy.wait()

    wide[pl.ds(0, SHOTS * NP * BEAMS), :] = records_v[...].astype(jnp.float32).reshape(SHOTS * NP * BEAMS, NS)
    energies = jnp.zeros((8, NS), jnp.float32)
    lane8 = lax.broadcasted_iota(jnp.int32, (8, NS), 1)
    for s in range(SHOTS):
        for b in range(BEAMS):
            rec = wide[pl.ds(s * NP * BEAMS + b, NP, stride=BEAMS), :]
            bufs[0][row_of(s, 0, 0) + b] = rec.astype(jnp.bfloat16)
            energy = jnp.sum(rec * rec, keepdims=True) * (1.0 / (NP * NS))
            energies = jnp.where(lane8 == ENERGY + s * BEAMS + b, jnp.broadcast_to(energy, (8, NS)), energies)
    named = (owner_v[...] * 128 + block_v[...]).astype(jnp.float32)
    mine[...] = jnp.where(lane8 >= COUNT, count[0, 0].astype(jnp.float32), energies)
    mine[:, 0:USES] = jnp.broadcast_to(named, (8, USES))
    pl.semaphore_wait(barrier, len(beside))

    started = {}

    def send(kind, route, axis, step, first, second, lo, size):
        seen = (wrap(first - step), second) if axis == 0 else (first, wrap(second - step))
        here, there = WHERE[first, second][0], WHERE[seen][0]
        along_x = (axis == 0) == (route == 0)
        n = len(started)
        copy = pltpu.make_async_remote_copy(
            src_ref=bufs[here].at[pl.ds(row_of(route, first, second) + lo, size)],
            dst_ref=bufs[there].at[pl.ds(row_of(route, *seen) + lo, size)],
            send_sem=send_sems.at[n],
            recv_sem=recv_sems.at[n],
            device_id=(row, at(0, step) if along_x else at(step, 0)),
            device_id_type=MESH,
        )
        copy.start()
        key = (kind, route, step) if axis == 0 else (kind, route, first, step)
        started[key] = copy

    both, ways = (0, 1), (1, -1)
    half = BEAMS // 2

    def along_second(first):
        for way in ways:
            for route in both:
                send("c", route, 1, way, first, 0, 0, BEAMS)

    def pass_on(first):
        for way in ways:
            for route in both:
                started["c", route, first, way].wait_recv()
                send("d", route, 1, way, first, -way, 0 if way > 0 else half, half)

    def arrived(first):
        for route in both:
            for way in ways:
                started["d", route, first, way].wait_recv()

    def image_some(p, begin, end):
        _, slots, base, held = CLASSES[p]
        buf, con, lit = bufs[p], cons[p], lits[p]

        def step(i, carry):
            places = [base + i * GROUP + d for d in range(GROUP)]
            picked = [(uses_s[0, u] & (NBLOCKS - 1), uses_s[1, u] & (held - 1)) for u in places]
            totals = [jnp.zeros((8, NS), jnp.float32) for _ in picked]
            squares = [jnp.zeros((8, NS), jnp.float32) for _ in picked]
            for q in range(NP // 8):
                rows = pl.ds(8 * q, 8)
                for d, (number, rec) in enumerate(picked):
                    t = travel_v[number, rows, :]
                    a = amp_v[number, rows, :]
                    pair = buf[rec, pl.ds(16 * (q // 2), 16), :].astype(jnp.float32)
                    r = pair[8 * (q % 2) : 8 * (q % 2) + 8]
                    k = t.astype(jnp.int32)
                    f = t - k.astype(jnp.float32)
                    w0 = (1.0 - f).astype(jnp.bfloat16).astype(jnp.float32)
                    w1 = f.astype(jnp.bfloat16).astype(jnp.float32)
                    v0 = jnp.take_along_axis(r, k, axis=1, mode="promise_in_bounds")
                    v1 = jnp.take_along_axis(r, k + 1, axis=1, mode="promise_in_bounds")
                    totals[d] += a * (v0 * w0 + v1 * w1)
                    squares[d] += a * a
            for d in range(GROUP):
                con[pl.ds(i * GROUP + d, 8, stride=slots), :] = totals[d]
                lit[pl.ds(i * GROUP + d, 8, stride=slots), :] = squares[d]
            return carry

        lax.fori_loop(begin // GROUP, end // GROUP, step, 0)

    def total_of(p, listed, energy):
        _, slots, base, _ = CLASSES[p]
        con = sum(cons[p][pl.ds(s * slots, slots), :] for s in range(8))
        lit = sum(lits[p][pl.ds(s * slots, slots), :] for s in range(8))
        target = jnp.broadcast_to(listed[2:3, base : base + slots], (NS, slots))
        weight = jnp.broadcast_to(energy[:, base : base + slots], (NS, slots))
        line = (lax.broadcasted_iota(jnp.int32, (NS, slots), 0) + 1).astype(jnp.float32)
        to_con = jnp.where(target == line, 1.0, 0.0)
        to_lit = jnp.where((target + 4.0 == line) & (target > 0.0), weight, 0.0)
        dot = lambda m, v: jnp.dot(m, v, precision=lax.Precision.HIGHEST, preferred_element_type=jnp.float32)
        return dot(to_con, con) + dot(to_lit, lit)

    for step in ways:
        for route in both:
            send("a", route, 0, step, 0, 0, 0, BEAMS)
    along_second(0)

    up = pltpu.make_async_remote_copy(
        mine, near.at[0], near_send.at[0], near_recv.at[0], device_id=(row + 1, col), device_id_type=MESH
    )
    down = pltpu.make_async_remote_copy(
        mine, near.at[1], near_send.at[1], near_recv.at[1], device_id=(row - 1, col), device_id_type=MESH
    )
    upward, downward = pl.when(row < ROWS - 1), pl.when(row > 0)
    upward(up.start)
    downward(down.start)
    for turn in range(3):
        for there in beside:
            pl.semaphore_signal(met.at[turn], inc=1, device_id=there, device_id_type=MESH)
        pl.semaphore_wait(met.at[turn], len(beside))
    downward(up.wait_recv)
    upward(down.wait_recv)
    kind8 = lax.rem(lane8, 5 * BEAMS) // BEAMS
    kind8 = jnp.where(lane8 < USES, kind8, 0)
    mixed[...] = jnp.where(kind8 == 1, near[1], jnp.where(kind8 == 2, near[0], mine[...]))
    shares = []
    for other in range(1, COLS):
        share = pltpu.make_async_remote_copy(
            mixed, lines.at[other], line_send.at[other], line_recv.at[other],
            device_id=(row, lax.rem(col + other, COLS)), device_id_type=MESH,
        )
        share.start()
        shares.append(share)
    lines[0] = mixed[...]

    for step in ways:
        for route in both:
            started["a", route, step].wait_recv()
            send("b", route, 0, step, -step, 0, 0 if step > 0 else half, half)
        along_second(-step)

    for share in shares:
        share.wait_recv()
    listed, energy, over = list_uses(row, col, lines)
    uses_v[...] = listed.astype(jnp.int32)
    to_smem = pltpu.make_async_copy(uses_v, uses_s, local_sems.at[2])
    to_smem.start()
    flag_mine[...] = over
    alarms = []
    for other in range(1, ROWS):
        alarm = pltpu.make_async_remote_copy(
            flag_mine, flags.at[other], flag_send.at[other], flag_recv.at[other],
            device_id=(lax.rem(row + other, ROWS), col), device_id_type=MESH,
        )
        alarm.start()
        alarms.append(alarm)

    for route in both:
        for step in ways:
            started["b", route, step].wait_recv()
    along_second(2)
    pass_on(0)
    to_smem.wait()
    for copy in loads:
        copy.wait()
    image_some(0, 0, 48)
    pass_on(1)
    pass_on(-1)
    image_some(1, 0, 64)
    pass_on(2)
    early = total_of(0, listed, energy) + total_of(1, listed, energy)
    arrived(0)
    image_some(2, 0, 40)
    early += total_of(2, listed, energy)
    early_v[...] = early.reshape(COLS, 8, NS)
    to_next = pltpu.make_async_remote_copy(
        early_v, edges.at[0], edge_send.at[0], edge_recv.at[0], device_id=(row + 1, col), device_id_type=MESH
    )
    to_prev = pltpu.make_async_remote_copy(
        early_v, edges.at[1], edge_send.at[1], edge_recv.at[1], device_id=(row - 1, col), device_id_type=MESH
    )
    upward(to_next.start)
    downward(to_prev.start)
    raised = flag_mine[...]
    for alarm, other in zip(alarms, range(1, ROWS)):
        alarm.wait_recv()
        raised = jnp.maximum(raised, flags[other])
    flag_out[0] = jnp.max(raised).astype(jnp.int32)
    arrived(1)
    arrived(-1)
    image_some(3, 0, 32)
    late_v[...] = total_of(3, listed, energy).reshape(COLS, 8, NS)
    next_row, prev_row = lax.rem(row + 1, ROWS), lax.rem(row + ROWS - 1, ROWS)
    direct = []

    def straight(source, dz, dx):
        for beside_row in (next_row, prev_row):
            n = len(direct)
            copy = pltpu.make_async_remote_copy(
                source.at[at(dz, dx)], late_in.at[n], late_send.at[n], late_recv.at[n],
                device_id=(beside_row, at(dz, dx)), device_id_type=MESH,
            )
            copy.start()
            direct.append(copy)

    for dz, dx in ((2, 1), (2, -1), (1, 2), (-1, 2)):
        straight(late_v, dz, dx)
    arrived(2)
    image_some(4, 0, 24)
    last_v[...] = total_of(4, listed, energy).reshape(COLS, 8, NS)
    straight(last_v, 2, 2)
    downward(to_next.wait_recv)
    upward(to_prev.wait_recv)
    own = early_v[...] + late_v[...] + last_v[...]
    sums[...] = own + pltpu.roll(edges[0], 7, 1) + pltpu.roll(edges[1], 1, 1)

    pieces = []
    for n, (dz, dx) in enumerate(FAR_FIRST):
        there = at(dz, dx)
        piece = pltpu.make_async_remote_copy(
            sums.at[there], parts.at[n], part_send.at[n], part_recv.at[n],
            device_id=(row, there), device_id_type=MESH,
        )
        piece.start()
        pieces.append(piece)
    for copy in started.values():
        copy.wait_send()
    for copy in shares + alarms + direct:
        copy.wait_send()
    upward(up.wait_send)
    downward(down.wait_send)
    upward(to_next.wait_send)
    downward(to_prev.wait_send)
    contrib, lighting = sums[col][1:2], sums[col][5:6]
    for n, copy in enumerate(direct):
        copy.wait_recv()
        line = 2 if n % 2 == 0 else 0
        contrib += late_in[n][line : line + 1]
        lighting += late_in[n][line + 4 : line + 5]
    whole = jnp.zeros((8, NS), jnp.float32)
    for n, piece in enumerate(pieces):
        piece.wait_recv()
        whole += parts[n]
    out[0] = (contrib + whole[1:2]) / jnp.sqrt(1.0 + (lighting + whole[5:6]))
    for piece in pieces:
        piece.wait_send()


def row_of(route, first, second):
    c, n = WHERE[first, second]
    return (route * len(CLASSES[c][0]) + n) * BEAMS


def list_uses(row, col, lines):
    table = jnp.concatenate([lines[lax.rem(col - tile + COLS, COLS)][0:1, :] for tile in range(COLS)], axis=0)
    shape = (COLS, NS)
    lane = lax.broadcasted_iota(jnp.int32, shape, 1)
    tile = lax.broadcasted_iota(jnp.int32, shape, 0)
    shot, kind, beam = lane // (5 * BEAMS), lax.rem(lane, 5 * BEAMS) // BEAMS, lax.rem(lane, BEAMS)
    names = table.astype(jnp.int32)

    def of_source(own):
        before, after = pltpu.roll(own, 1, 0), pltpu.roll(own, COLS - 1, 0)
        return jnp.where(kind == 3, before, jnp.where(kind == 4, after, own))

    last, first = (row == ROWS - 1).astype(jnp.int32), (row == 0).astype(jnp.int32)
    missing = (
        ((kind == 1) & (last == 1))
        | ((kind == 2) & (first == 1))
        | ((kind == 3) & (tile == 0))
        | ((kind == 4) & (tile == COLS - 1))
    )
    counts = of_source(jnp.broadcast_to(names[:, COUNT : COUNT + 1], shape))
    energy = of_source(
        jnp.take_along_axis(
            table, jnp.where(lane < USES, ENERGY + shot * BEAMS + beam, lane), axis=1, mode="promise_in_bounds"
        )
    )
    live = (lane < USES) & (beam < counts) & jnp.logical_not(missing)
    owners = names // 128

    source = tile + (kind == 4).astype(jnp.int32) - (kind == 3).astype(jnp.int32)
    along_z = (source // SIDE - owners // SIDE) & (SIDE - 1)
    along_x = (source - owners) & (SIDE - 1)
    code = jnp.where(shot == 0, along_x * SIDE + along_z, along_z * SIDE + along_x)
    group, record = jnp.zeros(shape, jnp.int32), jnp.zeros(shape, jnp.int32)
    for (first_step, second_step), (c, _) in WHERE.items():
        same = code == first_step % SIDE * SIDE + second_step % SIDE
        group = jnp.where(same, c, group)
        begin = [row_of(route, first_step, second_step) for route in (0, 1)]
        record = jnp.where(same, jnp.where(shot == 0, begin[0], begin[1]) + beam, record)

    column = lax.broadcasted_iota(jnp.int32, (NS, NS), 1)
    owned = jnp.where(live, owners * 8 + group, -1)
    over = jnp.zeros((1, 1), jnp.float32)
    for c, (_, slots, _, _) in enumerate(CLASSES):
        per_owner = jnp.concatenate(
            [jnp.sum((owned == o * 8 + c).astype(jnp.float32), axis=0, keepdims=True) for o in range(COLS)], axis=0
        )
        held = jnp.sum(per_owner, axis=1, keepdims=True)
        over = jnp.maximum(over, jnp.max((held > float(slots)).astype(jnp.float32), keepdims=True))

    earlier = lax.broadcasted_iota(jnp.int32, (NS, NS), 0) <= column
    above = lax.broadcasted_iota(jnp.int32, (COLS, COLS), 1) < lax.broadcasted_iota(jnp.int32, (COLS, COLS), 0)
    shift = 1 + (kind == 1).astype(jnp.int32) - (kind == 2).astype(jnp.int32)
    place = jnp.full(shape, -1.0)
    for c, (_, slots, base, _) in enumerate(CLASSES):
        marks = live & (owners == col) & (group == c)
        ones = marks.astype(jnp.float32)
        within = jnp.dot(ones, earlier.astype(jnp.float32), preferred_element_type=jnp.float32)
        totals = jnp.broadcast_to(jnp.sum(ones, axis=1, keepdims=True), shape)
        ahead = jnp.dot(above.astype(jnp.float32), totals, preferred_element_type=jnp.float32)
        rank = within + ahead - 1.0
        place = jnp.where(marks & (rank < float(slots)), rank + float(base), place)
    high = energy.astype(jnp.bfloat16).astype(jnp.float32)
    middle = (energy - high).astype(jnp.bfloat16).astype(jnp.float32)
    low = energy - high - middle
    fields = (
        lax.rem(names, 128).astype(jnp.float32),
        record.astype(jnp.float32),
        (tile * 8 + shift + 1).astype(jnp.float32),
        high,
        middle,
        low,
    )
    upright = jnp.transpose(place)
    slot = lax.broadcasted_iota(jnp.int32, (NS, SLOTS), 1).astype(jnp.float32)
    line = lax.broadcasted_iota(jnp.int32, (8, NS), 0)
    listed = jnp.zeros((8, SLOTS), jnp.float32)
    for t in range(COLS):
        here = (jnp.broadcast_to(upright[:, t : t + 1], (NS, SLOTS)) == slot).astype(jnp.bfloat16)
        rows = jnp.zeros((8, NS), jnp.float32)
        for f, field in enumerate(fields):
            rows = jnp.where(line == f, jnp.broadcast_to(field[t : t + 1, :], (8, NS)), rows)
        listed += jnp.dot(rows.astype(jnp.bfloat16), here, preferred_element_type=jnp.float32)
    return listed, listed[3:4] + listed[4:5] + listed[5:6], jnp.broadcast_to(over, (8, NS))


def fused(records, owner, block, count, travel, amp):
    vmem = pl.BlockSpec(memory_space=pltpu.VMEM)
    smem = pl.BlockSpec(memory_space=pltpu.SMEM)
    hbm = pl.BlockSpec(memory_space=pl.ANY)
    dma = pltpu.SemaphoreType.DMA
    f32 = jnp.float32
    return pl.pallas_call(
        fused_kernel,
        out_shape=(jax.ShapeDtypeStruct((1, 1, NS), f32), jax.ShapeDtypeStruct((1,), jnp.int32)),
        in_specs=[hbm, hbm, hbm, smem, hbm, hbm],
        out_specs=(vmem, smem),
        scratch_shapes=[
            pltpu.VMEM(((SHOTS * NP + 1) * BEAMS, NS), f32),
            *[pltpu.VMEM((held, NP, NS), jnp.bfloat16) for _, _, _, held in CLASSES],
            pltpu.VMEM(travel.shape, f32),
            pltpu.VMEM(amp.shape, f32),
            pltpu.VMEM((8, NS), f32),
            pltpu.VMEM((2, 8, NS), f32),
            pltpu.VMEM((8, NS), f32),
            pltpu.VMEM((COLS, 8, NS), f32),
            pltpu.VMEM((8, SLOTS), jnp.int32),
            pltpu.SMEM((8, SLOTS), jnp.int32),
            *[pltpu.VMEM((9 * slots, NS), f32) for _, slots, _, _ in CLASSES],
            *[pltpu.VMEM((9 * slots, NS), f32) for _, slots, _, _ in CLASSES],
            pltpu.VMEM((8, NS), f32),
            pltpu.VMEM((ROWS, 8, NS), f32),
            pltpu.VMEM((COLS, 8, NS), f32),
            pltpu.VMEM((COLS, 8, NS), f32),
            pltpu.VMEM((2, COLS, 8, NS), f32),
            pltpu.VMEM(records.shape, records.dtype),
            pltpu.VMEM(owner.shape, jnp.int32),
            pltpu.VMEM(block.shape, jnp.int32),
            pltpu.SemaphoreType.REGULAR((3,)),
            dma((6,)),
            dma((COPIES,)),
            dma((COPIES,)),
            dma((2,)),
            dma((2,)),
            dma((COLS,)),
            dma((COLS,)),
            dma((ROWS,)),
            dma((ROWS,)),
            dma((COLS,)),
            dma((COLS,)),
            dma((2,)),
            dma((2,)),
            pltpu.VMEM((COLS, 8, NS), f32),
            pltpu.VMEM((COLS, 8, NS), f32),
            pltpu.VMEM((COLS, 8, NS), f32),
            pltpu.VMEM((10, 8, NS), f32),
            dma((10,)),
            dma((10,)),
        ],
        compiler_params=pltpu.CompilerParams(
            collective_id=0, has_side_effects=True, vmem_limit_bytes=40 << 20
        ),
        cost_estimate=pl.CostEstimate(flops=10_000_000, bytes_accessed=16_000_000, transcendentals=0),
        name="migrate",
    )(records, owner, block, count, travel, amp)


def per_device(records, beam_count, owner_list, block_list, travel_table, amp_table):
    travel_table = pltpu.with_memory_space_constraint(travel_table, pltpu.HBM)
    amp_table = pltpu.with_memory_space_constraint(amp_table, pltpu.HBM)
    by_slowness = records.reshape(SHOTS, BEAMS, NP, NS).transpose(0, 2, 1, 3)
    owner, block = owner_list.reshape(1, USES), block_list.reshape(1, USES)
    quick, flag = fused(by_slowness, owner, block, beam_count, travel_table, amp_table)
    return lax.cond(
        flag[0] > 0,
        lambda: imaged_by_any_count(records, beam_count, owner_list, block_list, travel_table, amp_table),
        lambda: quick,
    )


def solution(mesh):
    placed = (
        P(None, "inline", "xline", None, None),
        P("inline", "xline"),
        P(("inline", "xline"), None),
        P(("inline", "xline"), None),
        P("xline", None, None),
        P("xline", None, None),
    )
    return jax.shard_map(
        per_device,
        mesh=mesh,
        in_specs=placed,
        out_specs=P("inline", "xline", None),
        check_vma=False,
    )
```

```python
import jax
import jax.numpy as jnp
from jax import lax
from jax.experimental import pallas as pl
from jax.experimental.pallas import tpu as pltpu
from jax.sharding import PartitionSpec as P

NS = 128
NP = 64
BEAMS = 8
SHOTS = 2
RECS = SHOTS * BEAMS
SIDE = 4
COLS = SIDE * SIDE
ROWS = 8
USES = 5 * RECS
LIST = 512
TARGETS = 3 * COLS
GROUP = 8
MESH = pl.DeviceIdType.MESH

ENERGY = USES
COUNT = USES + RECS


def greet(row, col):
    barrier = pltpu.get_barrier_semaphore()
    for other in range(1, COLS):
        pl.semaphore_signal(
            barrier, inc=1, device_id=(row, lax.rem(col + other, COLS)), device_id_type=MESH
        )

    @pl.when(row > 0)
    def _():
        pl.semaphore_signal(barrier, inc=1, device_id=(row - 1, col), device_id_type=MESH)

    @pl.when(row < ROWS - 1)
    def _():
        pl.semaphore_signal(barrier, inc=1, device_id=(row + 1, col), device_id_type=MESH)

    edges = (row > 0).astype(jnp.int32) + (row < ROWS - 1).astype(jnp.int32)
    pl.semaphore_wait(barrier, COLS - 1 + edges)


def gather_kernel(
    records, index, travel, amp,
    held, travel_out, amp_out, uses_out, index_out,
    near, mixed, lines, uses_vmem, index_vmem,
    local_sems, send_sems, recv_sems, near_send, near_recv, line_send, line_recv,
):
    row, col = lax.axis_index("inline"), lax.axis_index("xline")
    z, x = col // SIDE, lax.rem(col, SIDE)
    loads = [
        pltpu.make_async_copy(travel, travel_out, local_sems.at[0]),
        pltpu.make_async_copy(amp, amp_out, local_sems.at[1]),
        pltpu.make_async_copy(records, held.at[pl.ds(col * RECS, RECS)], local_sems.at[2]),
    ]
    near[...] = jnp.zeros_like(near)
    greet(row, col)

    def at(dz, dx):
        return lax.rem(z + dz + SIDE, SIDE) * SIDE + lax.rem(x + dx + SIDE, SIDE)

    started = {}

    def block(route, first, second, lo, size):
        tile = at(second, first) if route == 0 else at(first, second)
        return pl.ds(tile * RECS + route * BEAMS + lo, size)

    def toward(route, axis, step):
        along_x = (axis == 0) == (route == 0)
        return (row, at(0, step) if along_x else at(step, 0))

    def send(key, route, axis, step, first, second, lo, size):
        here = block(route, first, second, lo, size)
        n = len(started)
        if first == 0 and second == 0:
            source = records.at[pl.ds(route * BEAMS + lo, size)]
        else:
            source = held.at[here]
        copy = pltpu.make_async_remote_copy(
            src_ref=source,
            dst_ref=held.at[here],
            send_sem=send_sems.at[n],
            recv_sem=recv_sems.at[n],
            device_id=toward(route, axis, step),
            device_id_type=MESH,
        )
        copy.start()
        started[key] = copy

    half = BEAMS // 2
    both = (0, 1)
    for route in both:
        for step in (1, -1):
            send(("a", route, step), route, 0, step, 0, 0, 0, BEAMS)
    for route in both:
        for step in (1, -1):
            send(("c", route, 0, step), route, 1, step, 0, 0, 0, BEAMS)
    for copy in loads:
        copy.start()

    up = pltpu.make_async_remote_copy(
        index, near.at[0], near_send.at[0], near_recv.at[0], device_id=(row + 1, col), device_id_type=MESH
    )
    down = pltpu.make_async_remote_copy(
        index, near.at[1], near_send.at[1], near_recv.at[1], device_id=(row - 1, col), device_id_type=MESH
    )
    @pl.when(row < ROWS - 1)
    def _():
        up.start()

    @pl.when(row > 0)
    def _():
        down.start()

    @pl.when(row > 0)
    def _():
        up.wait_recv()

    @pl.when(row < ROWS - 1)
    def _():
        down.wait_recv()

    @pl.when(row < ROWS - 1)
    def _():
        up.wait_send()

    @pl.when(row > 0)
    def _():
        down.wait_send()

    kind = lax.broadcasted_iota(jnp.int32, (8, NS), 1) // RECS
    mixed[...] = jnp.where(kind == 1, near[1], jnp.where(kind == 2, near[0], index[...]))
    shares = []
    for other in range(1, COLS):
        share = pltpu.make_async_remote_copy(
            mixed,
            lines.at[other],
            line_send.at[other],
            line_recv.at[other],
            device_id=(row, lax.rem(col + other, COLS)),
            device_id_type=MESH,
        )
        share.start()
        shares.append(share)
    lines[0] = mixed[...]

    for route in both:
        for step in (1, -1):
            started["a", route, step].wait_recv()
            lo = 0 if step > 0 else half
            send(("b", route, step), route, 0, step, -step, 0, lo, half)
            for way in (1, -1):
                send(("c", route, -step, way), route, 1, way, -step, 0, 0, BEAMS)
    for route in both:
        for way in (1, -1):
            started["c", route, 0, way].wait_recv()
            lo = 0 if way > 0 else half
            send(("d", route, 0, way), route, 1, way, 0, -way, lo, half)

    build_list(row, col, shares, lines, index_vmem, uses_vmem)

    for route in both:
        for step in (1, -1):
            started["b", route, step].wait_recv()
        for way in (1, -1):
            send(("c", route, 2, way), route, 1, way, 2, 0, 0, BEAMS)
    for first in (-1, 1, 2):
        for route in both:
            for way in (1, -1):
                started["c", route, first, way].wait_recv()
                lo = 0 if way > 0 else half
                send(("d", route, first, way), route, 1, way, first, -way, lo, half)
    finish = [
        pltpu.make_async_copy(uses_vmem, uses_out, local_sems.at[3]),
        pltpu.make_async_copy(index_vmem, index_out, local_sems.at[4]),
    ]
    for copy in finish:
        copy.start()
    for first in (0, -1, 1, 2):
        for route in both:
            for way in (1, -1):
                started["d", route, first, way].wait_recv()
    for copy in started.values():
        copy.wait_send()
    for share in shares:
        share.wait_send()
    for copy in loads + finish:
        copy.wait()


def build_list(row, col, shares, lines, index_vmem, uses_vmem):
    for share in shares:
        share.wait_recv()
    for tile in range(COLS):
        index_vmem[pl.ds(tile, 1), :] = lines[lax.rem(col - tile + COLS, COLS)][0:1, :]
    table = index_vmem[...]
    names = table.astype(jnp.int32)
    shape = (COLS, NS)
    lane = lax.broadcasted_iota(jnp.int32, shape, 1)
    tile = lax.broadcasted_iota(jnp.int32, shape, 0)
    kind, beam = lane // RECS, lax.rem(lane, BEAMS)
    counts = jnp.broadcast_to(names[:, COUNT : COUNT + 1], shape)
    before = jnp.where(tile > 0, pltpu.roll(counts, 1, 0), 0)
    after = jnp.where(tile < COLS - 1, pltpu.roll(counts, COLS - 1, 0), 0)
    last, first = (row == ROWS - 1).astype(jnp.int32), (row == 0).astype(jnp.int32)
    live = jnp.where(kind == 3, before, jnp.where(kind == 4, after, counts))
    live = jnp.where(kind == 1, counts * (1 - last), live)
    live = jnp.where(kind == 2, counts * (1 - first), live)
    wanted = (lane < USES) & (beam < live) & (names // 128 == col)
    marks = wanted.astype(jnp.float32)
    earlier = lax.broadcasted_iota(jnp.int32, (NS, NS), 0) <= lax.broadcasted_iota(jnp.int32, (NS, NS), 1)
    within = jnp.dot(marks, earlier.astype(jnp.float32), preferred_element_type=jnp.float32)
    above = lax.broadcasted_iota(jnp.int32, (COLS, COLS), 1) < lax.broadcasted_iota(jnp.int32, (COLS, COLS), 0)
    totals = jnp.broadcast_to(jnp.sum(marks, axis=1, keepdims=True), shape)
    ahead = jnp.dot(above.astype(jnp.float32), totals, preferred_element_type=jnp.float32)
    place = jnp.where(wanted, within + ahead - 1.0, -1.0)
    number = jnp.sum(marks)

    source = tile + (kind == 4).astype(jnp.int32) - (kind == 3).astype(jnp.int32)
    shift = 1 + (kind == 1).astype(jnp.int32) - (kind == 2).astype(jnp.int32)
    fields = (
        lax.rem(names, 128).astype(jnp.float32),
        (source * RECS + lax.rem(lane, RECS)).astype(jnp.float32),
        (shift * COLS + tile).astype(jnp.float32),
    )
    upright = jnp.transpose(place)
    slot = lax.broadcasted_iota(jnp.int32, (NS, LIST), 1).astype(jnp.float32)
    line = lax.broadcasted_iota(jnp.int32, (8, NS), 0)
    listed = jnp.zeros((8, LIST), jnp.float32)
    for t in range(COLS):
        here = (jnp.broadcast_to(upright[:, t : t + 1], (NS, LIST)) == slot).astype(jnp.bfloat16)
        rows = jnp.zeros((8, NS), jnp.float32)
        for f, field in enumerate(fields):
            rows = jnp.where(line == f, jnp.broadcast_to(field[t : t + 1, :], (8, NS)), rows)
        listed += jnp.dot(rows.astype(jnp.bfloat16), here, preferred_element_type=jnp.float32)
    place_in = lax.broadcasted_iota(jnp.int32, (8, LIST), 1).astype(jnp.float32)
    part = lax.broadcasted_iota(jnp.int32, (8, LIST), 0)
    listed = jnp.where((part == 2) & (place_in >= number), float(TARGETS), listed)
    listed = jnp.where(part == 3, number, listed)
    uses_vmem[...] = listed.astype(jnp.int32)


def gather(records, index, travel, amp):
    hbm = pl.BlockSpec(memory_space=pl.ANY)
    vmem = pl.BlockSpec(memory_space=pltpu.VMEM)
    smem = pl.BlockSpec(memory_space=pltpu.SMEM)
    return pl.pallas_call(
        gather_kernel,
        out_shape=(
            pltpu.VMEM((COLS * RECS, NP, NS), jnp.bfloat16),
            pltpu.VMEM(travel.shape, jnp.float32),
            pltpu.VMEM(amp.shape, jnp.float32),
            jax.ShapeDtypeStruct((8, LIST), jnp.int32),
            jax.ShapeDtypeStruct((COLS, NS), jnp.float32),
        ),
        in_specs=[hbm, vmem, hbm, hbm],
        out_specs=(vmem, vmem, vmem, hbm, hbm),
        scratch_shapes=[
            pltpu.VMEM((2, 8, NS), jnp.float32),
            pltpu.VMEM((8, NS), jnp.float32),
            pltpu.VMEM((COLS, 8, NS), jnp.float32),
            pltpu.VMEM((8, LIST), jnp.int32),
            pltpu.VMEM((COLS, NS), jnp.float32),
            pltpu.SemaphoreType.DMA((5,)),
            pltpu.SemaphoreType.DMA((40,)),
            pltpu.SemaphoreType.DMA((40,)),
            pltpu.SemaphoreType.DMA((2,)),
            pltpu.SemaphoreType.DMA((2,)),
            pltpu.SemaphoreType.DMA((COLS,)),
            pltpu.SemaphoreType.DMA((COLS,)),
        ],
        compiler_params=pltpu.CompilerParams(
            collective_id=1, has_side_effects=True, vmem_limit_bytes=32 << 20
        ),
        cost_estimate=pl.CostEstimate(flops=10_000_000, bytes_accessed=16_000_000, transcendentals=0),
        name="gather_records",
    )(records, index, travel, amp)


def image_kernel(uses, index, records, travel, amp, out, acc):
    acc[...] = jnp.zeros_like(acc)

    def step(i, carry):
        picked = []
        for d in range(GROUP):
            u = i * GROUP + d
            picked.append((uses[0, u], uses[1, u], uses[2, u]))
        totals = [jnp.zeros((8, NS), jnp.float32) for _ in picked]
        squares = [jnp.zeros((8, NS), jnp.float32) for _ in picked]
        for q in range(NP // 8):
            rows = pl.ds(8 * q, 8)
            for d, (block, rec, _) in enumerate(picked):
                t = travel[block, rows, :]
                a = amp[block, rows, :]
                pair = records[rec, pl.ds(16 * (q // 2), 16), :].astype(jnp.float32)
                r = pair[8 * (q % 2) : 8 * (q % 2) + 8]
                k = t.astype(jnp.int32)
                f = t - k.astype(jnp.float32)
                w0 = (1.0 - f).astype(jnp.bfloat16).astype(jnp.float32)
                w1 = f.astype(jnp.bfloat16).astype(jnp.float32)
                v0 = jnp.take_along_axis(r, k, axis=1, mode="promise_in_bounds")
                v1 = jnp.take_along_axis(r, k + 1, axis=1, mode="promise_in_bounds")
                totals[d] += a * (v0 * w0 + v1 * w1)
                squares[d] += a * a
        for d, (_, rec, target) in enumerate(picked):
            energy = index[rec // RECS, ENERGY + lax.rem(rec, RECS)]
            acc[target, 0] += totals[d]
            acc[target, 1] += squares[d] * energy
        return carry

    lax.fori_loop(0, (uses[3, 0] + GROUP - 1) // GROUP, step, 0)
    out[...] = jnp.sum(acc[pl.ds(0, TARGETS)], axis=2)


def image(uses, index, records, travel, amp):
    vmem = pl.BlockSpec(memory_space=pltpu.VMEM)
    smem = pl.BlockSpec(memory_space=pltpu.SMEM)
    return pl.pallas_call(
        image_kernel,
        out_shape=pltpu.VMEM((TARGETS, 2, NS), jnp.float32),
        in_specs=[smem, smem, vmem, vmem, vmem],
        out_specs=vmem,
        scratch_shapes=[pltpu.VMEM((TARGETS + 1, 2, 8, NS), jnp.float32)],
        compiler_params=pltpu.CompilerParams(vmem_limit_bytes=32 << 20),
        cost_estimate=pl.CostEstimate(flops=10_000_000, bytes_accessed=8_000_000, transcendentals=0),
        name="image_uses",
    )(uses, index, records, travel, amp)


def exchange_kernel(sums, out, near, total, parts, near_send, near_recv, part_send, part_recv):
    row, col = lax.axis_index("inline"), lax.axis_index("xline")
    greet(row, col)
    up = pltpu.make_async_remote_copy(
        sums.at[2], near.at[0], near_send.at[0], near_recv.at[0], device_id=(row + 1, col), device_id_type=MESH
    )
    down = pltpu.make_async_remote_copy(
        sums.at[0], near.at[1], near_send.at[1], near_recv.at[1], device_id=(row - 1, col), device_id_type=MESH
    )

    @pl.when(row < ROWS - 1)
    def _():
        up.start()

    @pl.when(row > 0)
    def _():
        down.start()

    total[...] = sums[1]

    @pl.when(row > 0)
    def _():
        up.wait_recv()
        total[...] += near[0]

    @pl.when(row < ROWS - 1)
    def _():
        down.wait_recv()
        total[...] += near[1]

    copies = []
    for other in range(1, COLS):
        there = lax.rem(col + other, COLS)
        copy = pltpu.make_async_remote_copy(
            total.at[there],
            parts.at[other],
            part_send.at[other],
            part_recv.at[other],
            device_id=(row, there),
            device_id_type=MESH,
        )
        copy.start()
        copies.append(copy)
    mine = total[col]
    for copy, other in zip(copies, range(1, COLS)):
        copy.wait_recv()
        mine += parts[other]
    out[0] = mine[0:1] / jnp.sqrt(1.0 + mine[1:2])
    for copy in copies:
        copy.wait_send()

    @pl.when(row < ROWS - 1)
    def _():
        up.wait_send()

    @pl.when(row > 0)
    def _():
        down.wait_send()


def exchange(sums):
    vmem = pl.BlockSpec(memory_space=pltpu.VMEM)
    return pl.pallas_call(
        exchange_kernel,
        out_shape=jax.ShapeDtypeStruct((1, 1, NS), jnp.float32),
        in_specs=[vmem],
        out_specs=vmem,
        scratch_shapes=[
            pltpu.VMEM((2, COLS, 2, NS), jnp.float32),
            pltpu.VMEM((COLS, 2, NS), jnp.float32),
            pltpu.VMEM((COLS, 2, NS), jnp.float32),
            pltpu.SemaphoreType.DMA((2,)),
            pltpu.SemaphoreType.DMA((2,)),
            pltpu.SemaphoreType.DMA((COLS,)),
            pltpu.SemaphoreType.DMA((COLS,)),
        ],
        compiler_params=pltpu.CompilerParams(collective_id=2, has_side_effects=True),
        cost_estimate=pl.CostEstimate(flops=10_000, bytes_accessed=100_000, transcendentals=0),
        name="exchange_sums",
    )(sums)


def imaged_by_any_count(records, beam_count, owner_list, block_list, travel_table, amp_table):
    records = records.reshape(RECS, NP, NS)
    named = (owner_list * 128 + block_list)[:, 0].astype(jnp.float32)
    named = named.reshape(SHOTS, 5, BEAMS).transpose(1, 0, 2).reshape(USES)
    energy = jnp.mean(jnp.square(records.astype(jnp.float32)), axis=(1, 2))
    count = jnp.broadcast_to(beam_count[0].astype(jnp.float32), (NS - COUNT,))
    index = jnp.broadcast_to(jnp.concatenate([named, energy, count]), (8, NS))
    gathered, travel, amp, uses, index = gather(records, index, travel_table, amp_table)
    sums = image(uses, index, gathered, travel, amp)
    return exchange(sums.reshape(3, COLS, 2, NS))


CLASSES = (
    (((0, 0), (1, 0), (-1, 0), (2, 0)), 48, 0, 64),
    (((0, 1), (0, -1), (1, 1), (1, -1), (-1, 1), (-1, -1)), 64, 64, 128),
    (((2, 1), (2, -1), (0, 2)), 40, 144, 64),
    (((1, 2), (-1, 2)), 32, 184, 32),
    (((2, 2),), 24, 216, 16),
)
WHERE = {tile: (c, n) for c, (tiles, _, _, _) in enumerate(CLASSES) for n, tile in enumerate(tiles)}
FAR_FIRST = sorted(
    ((dz, dx) for dz in (0, 1, -1, 2) for dx in (0, 1, -1, 2) if (dz, dx) != (0, 0)),
    key=lambda step: -abs(step[0]) - abs(step[1]),
)
SLOTS = 256
NBLOCKS = 128
COPIES = 40


def wrap(steps):
    return (steps + 1) % SIDE - 1


def fused_kernel(
    records, owner, block, count, travel, amp,
    out, flag_out,
    wide, buf0, buf1, buf2, buf3, buf4, travel_v, amp_v,
    mine, near, mixed, lines, uses_v, uses_s,
    con0, con1, con2, con3, con4, lit0, lit1, lit2, lit3, lit4,
    flag_mine, flags, sums, parts, edges, records_v, owner_v, block_v, met,
    local_sems, send_sems, recv_sems, near_send, near_recv, line_send, line_recv,
    flag_send, flag_recv, part_send, part_recv, edge_send, edge_recv,
    early_v, late_v, last_v, late_in, late_send, late_recv, energy_v,
):
    row, col = lax.axis_index("inline"), lax.axis_index("xline")
    z, x = col // SIDE, lax.rem(col, SIDE)
    bufs = (buf0, buf1, buf2, buf3, buf4)
    cons, lits = (con0, con1, con2, con3, con4), (lit0, lit1, lit2, lit3, lit4)
    near[...] = jnp.zeros_like(near)
    edges[...] = jnp.zeros_like(edges)

    def at(dz, dx):
        return lax.rem(z + dz + SIDE, SIDE) * SIDE + lax.rem(x + dx + SIDE, SIDE)

    beside = [(row, at(dz, dx)) for dz, dx in ((0, 1), (0, -1), (1, 0), (-1, 0))]
    beside += [(lax.rem(row + 1, ROWS), col), (lax.rem(row + ROWS - 1, ROWS), col)]
    barrier = pltpu.get_barrier_semaphore()
    for there in beside:
        pl.semaphore_signal(barrier, inc=1, device_id=there, device_id_type=MESH)
    inputs = [
        pltpu.make_async_copy(records, records_v, local_sems.at[3]),
        pltpu.make_async_copy(owner, owner_v, local_sems.at[4]),
        pltpu.make_async_copy(block, block_v, local_sems.at[5]),
    ]
    for copy in inputs:
        copy.start()
    loads = [
        pltpu.make_async_copy(travel, travel_v, local_sems.at[0]),
        pltpu.make_async_copy(amp, amp_v, local_sems.at[1]),
    ]
    for copy in loads:
        copy.start()

    for copy in inputs:
        copy.wait()

    wide[pl.ds(0, SHOTS * NP * BEAMS), :] = records_v[...].astype(jnp.float32).reshape(SHOTS * NP * BEAMS, NS)
    energies = jnp.zeros((8, NS), jnp.float32)
    lane8 = lax.broadcasted_iota(jnp.int32, (8, NS), 1)
    for s in range(SHOTS):
        for b in range(BEAMS):
            rec = wide[pl.ds(s * NP * BEAMS + b, NP, stride=BEAMS), :]
            bufs[0][row_of(s, 0, 0) + b] = rec.astype(jnp.bfloat16)
            energy = jnp.sum(rec * rec, keepdims=True) * (1.0 / (NP * NS))
            energies = jnp.where(lane8 == ENERGY + s * BEAMS + b, jnp.broadcast_to(energy, (8, NS)), energies)
    named = (owner_v[...] * 128 + block_v[...]).astype(jnp.float32)
    mine[...] = jnp.where(lane8 >= COUNT, count[0, 0].astype(jnp.float32), energies)
    mine[:, 0:USES] = jnp.broadcast_to(named, (8, USES))
    pl.semaphore_wait(barrier, len(beside))

    started = {}

    def send(kind, route, axis, step, first, second, lo, size):
        seen = (wrap(first - step), second) if axis == 0 else (first, wrap(second - step))
        here, there = WHERE[first, second][0], WHERE[seen][0]
        along_x = (axis == 0) == (route == 0)
        n = len(started)
        copy = pltpu.make_async_remote_copy(
            src_ref=bufs[here].at[pl.ds(row_of(route, first, second) + lo, size)],
            dst_ref=bufs[there].at[pl.ds(row_of(route, *seen) + lo, size)],
            send_sem=send_sems.at[n],
            recv_sem=recv_sems.at[n],
            device_id=(row, at(0, step) if along_x else at(step, 0)),
            device_id_type=MESH,
        )
        copy.start()
        key = (kind, route, step) if axis == 0 else (kind, route, first, step)
        started[key] = copy

    both, ways = (0, 1), (1, -1)
    half = BEAMS // 2

    def along_second(first):
        for way in ways:
            for route in both:
                send("c", route, 1, way, first, 0, 0, BEAMS)

    def pass_on(first):
        for way in ways:
            for route in both:
                started["c", route, first, way].wait_recv()
                send("d", route, 1, way, first, -way, 0 if way > 0 else half, half)

    def arrived(first):
        for route in both:
            for way in ways:
                started["d", route, first, way].wait_recv()

    def image_some(p, begin, end, group=GROUP):
        _, slots, base, held = CLASSES[p]
        buf, con, lit = bufs[p], cons[p], lits[p]

        def step(i, carry):
            places = [base + i * group + d for d in range(group)]
            picked = [(uses_s[0, u] & (NBLOCKS - 1), uses_s[1, u] & (held - 1)) for u in places]
            for d, (number, rec) in enumerate(picked):
                total, square = jnp.zeros((8, NS), jnp.float32), jnp.zeros((8, NS), jnp.float32)
                for q in range(NP // 8):
                    rows = pl.ds(8 * q, 8)
                    t = travel_v[number, rows, :]
                    a = amp_v[number, rows, :]
                    pair = buf[rec, pl.ds(16 * (q // 2), 16), :].astype(jnp.float32)
                    r = pair[8 * (q % 2) : 8 * (q % 2) + 8]
                    k = t.astype(jnp.int32)
                    f = t - k.astype(jnp.float32)
                    w0 = (1.0 - f).astype(jnp.bfloat16).astype(jnp.float32)
                    w1 = f.astype(jnp.bfloat16).astype(jnp.float32)
                    v0 = jnp.take_along_axis(r, k, axis=1, mode="promise_in_bounds")
                    v1 = jnp.take_along_axis(r, k + 1, axis=1, mode="promise_in_bounds")
                    total += a * (v0 * w0 + v1 * w1)
                    square += a * a
                con[pl.ds(i * group + d, 8, stride=slots), :] = total
                lit[pl.ds(i * group + d, 8, stride=slots), :] = square
            return carry

        if end - begin == group:
            step(begin // group, 0)
        else:
            lax.fori_loop(begin // group, end // group, step, 0)

    def total_of(p, listed):
        _, slots, base, _ = CLASSES[p]
        con = sum(cons[p][pl.ds(s * slots, slots), :] for s in range(8))
        lit = sum(lits[p][pl.ds(s * slots, slots), :] for s in range(8)) * energy_v[pl.ds(base, slots), :]
        target = jnp.broadcast_to(listed[2:3, base : base + slots], (NS, slots))
        line = (lax.broadcasted_iota(jnp.int32, (NS, slots), 0) + 1).astype(jnp.float32)
        to_tile = jnp.where(target == line, 1.0, 0.0).astype(jnp.bfloat16)
        rest = jnp.concatenate([con, lit], axis=1)
        total = jnp.zeros((NS, 2 * NS), jnp.float32)
        for _ in range(3):
            part = rest.astype(jnp.bfloat16)
            rest = rest - part.astype(jnp.float32)
            total += jnp.dot(to_tile, part, preferred_element_type=jnp.float32)
        return total[:, :NS] + pltpu.roll(total[:, NS:], 4, 0)

    for step in ways:
        for route in both:
            send("a", route, 0, step, 0, 0, 0, BEAMS)
    along_second(0)

    up = pltpu.make_async_remote_copy(
        mine, near.at[0], near_send.at[0], near_recv.at[0], device_id=(row + 1, col), device_id_type=MESH
    )
    down = pltpu.make_async_remote_copy(
        mine, near.at[1], near_send.at[1], near_recv.at[1], device_id=(row - 1, col), device_id_type=MESH
    )
    upward, downward = pl.when(row < ROWS - 1), pl.when(row > 0)
    upward(up.start)
    downward(down.start)
    for turn in range(3):
        for there in beside:
            pl.semaphore_signal(met.at[turn], inc=1, device_id=there, device_id_type=MESH)
        pl.semaphore_wait(met.at[turn], len(beside))
    downward(up.wait_recv)
    upward(down.wait_recv)
    kind8 = lax.rem(lane8, 5 * BEAMS) // BEAMS
    kind8 = jnp.where(lane8 < USES, kind8, 0)
    mixed[...] = jnp.where(kind8 == 1, near[1], jnp.where(kind8 == 2, near[0], mine[...]))
    shares = []
    for other in range(1, COLS):
        share = pltpu.make_async_remote_copy(
            mixed, lines.at[other], line_send.at[other], line_recv.at[other],
            device_id=(row, lax.rem(col + other, COLS)), device_id_type=MESH,
        )
        share.start()
        shares.append(share)
    lines[0] = mixed[...]

    for step in ways:
        for route in both:
            started["a", route, step].wait_recv()
            send("b", route, 0, step, -step, 0, 0 if step > 0 else half, half)
        along_second(-step)

    for share in shares:
        share.wait_recv()
    listed, energy, over = list_uses(row, col, lines)
    energy_v[...] = jnp.transpose(jnp.broadcast_to(energy, (NS, SLOTS)))
    uses_v[...] = listed.astype(jnp.int32)
    to_smem = pltpu.make_async_copy(uses_v, uses_s, local_sems.at[2])
    to_smem.start()
    flag_mine[...] = over
    alarms = []
    for other in range(1, ROWS):
        alarm = pltpu.make_async_remote_copy(
            flag_mine, flags.at[other], flag_send.at[other], flag_recv.at[other],
            device_id=(lax.rem(row + other, ROWS), col), device_id_type=MESH,
        )
        alarm.start()
        alarms.append(alarm)

    for route in both:
        for step in ways:
            started["b", route, step].wait_recv()
    along_second(2)
    pass_on(0)
    to_smem.wait()
    for copy in loads:
        copy.wait()
    image_some(0, 0, 48)
    pass_on(1)
    pass_on(-1)
    image_some(1, 0, 64)
    pass_on(2)
    early = total_of(0, listed) + total_of(1, listed)
    arrived(0)
    image_some(2, 0, 40)
    early += total_of(2, listed)
    early_v[...] = early.reshape(COLS, 8, NS)
    to_next = pltpu.make_async_remote_copy(
        early_v, edges.at[0], edge_send.at[0], edge_recv.at[0], device_id=(row + 1, col), device_id_type=MESH
    )
    to_prev = pltpu.make_async_remote_copy(
        early_v, edges.at[1], edge_send.at[1], edge_recv.at[1], device_id=(row - 1, col), device_id_type=MESH
    )
    upward(to_next.start)
    downward(to_prev.start)
    raised = flag_mine[...]
    for alarm, other in zip(alarms, range(1, ROWS)):
        alarm.wait_recv()
        raised = jnp.maximum(raised, flags[other])
    flag_out[0] = jnp.max(raised).astype(jnp.int32)
    arrived(1)
    arrived(-1)
    image_some(3, 0, 32, 32)
    late_v[...] = total_of(3, listed).reshape(COLS, 8, NS)
    next_row, prev_row = lax.rem(row + 1, ROWS), lax.rem(row + ROWS - 1, ROWS)
    direct = []

    def straight(source, dz, dx):
        for beside_row in (next_row, prev_row):
            n = len(direct)
            copy = pltpu.make_async_remote_copy(
                source.at[at(dz, dx)], late_in.at[n], late_send.at[n], late_recv.at[n],
                device_id=(beside_row, at(dz, dx)), device_id_type=MESH,
            )
            copy.start()
            direct.append(copy)

    for dz, dx in ((2, 1), (2, -1), (1, 2), (-1, 2)):
        straight(late_v, dz, dx)
    arrived(2)
    image_some(4, 0, 24, 24)
    last_v[...] = total_of(4, listed).reshape(COLS, 8, NS)
    straight(last_v, 2, 2)
    downward(to_next.wait_recv)
    upward(to_prev.wait_recv)
    own = early_v[...] + late_v[...] + last_v[...]
    sums[...] = own + pltpu.roll(edges[0], 7, 1) + pltpu.roll(edges[1], 1, 1)

    pieces = []
    for n, (dz, dx) in enumerate(FAR_FIRST):
        there = at(dz, dx)
        piece = pltpu.make_async_remote_copy(
            sums.at[there], parts.at[n], part_send.at[n], part_recv.at[n],
            device_id=(row, there), device_id_type=MESH,
        )
        piece.start()
        pieces.append(piece)
    for copy in started.values():
        copy.wait_send()
    for copy in shares + alarms + direct:
        copy.wait_send()
    upward(up.wait_send)
    downward(down.wait_send)
    upward(to_next.wait_send)
    downward(to_prev.wait_send)
    contrib, lighting = sums[col][1:2], sums[col][5:6]
    for n, copy in enumerate(direct):
        copy.wait_recv()
        line = 2 if n % 2 == 0 else 0
        contrib += late_in[n][line : line + 1]
        lighting += late_in[n][line + 4 : line + 5]
    whole = jnp.zeros((8, NS), jnp.float32)
    for n, piece in enumerate(pieces):
        piece.wait_recv()
        whole += parts[n]
    out[0] = (contrib + whole[1:2]) / jnp.sqrt(1.0 + (lighting + whole[5:6]))
    for piece in pieces:
        piece.wait_send()


def row_of(route, first, second):
    c, n = WHERE[first, second]
    return (route * len(CLASSES[c][0]) + n) * BEAMS


def list_uses(row, col, lines):
    table = jnp.concatenate([lines[lax.rem(col - tile + COLS, COLS)][0:1, :] for tile in range(COLS)], axis=0)
    shape = (COLS, NS)
    lane = lax.broadcasted_iota(jnp.int32, shape, 1)
    tile = lax.broadcasted_iota(jnp.int32, shape, 0)
    shot, kind, beam = lane // (5 * BEAMS), lax.rem(lane, 5 * BEAMS) // BEAMS, lax.rem(lane, BEAMS)
    names = table.astype(jnp.int32)

    def of_source(own):
        before, after = pltpu.roll(own, 1, 0), pltpu.roll(own, COLS - 1, 0)
        return jnp.where(kind == 3, before, jnp.where(kind == 4, after, own))

    last, first = (row == ROWS - 1).astype(jnp.int32), (row == 0).astype(jnp.int32)
    missing = (
        ((kind == 1) & (last == 1))
        | ((kind == 2) & (first == 1))
        | ((kind == 3) & (tile == 0))
        | ((kind == 4) & (tile == COLS - 1))
    )
    counts = of_source(jnp.broadcast_to(names[:, COUNT : COUNT + 1], shape))
    energy = of_source(
        jnp.take_along_axis(
            table, jnp.where(lane < USES, ENERGY + shot * BEAMS + beam, lane), axis=1, mode="promise_in_bounds"
        )
    )
    live = (lane < USES) & (beam < counts) & jnp.logical_not(missing)
    owners = names // 128

    source = tile + (kind == 4).astype(jnp.int32) - (kind == 3).astype(jnp.int32)
    along_z = (source // SIDE - owners // SIDE) & (SIDE - 1)
    along_x = (source - owners) & (SIDE - 1)
    code = jnp.where(shot == 0, along_x * SIDE + along_z, along_z * SIDE + along_x)
    group, record = jnp.zeros(shape, jnp.int32), jnp.zeros(shape, jnp.int32)
    for (first_step, second_step), (c, _) in WHERE.items():
        same = code == first_step % SIDE * SIDE + second_step % SIDE
        group = jnp.where(same, c, group)
        begin = [row_of(route, first_step, second_step) for route in (0, 1)]
        record = jnp.where(same, jnp.where(shot == 0, begin[0], begin[1]) + beam, record)

    column = lax.broadcasted_iota(jnp.int32, (NS, NS), 1)
    owned = jnp.where(live, owners * 8 + group, -1)
    over = jnp.zeros((1, 1), jnp.float32)
    for c, (_, slots, _, _) in enumerate(CLASSES):
        per_owner = jnp.concatenate(
            [jnp.sum((owned == o * 8 + c).astype(jnp.float32), axis=0, keepdims=True) for o in range(COLS)], axis=0
        )
        held = jnp.sum(per_owner, axis=1, keepdims=True)
        over = jnp.maximum(over, jnp.max((held > float(slots)).astype(jnp.float32), keepdims=True))

    earlier = lax.broadcasted_iota(jnp.int32, (NS, NS), 0) <= column
    above = lax.broadcasted_iota(jnp.int32, (COLS, COLS), 1) < lax.broadcasted_iota(jnp.int32, (COLS, COLS), 0)
    shift = 1 + (kind == 1).astype(jnp.int32) - (kind == 2).astype(jnp.int32)
    place = jnp.full(shape, -1.0)
    for c, (_, slots, base, _) in enumerate(CLASSES):
        marks = live & (owners == col) & (group == c)
        ones = marks.astype(jnp.float32)
        within = jnp.dot(ones, earlier.astype(jnp.float32), preferred_element_type=jnp.float32)
        totals = jnp.broadcast_to(jnp.sum(ones, axis=1, keepdims=True), shape)
        ahead = jnp.dot(above.astype(jnp.float32), totals, preferred_element_type=jnp.float32)
        rank = within + ahead - 1.0
        place = jnp.where(marks & (rank < float(slots)), rank + float(base), place)
    high = energy.astype(jnp.bfloat16).astype(jnp.float32)
    middle = (energy - high).astype(jnp.bfloat16).astype(jnp.float32)
    low = energy - high - middle
    fields = (
        lax.rem(names, 128).astype(jnp.float32),
        record.astype(jnp.float32),
        (tile * 8 + shift + 1).astype(jnp.float32),
        high,
        middle,
        low,
    )
    upright = jnp.transpose(place)
    slot = lax.broadcasted_iota(jnp.int32, (NS, SLOTS), 1).astype(jnp.float32)
    line = lax.broadcasted_iota(jnp.int32, (8, NS), 0)
    listed = jnp.zeros((8, SLOTS), jnp.float32)
    for t in range(COLS):
        here = (jnp.broadcast_to(upright[:, t : t + 1], (NS, SLOTS)) == slot).astype(jnp.bfloat16)
        rows = jnp.zeros((8, NS), jnp.float32)
        for f, field in enumerate(fields):
            rows = jnp.where(line == f, jnp.broadcast_to(field[t : t + 1, :], (8, NS)), rows)
        listed += jnp.dot(rows.astype(jnp.bfloat16), here, preferred_element_type=jnp.float32)
    return listed, listed[3:4] + listed[4:5] + listed[5:6], jnp.broadcast_to(over, (8, NS))


def fused(records, owner, block, count, travel, amp):
    vmem = pl.BlockSpec(memory_space=pltpu.VMEM)
    smem = pl.BlockSpec(memory_space=pltpu.SMEM)
    hbm = pl.BlockSpec(memory_space=pl.ANY)
    dma = pltpu.SemaphoreType.DMA
    f32 = jnp.float32
    return pl.pallas_call(
        fused_kernel,
        out_shape=(jax.ShapeDtypeStruct((1, 1, NS), f32), jax.ShapeDtypeStruct((1,), jnp.int32)),
        in_specs=[hbm, hbm, hbm, smem, hbm, hbm],
        out_specs=(vmem, smem),
        scratch_shapes=[
            pltpu.VMEM(((SHOTS * NP + 1) * BEAMS, NS), f32),
            *[pltpu.VMEM((held, NP, NS), jnp.bfloat16) for _, _, _, held in CLASSES],
            pltpu.VMEM(travel.shape, f32),
            pltpu.VMEM(amp.shape, f32),
            pltpu.VMEM((8, NS), f32),
            pltpu.VMEM((2, 8, NS), f32),
            pltpu.VMEM((8, NS), f32),
            pltpu.VMEM((COLS, 8, NS), f32),
            pltpu.VMEM((8, SLOTS), jnp.int32),
            pltpu.SMEM((8, SLOTS), jnp.int32),
            *[pltpu.VMEM((9 * slots, NS), f32) for _, slots, _, _ in CLASSES],
            *[pltpu.VMEM((9 * slots, NS), f32) for _, slots, _, _ in CLASSES],
            pltpu.VMEM((8, NS), f32),
            pltpu.VMEM((ROWS, 8, NS), f32),
            pltpu.VMEM((COLS, 8, NS), f32),
            pltpu.VMEM((COLS, 8, NS), f32),
            pltpu.VMEM((2, COLS, 8, NS), f32),
            pltpu.VMEM(records.shape, records.dtype),
            pltpu.VMEM(owner.shape, jnp.int32),
            pltpu.VMEM(block.shape, jnp.int32),
            pltpu.SemaphoreType.REGULAR((3,)),
            dma((6,)),
            dma((COPIES,)),
            dma((COPIES,)),
            dma((2,)),
            dma((2,)),
            dma((COLS,)),
            dma((COLS,)),
            dma((ROWS,)),
            dma((ROWS,)),
            dma((COLS,)),
            dma((COLS,)),
            dma((2,)),
            dma((2,)),
            pltpu.VMEM((COLS, 8, NS), f32),
            pltpu.VMEM((COLS, 8, NS), f32),
            pltpu.VMEM((COLS, 8, NS), f32),
            pltpu.VMEM((10, 8, NS), f32),
            dma((10,)),
            dma((10,)),
            pltpu.VMEM((SLOTS, NS), f32),
        ],
        compiler_params=pltpu.CompilerParams(
            collective_id=0, has_side_effects=True, vmem_limit_bytes=40 << 20
        ),
        cost_estimate=pl.CostEstimate(flops=10_000_000, bytes_accessed=16_000_000, transcendentals=0),
        name="migrate",
    )(records, owner, block, count, travel, amp)


def per_device(records, beam_count, owner_list, block_list, travel_table, amp_table):
    travel_table = pltpu.with_memory_space_constraint(travel_table, pltpu.HBM)
    amp_table = pltpu.with_memory_space_constraint(amp_table, pltpu.HBM)
    by_slowness = records.reshape(SHOTS, BEAMS, NP, NS).transpose(0, 2, 1, 3)
    owner, block = owner_list.reshape(1, USES), block_list.reshape(1, USES)
    quick, flag = fused(by_slowness, owner, block, beam_count, travel_table, amp_table)
    return lax.cond(
        flag[0] > 0,
        lambda: imaged_by_any_count(records, beam_count, owner_list, block_list, travel_table, amp_table),
        lambda: quick,
    )


def solution(mesh):
    placed = (
        P(None, "inline", "xline", None, None),
        P("inline", "xline"),
        P(("inline", "xline"), None),
        P(("inline", "xline"), None),
        P("xline", None, None),
        P("xline", None, None),
    )
    return jax.shard_map(
        per_device,
        mesh=mesh,
        in_specs=placed,
        out_specs=P("inline", "xline", None),
        check_vma=False,
    )
```

```python
import jax
import jax.numpy as jnp
from jax import lax
from jax.experimental import pallas as pl
from jax.experimental.pallas import tpu as pltpu
from jax.sharding import PartitionSpec as P

NS = 128
NP = 64
BEAMS = 8
SHOTS = 2
RECS = SHOTS * BEAMS
SIDE = 4
COLS = SIDE * SIDE
ROWS = 8
USES = 5 * RECS
LIST = 512
TARGETS = 3 * COLS
GROUP = 8
MESH = pl.DeviceIdType.MESH

ENERGY = USES
COUNT = USES + RECS


def greet(row, col):
    barrier = pltpu.get_barrier_semaphore()
    for other in range(1, COLS):
        pl.semaphore_signal(
            barrier, inc=1, device_id=(row, lax.rem(col + other, COLS)), device_id_type=MESH
        )

    @pl.when(row > 0)
    def _():
        pl.semaphore_signal(barrier, inc=1, device_id=(row - 1, col), device_id_type=MESH)

    @pl.when(row < ROWS - 1)
    def _():
        pl.semaphore_signal(barrier, inc=1, device_id=(row + 1, col), device_id_type=MESH)

    edges = (row > 0).astype(jnp.int32) + (row < ROWS - 1).astype(jnp.int32)
    pl.semaphore_wait(barrier, COLS - 1 + edges)


def gather_kernel(
    records, index, travel, amp,
    held, travel_out, amp_out, uses_out, index_out,
    near, mixed, lines, uses_vmem, index_vmem,
    local_sems, send_sems, recv_sems, near_send, near_recv, line_send, line_recv,
):
    row, col = lax.axis_index("inline"), lax.axis_index("xline")
    z, x = col // SIDE, lax.rem(col, SIDE)
    loads = [
        pltpu.make_async_copy(travel, travel_out, local_sems.at[0]),
        pltpu.make_async_copy(amp, amp_out, local_sems.at[1]),
        pltpu.make_async_copy(records, held.at[pl.ds(col * RECS, RECS)], local_sems.at[2]),
    ]
    near[...] = jnp.zeros_like(near)
    greet(row, col)

    def at(dz, dx):
        return lax.rem(z + dz + SIDE, SIDE) * SIDE + lax.rem(x + dx + SIDE, SIDE)

    started = {}

    def block(route, first, second, lo, size):
        tile = at(second, first) if route == 0 else at(first, second)
        return pl.ds(tile * RECS + route * BEAMS + lo, size)

    def toward(route, axis, step):
        along_x = (axis == 0) == (route == 0)
        return (row, at(0, step) if along_x else at(step, 0))

    def send(key, route, axis, step, first, second, lo, size):
        here = block(route, first, second, lo, size)
        n = len(started)
        if first == 0 and second == 0:
            source = records.at[pl.ds(route * BEAMS + lo, size)]
        else:
            source = held.at[here]
        copy = pltpu.make_async_remote_copy(
            src_ref=source,
            dst_ref=held.at[here],
            send_sem=send_sems.at[n],
            recv_sem=recv_sems.at[n],
            device_id=toward(route, axis, step),
            device_id_type=MESH,
        )
        copy.start()
        started[key] = copy

    half = BEAMS // 2
    both = (0, 1)
    for route in both:
        for step in (1, -1):
            send(("a", route, step), route, 0, step, 0, 0, 0, BEAMS)
    for route in both:
        for step in (1, -1):
            send(("c", route, 0, step), route, 1, step, 0, 0, 0, BEAMS)
    for copy in loads:
        copy.start()

    up = pltpu.make_async_remote_copy(
        index, near.at[0], near_send.at[0], near_recv.at[0], device_id=(row + 1, col), device_id_type=MESH
    )
    down = pltpu.make_async_remote_copy(
        index, near.at[1], near_send.at[1], near_recv.at[1], device_id=(row - 1, col), device_id_type=MESH
    )
    @pl.when(row < ROWS - 1)
    def _():
        up.start()

    @pl.when(row > 0)
    def _():
        down.start()

    @pl.when(row > 0)
    def _():
        up.wait_recv()

    @pl.when(row < ROWS - 1)
    def _():
        down.wait_recv()

    @pl.when(row < ROWS - 1)
    def _():
        up.wait_send()

    @pl.when(row > 0)
    def _():
        down.wait_send()

    kind = lax.broadcasted_iota(jnp.int32, (8, NS), 1) // RECS
    mixed[...] = jnp.where(kind == 1, near[1], jnp.where(kind == 2, near[0], index[...]))
    shares = []
    for other in range(1, COLS):
        share = pltpu.make_async_remote_copy(
            mixed,
            lines.at[other],
            line_send.at[other],
            line_recv.at[other],
            device_id=(row, lax.rem(col + other, COLS)),
            device_id_type=MESH,
        )
        share.start()
        shares.append(share)
    lines[0] = mixed[...]

    for route in both:
        for step in (1, -1):
            started["a", route, step].wait_recv()
            lo = 0 if step > 0 else half
            send(("b", route, step), route, 0, step, -step, 0, lo, half)
            for way in (1, -1):
                send(("c", route, -step, way), route, 1, way, -step, 0, 0, BEAMS)
    for route in both:
        for way in (1, -1):
            started["c", route, 0, way].wait_recv()
            lo = 0 if way > 0 else half
            send(("d", route, 0, way), route, 1, way, 0, -way, lo, half)

    build_list(row, col, shares, lines, index_vmem, uses_vmem)

    for route in both:
        for step in (1, -1):
            started["b", route, step].wait_recv()
        for way in (1, -1):
            send(("c", route, 2, way), route, 1, way, 2, 0, 0, BEAMS)
    for first in (-1, 1, 2):
        for route in both:
            for way in (1, -1):
                started["c", route, first, way].wait_recv()
                lo = 0 if way > 0 else half
                send(("d", route, first, way), route, 1, way, first, -way, lo, half)
    finish = [
        pltpu.make_async_copy(uses_vmem, uses_out, local_sems.at[3]),
        pltpu.make_async_copy(index_vmem, index_out, local_sems.at[4]),
    ]
    for copy in finish:
        copy.start()
    for first in (0, -1, 1, 2):
        for route in both:
            for way in (1, -1):
                started["d", route, first, way].wait_recv()
    for copy in started.values():
        copy.wait_send()
    for share in shares:
        share.wait_send()
    for copy in loads + finish:
        copy.wait()


def build_list(row, col, shares, lines, index_vmem, uses_vmem):
    for share in shares:
        share.wait_recv()
    for tile in range(COLS):
        index_vmem[pl.ds(tile, 1), :] = lines[lax.rem(col - tile + COLS, COLS)][0:1, :]
    table = index_vmem[...]
    names = table.astype(jnp.int32)
    shape = (COLS, NS)
    lane = lax.broadcasted_iota(jnp.int32, shape, 1)
    tile = lax.broadcasted_iota(jnp.int32, shape, 0)
    kind, beam = lane // RECS, lax.rem(lane, BEAMS)
    counts = jnp.broadcast_to(names[:, COUNT : COUNT + 1], shape)
    before = jnp.where(tile > 0, pltpu.roll(counts, 1, 0), 0)
    after = jnp.where(tile < COLS - 1, pltpu.roll(counts, COLS - 1, 0), 0)
    last, first = (row == ROWS - 1).astype(jnp.int32), (row == 0).astype(jnp.int32)
    live = jnp.where(kind == 3, before, jnp.where(kind == 4, after, counts))
    live = jnp.where(kind == 1, counts * (1 - last), live)
    live = jnp.where(kind == 2, counts * (1 - first), live)
    wanted = (lane < USES) & (beam < live) & (names // 128 == col)
    marks = wanted.astype(jnp.float32)
    earlier = lax.broadcasted_iota(jnp.int32, (NS, NS), 0) <= lax.broadcasted_iota(jnp.int32, (NS, NS), 1)
    within = jnp.dot(marks, earlier.astype(jnp.float32), preferred_element_type=jnp.float32)
    above = lax.broadcasted_iota(jnp.int32, (COLS, COLS), 1) < lax.broadcasted_iota(jnp.int32, (COLS, COLS), 0)
    totals = jnp.broadcast_to(jnp.sum(marks, axis=1, keepdims=True), shape)
    ahead = jnp.dot(above.astype(jnp.float32), totals, preferred_element_type=jnp.float32)
    place = jnp.where(wanted, within + ahead - 1.0, -1.0)
    number = jnp.sum(marks)

    source = tile + (kind == 4).astype(jnp.int32) - (kind == 3).astype(jnp.int32)
    shift = 1 + (kind == 1).astype(jnp.int32) - (kind == 2).astype(jnp.int32)
    fields = (
        lax.rem(names, 128).astype(jnp.float32),
        (source * RECS + lax.rem(lane, RECS)).astype(jnp.float32),
        (shift * COLS + tile).astype(jnp.float32),
    )
    upright = jnp.transpose(place)
    slot = lax.broadcasted_iota(jnp.int32, (NS, LIST), 1).astype(jnp.float32)
    line = lax.broadcasted_iota(jnp.int32, (8, NS), 0)
    listed = jnp.zeros((8, LIST), jnp.float32)
    for t in range(COLS):
        here = (jnp.broadcast_to(upright[:, t : t + 1], (NS, LIST)) == slot).astype(jnp.bfloat16)
        rows = jnp.zeros((8, NS), jnp.float32)
        for f, field in enumerate(fields):
            rows = jnp.where(line == f, jnp.broadcast_to(field[t : t + 1, :], (8, NS)), rows)
        listed += jnp.dot(rows.astype(jnp.bfloat16), here, preferred_element_type=jnp.float32)
    place_in = lax.broadcasted_iota(jnp.int32, (8, LIST), 1).astype(jnp.float32)
    part = lax.broadcasted_iota(jnp.int32, (8, LIST), 0)
    listed = jnp.where((part == 2) & (place_in >= number), float(TARGETS), listed)
    listed = jnp.where(part == 3, number, listed)
    uses_vmem[...] = listed.astype(jnp.int32)


def gather(records, index, travel, amp):
    hbm = pl.BlockSpec(memory_space=pl.ANY)
    vmem = pl.BlockSpec(memory_space=pltpu.VMEM)
    smem = pl.BlockSpec(memory_space=pltpu.SMEM)
    return pl.pallas_call(
        gather_kernel,
        out_shape=(
            pltpu.VMEM((COLS * RECS, NP, NS), jnp.bfloat16),
            pltpu.VMEM(travel.shape, jnp.float32),
            pltpu.VMEM(amp.shape, jnp.float32),
            jax.ShapeDtypeStruct((8, LIST), jnp.int32),
            jax.ShapeDtypeStruct((COLS, NS), jnp.float32),
        ),
        in_specs=[hbm, vmem, hbm, hbm],
        out_specs=(vmem, vmem, vmem, hbm, hbm),
        scratch_shapes=[
            pltpu.VMEM((2, 8, NS), jnp.float32),
            pltpu.VMEM((8, NS), jnp.float32),
            pltpu.VMEM((COLS, 8, NS), jnp.float32),
            pltpu.VMEM((8, LIST), jnp.int32),
            pltpu.VMEM((COLS, NS), jnp.float32),
            pltpu.SemaphoreType.DMA((5,)),
            pltpu.SemaphoreType.DMA((40,)),
            pltpu.SemaphoreType.DMA((40,)),
            pltpu.SemaphoreType.DMA((2,)),
            pltpu.SemaphoreType.DMA((2,)),
            pltpu.SemaphoreType.DMA((COLS,)),
            pltpu.SemaphoreType.DMA((COLS,)),
        ],
        compiler_params=pltpu.CompilerParams(
            collective_id=1, has_side_effects=True, vmem_limit_bytes=32 << 20
        ),
        cost_estimate=pl.CostEstimate(flops=10_000_000, bytes_accessed=16_000_000, transcendentals=0),
        name="gather_records",
    )(records, index, travel, amp)


def image_kernel(uses, index, records, travel, amp, out, acc):
    acc[...] = jnp.zeros_like(acc)

    def step(i, carry):
        picked = []
        for d in range(GROUP):
            u = i * GROUP + d
            picked.append((uses[0, u], uses[1, u], uses[2, u]))
        totals = [jnp.zeros((8, NS), jnp.float32) for _ in picked]
        squares = [jnp.zeros((8, NS), jnp.float32) for _ in picked]
        for q in range(NP // 8):
            rows = pl.ds(8 * q, 8)
            for d, (block, rec, _) in enumerate(picked):
                t = travel[block, rows, :]
                a = amp[block, rows, :]
                pair = records[rec, pl.ds(16 * (q // 2), 16), :].astype(jnp.float32)
                r = pair[8 * (q % 2) : 8 * (q % 2) + 8]
                k = t.astype(jnp.int32)
                f = t - k.astype(jnp.float32)
                w0 = (1.0 - f).astype(jnp.bfloat16).astype(jnp.float32)
                w1 = f.astype(jnp.bfloat16).astype(jnp.float32)
                v0 = jnp.take_along_axis(r, k, axis=1, mode="promise_in_bounds")
                v1 = jnp.take_along_axis(r, k + 1, axis=1, mode="promise_in_bounds")
                totals[d] += a * (v0 * w0 + v1 * w1)
                squares[d] += a * a
        for d, (_, rec, target) in enumerate(picked):
            energy = index[rec // RECS, ENERGY + lax.rem(rec, RECS)]
            acc[target, 0] += totals[d]
            acc[target, 1] += squares[d] * energy
        return carry

    lax.fori_loop(0, (uses[3, 0] + GROUP - 1) // GROUP, step, 0)
    out[...] = jnp.sum(acc[pl.ds(0, TARGETS)], axis=2)


def image(uses, index, records, travel, amp):
    vmem = pl.BlockSpec(memory_space=pltpu.VMEM)
    smem = pl.BlockSpec(memory_space=pltpu.SMEM)
    return pl.pallas_call(
        image_kernel,
        out_shape=pltpu.VMEM((TARGETS, 2, NS), jnp.float32),
        in_specs=[smem, smem, vmem, vmem, vmem],
        out_specs=vmem,
        scratch_shapes=[pltpu.VMEM((TARGETS + 1, 2, 8, NS), jnp.float32)],
        compiler_params=pltpu.CompilerParams(vmem_limit_bytes=32 << 20),
        cost_estimate=pl.CostEstimate(flops=10_000_000, bytes_accessed=8_000_000, transcendentals=0),
        name="image_uses",
    )(uses, index, records, travel, amp)


def exchange_kernel(sums, out, near, total, parts, near_send, near_recv, part_send, part_recv):
    row, col = lax.axis_index("inline"), lax.axis_index("xline")
    greet(row, col)
    up = pltpu.make_async_remote_copy(
        sums.at[2], near.at[0], near_send.at[0], near_recv.at[0], device_id=(row + 1, col), device_id_type=MESH
    )
    down = pltpu.make_async_remote_copy(
        sums.at[0], near.at[1], near_send.at[1], near_recv.at[1], device_id=(row - 1, col), device_id_type=MESH
    )

    @pl.when(row < ROWS - 1)
    def _():
        up.start()

    @pl.when(row > 0)
    def _():
        down.start()

    total[...] = sums[1]

    @pl.when(row > 0)
    def _():
        up.wait_recv()
        total[...] += near[0]

    @pl.when(row < ROWS - 1)
    def _():
        down.wait_recv()
        total[...] += near[1]

    copies = []
    for other in range(1, COLS):
        there = lax.rem(col + other, COLS)
        copy = pltpu.make_async_remote_copy(
            total.at[there],
            parts.at[other],
            part_send.at[other],
            part_recv.at[other],
            device_id=(row, there),
            device_id_type=MESH,
        )
        copy.start()
        copies.append(copy)
    mine = total[col]
    for copy, other in zip(copies, range(1, COLS)):
        copy.wait_recv()
        mine += parts[other]
    out[0] = mine[0:1] / jnp.sqrt(1.0 + mine[1:2])
    for copy in copies:
        copy.wait_send()

    @pl.when(row < ROWS - 1)
    def _():
        up.wait_send()

    @pl.when(row > 0)
    def _():
        down.wait_send()


def exchange(sums):
    vmem = pl.BlockSpec(memory_space=pltpu.VMEM)
    return pl.pallas_call(
        exchange_kernel,
        out_shape=jax.ShapeDtypeStruct((1, 1, NS), jnp.float32),
        in_specs=[vmem],
        out_specs=vmem,
        scratch_shapes=[
            pltpu.VMEM((2, COLS, 2, NS), jnp.float32),
            pltpu.VMEM((COLS, 2, NS), jnp.float32),
            pltpu.VMEM((COLS, 2, NS), jnp.float32),
            pltpu.SemaphoreType.DMA((2,)),
            pltpu.SemaphoreType.DMA((2,)),
            pltpu.SemaphoreType.DMA((COLS,)),
            pltpu.SemaphoreType.DMA((COLS,)),
        ],
        compiler_params=pltpu.CompilerParams(collective_id=2, has_side_effects=True),
        cost_estimate=pl.CostEstimate(flops=10_000, bytes_accessed=100_000, transcendentals=0),
        name="exchange_sums",
    )(sums)


def imaged_by_any_count(records, beam_count, owner_list, block_list, travel_table, amp_table):
    records = records.reshape(RECS, NP, NS)
    named = (owner_list * 128 + block_list)[:, 0].astype(jnp.float32)
    named = named.reshape(SHOTS, 5, BEAMS).transpose(1, 0, 2).reshape(USES)
    energy = jnp.mean(jnp.square(records.astype(jnp.float32)), axis=(1, 2))
    count = jnp.broadcast_to(beam_count[0].astype(jnp.float32), (NS - COUNT,))
    index = jnp.broadcast_to(jnp.concatenate([named, energy, count]), (8, NS))
    gathered, travel, amp, uses, index = gather(records, index, travel_table, amp_table)
    sums = image(uses, index, gathered, travel, amp)
    return exchange(sums.reshape(3, COLS, 2, NS))


CLASSES = (
    (((0, 0), (1, 0), (-1, 0), (2, 0)), 48, 0, 64),
    (((0, 1), (0, -1), (1, 1), (1, -1), (-1, 1), (-1, -1)), 64, 64, 128),
    (((2, 1), (2, -1), (0, 2)), 40, 144, 64),
    (((1, 2), (-1, 2)), 32, 184, 32),
    (((2, 2),), 24, 216, 16),
)
WHERE = {tile: (c, n) for c, (tiles, _, _, _) in enumerate(CLASSES) for n, tile in enumerate(tiles)}
FAR_FIRST = sorted(
    ((dz, dx) for dz in (0, 1, -1, 2) for dx in (0, 1, -1, 2) if (dz, dx) != (0, 0)),
    key=lambda step: -abs(step[0]) - abs(step[1]),
)
SLOTS = 256
NBLOCKS = 128
COPIES = 40


def wrap(steps):
    return (steps + 1) % SIDE - 1


def fused_kernel(
    records, owner, block, count, travel, amp,
    out, flag_out,
    wide, buf0, buf1, buf2, buf3, buf4, travel_v, amp_v,
    mine, near, mixed, lines, uses_v, uses_s,
    con0, con1, con2, con3, con4, lit0, lit1, lit2, lit3, lit4,
    flag_mine, flags, sums, parts, edges, records_v, owner_v, block_v, met,
    local_sems, send_sems, recv_sems, near_send, near_recv, line_send, line_recv,
    flag_send, flag_recv, part_send, part_recv, edge_send, edge_recv,
    early_v, late_v, last_v, late_in, late_send, late_recv, energy_v,
):
    row, col = lax.axis_index("inline"), lax.axis_index("xline")
    z, x = col // SIDE, lax.rem(col, SIDE)
    bufs = (buf0, buf1, buf2, buf3, buf4)
    cons, lits = (con0, con1, con2, con3, con4), (lit0, lit1, lit2, lit3, lit4)
    near[...] = jnp.zeros_like(near)
    edges[...] = jnp.zeros_like(edges)

    def at(dz, dx):
        return lax.rem(z + dz + SIDE, SIDE) * SIDE + lax.rem(x + dx + SIDE, SIDE)

    beside = [(row, at(dz, dx)) for dz, dx in ((0, 1), (0, -1), (1, 0), (-1, 0))]
    beside += [(lax.rem(row + 1, ROWS), col), (lax.rem(row + ROWS - 1, ROWS), col)]
    barrier = pltpu.get_barrier_semaphore()
    for there in beside:
        pl.semaphore_signal(barrier, inc=1, device_id=there, device_id_type=MESH)
    inputs = [
        pltpu.make_async_copy(records, records_v, local_sems.at[3]),
        pltpu.make_async_copy(owner, owner_v, local_sems.at[4]),
        pltpu.make_async_copy(block, block_v, local_sems.at[5]),
    ]
    for copy in inputs:
        copy.start()
    loads = [
        pltpu.make_async_copy(travel, travel_v, local_sems.at[0]),
        pltpu.make_async_copy(amp, amp_v, local_sems.at[1]),
    ]
    for copy in loads:
        copy.start()

    for copy in inputs:
        copy.wait()

    wide[pl.ds(0, SHOTS * NP * BEAMS), :] = records_v[...].astype(jnp.float32).reshape(SHOTS * NP * BEAMS, NS)
    energies = jnp.zeros((8, NS), jnp.float32)
    lane8 = lax.broadcasted_iota(jnp.int32, (8, NS), 1)
    for s in range(SHOTS):
        for b in range(BEAMS):
            rec = wide[pl.ds(s * NP * BEAMS + b, NP, stride=BEAMS), :]
            bufs[0][row_of(s, 0, 0) + b] = rec.astype(jnp.bfloat16)
            energy = jnp.sum(rec * rec, keepdims=True) * (1.0 / (NP * NS))
            energies = jnp.where(lane8 == ENERGY + s * BEAMS + b, jnp.broadcast_to(energy, (8, NS)), energies)
    named = (owner_v[...] * 128 + block_v[...]).astype(jnp.float32)
    mine[...] = jnp.where(lane8 >= COUNT, count[0, 0].astype(jnp.float32), energies)
    mine[:, 0:USES] = jnp.broadcast_to(named, (8, USES))
    pl.semaphore_wait(barrier, len(beside))

    started = {}

    def send(kind, route, axis, step, first, second, lo, size):
        seen = (wrap(first - step), second) if axis == 0 else (first, wrap(second - step))
        here, there = WHERE[first, second][0], WHERE[seen][0]
        along_x = (axis == 0) == (route == 0)
        n = len(started)
        copy = pltpu.make_async_remote_copy(
            src_ref=bufs[here].at[pl.ds(row_of(route, first, second) + lo, size)],
            dst_ref=bufs[there].at[pl.ds(row_of(route, *seen) + lo, size)],
            send_sem=send_sems.at[n],
            recv_sem=recv_sems.at[n],
            device_id=(row, at(0, step) if along_x else at(step, 0)),
            device_id_type=MESH,
        )
        copy.start()
        key = (kind, route, step) if axis == 0 else (kind, route, first, step)
        started[key] = copy

    both, ways = (0, 1), (1, -1)
    half = BEAMS // 2

    def along_second(first):
        for way in ways:
            for route in both:
                send("c", route, 1, way, first, 0, 0, BEAMS)

    def pass_on(first):
        for way in ways:
            for route in both:
                started["c", route, first, way].wait_recv()
                send("d", route, 1, way, first, -way, 0 if way > 0 else half, half)

    def arrived(first):
        for route in both:
            for way in ways:
                started["d", route, first, way].wait_recv()

    def image_some(p, begin, end, group=GROUP):
        _, slots, base, held = CLASSES[p]
        buf, con, lit = bufs[p], cons[p], lits[p]

        def step(i, carry):
            places = [base + i * group + d for d in range(group)]
            picked = [(uses_s[0, u] & (NBLOCKS - 1), uses_s[1, u] & (held - 1)) for u in places]
            for d, (number, rec) in enumerate(picked):
                total, square = jnp.zeros((8, NS), jnp.float32), jnp.zeros((8, NS), jnp.float32)
                for q in range(NP // 8):
                    rows = pl.ds(8 * q, 8)
                    t = travel_v[number, rows, :]
                    a = amp_v[number, rows, :]
                    pair = buf[rec, pl.ds(16 * (q // 2), 16), :].astype(jnp.float32)
                    r = pair[8 * (q % 2) : 8 * (q % 2) + 8]
                    k = t.astype(jnp.int32)
                    f = t - k.astype(jnp.float32)
                    w0 = (1.0 - f).astype(jnp.bfloat16).astype(jnp.float32)
                    w1 = f.astype(jnp.bfloat16).astype(jnp.float32)
                    v0 = jnp.take_along_axis(r, k, axis=1, mode="promise_in_bounds")
                    v1 = jnp.take_along_axis(r, k + 1, axis=1, mode="promise_in_bounds")
                    total += a * (v0 * w0 + v1 * w1)
                    square += a * a
                con[pl.ds(i * group + d, 8, stride=slots), :] = total
                lit[pl.ds(i * group + d, 8, stride=slots), :] = square
            return carry

        if end - begin == group:
            step(begin // group, 0)
        else:
            lax.fori_loop(begin // group, end // group, step, 0)

    def total_of(p, listed):
        _, slots, base, _ = CLASSES[p]
        con = sum(cons[p][pl.ds(s * slots, slots), :] for s in range(8))
        lit = sum(lits[p][pl.ds(s * slots, slots), :] for s in range(8)) * energy_v[pl.ds(base, slots), :]
        target = jnp.broadcast_to(listed[2:3, base : base + slots], (NS, slots))
        line = (lax.broadcasted_iota(jnp.int32, (NS, slots), 0) + 1).astype(jnp.float32)
        to_tile = jnp.where(target == line, 1.0, 0.0).astype(jnp.bfloat16)
        rest = jnp.concatenate([con, lit], axis=1)
        total = jnp.zeros((NS, 2 * NS), jnp.float32)
        for _ in range(3):
            part = rest.astype(jnp.bfloat16)
            rest = rest - part.astype(jnp.float32)
            total += jnp.dot(to_tile, part, preferred_element_type=jnp.float32)
        return total[:, :NS] + pltpu.roll(total[:, NS:], 4, 0)

    for step in ways:
        for route in both:
            send("a", route, 0, step, 0, 0, 0, BEAMS)
    along_second(0)

    up = pltpu.make_async_remote_copy(
        mine, near.at[0], near_send.at[0], near_recv.at[0], device_id=(row + 1, col), device_id_type=MESH
    )
    down = pltpu.make_async_remote_copy(
        mine, near.at[1], near_send.at[1], near_recv.at[1], device_id=(row - 1, col), device_id_type=MESH
    )
    upward, downward = pl.when(row < ROWS - 1), pl.when(row > 0)
    upward(up.start)
    downward(down.start)
    apart = [(row, at(dz, dx)) for dz, dx in ((1, 1), (1, -1), (-1, 1), (-1, -1), (0, 2), (2, 0))]
    apart += [(lax.rem(row + 2, ROWS), col), (lax.rem(row + ROWS - 2, ROWS), col)]
    for turn, others in enumerate((beside, apart)):
        for there in others:
            pl.semaphore_signal(met.at[turn], inc=1, device_id=there, device_id_type=MESH)
        pl.semaphore_wait(met.at[turn], len(others))
    downward(up.wait_recv)
    upward(down.wait_recv)
    kind8 = lax.rem(lane8, 5 * BEAMS) // BEAMS
    kind8 = jnp.where(lane8 < USES, kind8, 0)
    mixed[...] = jnp.where(kind8 == 1, near[1], jnp.where(kind8 == 2, near[0], mine[...]))
    shares = []
    for other in range(1, COLS):
        share = pltpu.make_async_remote_copy(
            mixed, lines.at[other], line_send.at[other], line_recv.at[other],
            device_id=(row, lax.rem(col + other, COLS)), device_id_type=MESH,
        )
        share.start()
        shares.append(share)
    lines[0] = mixed[...]

    for step in ways:
        for route in both:
            started["a", route, step].wait_recv()
            send("b", route, 0, step, -step, 0, 0 if step > 0 else half, half)
        along_second(-step)

    for share in shares:
        share.wait_recv()
    listed, energy, over = list_uses(row, col, lines)
    energy_v[...] = jnp.transpose(jnp.broadcast_to(energy, (NS, SLOTS)))
    uses_v[...] = listed.astype(jnp.int32)
    to_smem = pltpu.make_async_copy(uses_v, uses_s, local_sems.at[2])
    to_smem.start()
    flag_mine[...] = over
    alarms = []
    for other in range(1, ROWS):
        alarm = pltpu.make_async_remote_copy(
            flag_mine, flags.at[other], flag_send.at[other], flag_recv.at[other],
            device_id=(lax.rem(row + other, ROWS), col), device_id_type=MESH,
        )
        alarm.start()
        alarms.append(alarm)

    for route in both:
        for step in ways:
            started["b", route, step].wait_recv()
    along_second(2)
    pass_on(0)
    to_smem.wait()
    for copy in loads:
        copy.wait()
    image_some(0, 0, 48, 16)
    pass_on(1)
    pass_on(-1)
    image_some(1, 0, 64, 16)
    pass_on(2)
    early = total_of(0, listed) + total_of(1, listed)
    arrived(0)
    image_some(2, 0, 40, 20)
    early += total_of(2, listed)
    early_v[...] = early.reshape(COLS, 8, NS)
    to_next = pltpu.make_async_remote_copy(
        early_v, edges.at[0], edge_send.at[0], edge_recv.at[0], device_id=(row + 1, col), device_id_type=MESH
    )
    to_prev = pltpu.make_async_remote_copy(
        early_v, edges.at[1], edge_send.at[1], edge_recv.at[1], device_id=(row - 1, col), device_id_type=MESH
    )
    upward(to_next.start)
    downward(to_prev.start)
    raised = flag_mine[...]
    for alarm, other in zip(alarms, range(1, ROWS)):
        alarm.wait_recv()
        raised = jnp.maximum(raised, flags[other])
    flag_out[0] = jnp.max(raised).astype(jnp.int32)
    arrived(1)
    arrived(-1)
    image_some(3, 0, 32, 32)
    late_v[...] = total_of(3, listed).reshape(COLS, 8, NS)
    next_row, prev_row = lax.rem(row + 1, ROWS), lax.rem(row + ROWS - 1, ROWS)
    direct = []

    def straight(source, dz, dx):
        for beside_row in (next_row, prev_row):
            n = len(direct)
            copy = pltpu.make_async_remote_copy(
                source.at[at(dz, dx)], late_in.at[n], late_send.at[n], late_recv.at[n],
                device_id=(beside_row, at(dz, dx)), device_id_type=MESH,
            )
            copy.start()
            direct.append(copy)

    for dz, dx in ((2, 1), (2, -1), (1, 2), (-1, 2)):
        straight(late_v, dz, dx)
    arrived(2)
    image_some(4, 0, 24, 24)
    last_v[...] = total_of(4, listed).reshape(COLS, 8, NS)
    straight(last_v, 2, 2)
    downward(to_next.wait_recv)
    upward(to_prev.wait_recv)
    own = early_v[...] + late_v[...] + last_v[...]
    sums[...] = own + pltpu.roll(edges[0], 7, 1) + pltpu.roll(edges[1], 1, 1)

    pieces = []
    for n, (dz, dx) in enumerate(FAR_FIRST):
        there = at(dz, dx)
        piece = pltpu.make_async_remote_copy(
            sums.at[there], parts.at[n], part_send.at[n], part_recv.at[n],
            device_id=(row, there), device_id_type=MESH,
        )
        piece.start()
        pieces.append(piece)
    for copy in started.values():
        copy.wait_send()
    for copy in shares + alarms + direct:
        copy.wait_send()
    upward(up.wait_send)
    downward(down.wait_send)
    upward(to_next.wait_send)
    downward(to_prev.wait_send)
    contrib, lighting = sums[col][1:2], sums[col][5:6]
    for n, copy in enumerate(direct):
        copy.wait_recv()
        line = 2 if n % 2 == 0 else 0
        contrib += late_in[n][line : line + 1]
        lighting += late_in[n][line + 4 : line + 5]
    whole = jnp.zeros((8, NS), jnp.float32)
    for n, piece in enumerate(pieces):
        piece.wait_recv()
        whole += parts[n]
    out[0] = (contrib + whole[1:2]) / jnp.sqrt(1.0 + (lighting + whole[5:6]))
    for piece in pieces:
        piece.wait_send()


def row_of(route, first, second):
    c, n = WHERE[first, second]
    return (route * len(CLASSES[c][0]) + n) * BEAMS


def list_uses(row, col, lines):
    table = jnp.concatenate([lines[lax.rem(col - tile + COLS, COLS)][0:1, :] for tile in range(COLS)], axis=0)
    shape = (COLS, NS)
    lane = lax.broadcasted_iota(jnp.int32, shape, 1)
    tile = lax.broadcasted_iota(jnp.int32, shape, 0)
    shot, kind, beam = lane // (5 * BEAMS), lax.rem(lane, 5 * BEAMS) // BEAMS, lax.rem(lane, BEAMS)
    names = table.astype(jnp.int32)

    def of_source(own):
        before, after = pltpu.roll(own, 1, 0), pltpu.roll(own, COLS - 1, 0)
        return jnp.where(kind == 3, before, jnp.where(kind == 4, after, own))

    last, first = (row == ROWS - 1).astype(jnp.int32), (row == 0).astype(jnp.int32)
    missing = (
        ((kind == 1) & (last == 1))
        | ((kind == 2) & (first == 1))
        | ((kind == 3) & (tile == 0))
        | ((kind == 4) & (tile == COLS - 1))
    )
    counts = of_source(jnp.broadcast_to(names[:, COUNT : COUNT + 1], shape))
    energy = of_source(
        jnp.take_along_axis(
            table, jnp.where(lane < USES, ENERGY + shot * BEAMS + beam, lane), axis=1, mode="promise_in_bounds"
        )
    )
    live = (lane < USES) & (beam < counts) & jnp.logical_not(missing)
    owners = names // 128

    source = tile + (kind == 4).astype(jnp.int32) - (kind == 3).astype(jnp.int32)
    along_z = (source // SIDE - owners // SIDE) & (SIDE - 1)
    along_x = (source - owners) & (SIDE - 1)
    code = jnp.where(shot == 0, along_x * SIDE + along_z, along_z * SIDE + along_x)
    group, record = jnp.zeros(shape, jnp.int32), jnp.zeros(shape, jnp.int32)
    for (first_step, second_step), (c, _) in WHERE.items():
        same = code == first_step % SIDE * SIDE + second_step % SIDE
        group = jnp.where(same, c, group)
        begin = [row_of(route, first_step, second_step) for route in (0, 1)]
        record = jnp.where(same, jnp.where(shot == 0, begin[0], begin[1]) + beam, record)

    column = lax.broadcasted_iota(jnp.int32, (NS, NS), 1)
    owned = jnp.where(live, owners * 8 + group, -1)
    over = jnp.zeros((1, 1), jnp.float32)
    for c, (_, slots, _, _) in enumerate(CLASSES):
        per_owner = jnp.concatenate(
            [jnp.sum((owned == o * 8 + c).astype(jnp.float32), axis=0, keepdims=True) for o in range(COLS)], axis=0
        )
        held = jnp.sum(per_owner, axis=1, keepdims=True)
        over = jnp.maximum(over, jnp.max((held > float(slots)).astype(jnp.float32), keepdims=True))

    earlier = lax.broadcasted_iota(jnp.int32, (NS, NS), 0) <= column
    above = lax.broadcasted_iota(jnp.int32, (COLS, COLS), 1) < lax.broadcasted_iota(jnp.int32, (COLS, COLS), 0)
    shift = 1 + (kind == 1).astype(jnp.int32) - (kind == 2).astype(jnp.int32)
    place = jnp.full(shape, -1.0)
    for c, (_, slots, base, _) in enumerate(CLASSES):
        marks = live & (owners == col) & (group == c)
        ones = marks.astype(jnp.float32)
        within = jnp.dot(ones, earlier.astype(jnp.float32), preferred_element_type=jnp.float32)
        totals = jnp.broadcast_to(jnp.sum(ones, axis=1, keepdims=True), shape)
        ahead = jnp.dot(above.astype(jnp.float32), totals, preferred_element_type=jnp.float32)
        rank = within + ahead - 1.0
        place = jnp.where(marks & (rank < float(slots)), rank + float(base), place)
    high = energy.astype(jnp.bfloat16).astype(jnp.float32)
    middle = (energy - high).astype(jnp.bfloat16).astype(jnp.float32)
    low = energy - high - middle
    fields = (
        lax.rem(names, 128).astype(jnp.float32),
        record.astype(jnp.float32),
        (tile * 8 + shift + 1).astype(jnp.float32),
        high,
        middle,
        low,
    )
    upright = jnp.transpose(place)
    slot = lax.broadcasted_iota(jnp.int32, (NS, SLOTS), 1).astype(jnp.float32)
    line = lax.broadcasted_iota(jnp.int32, (8, NS), 0)
    listed = jnp.zeros((8, SLOTS), jnp.float32)
    for t in range(COLS):
        here = (jnp.broadcast_to(upright[:, t : t + 1], (NS, SLOTS)) == slot).astype(jnp.bfloat16)
        rows = jnp.zeros((8, NS), jnp.float32)
        for f, field in enumerate(fields):
            rows = jnp.where(line == f, jnp.broadcast_to(field[t : t + 1, :], (8, NS)), rows)
        listed += jnp.dot(rows.astype(jnp.bfloat16), here, preferred_element_type=jnp.float32)
    return listed, listed[3:4] + listed[4:5] + listed[5:6], jnp.broadcast_to(over, (8, NS))


def fused(records, owner, block, count, travel, amp):
    vmem = pl.BlockSpec(memory_space=pltpu.VMEM)
    smem = pl.BlockSpec(memory_space=pltpu.SMEM)
    hbm = pl.BlockSpec(memory_space=pl.ANY)
    dma = pltpu.SemaphoreType.DMA
    f32 = jnp.float32
    return pl.pallas_call(
        fused_kernel,
        out_shape=(jax.ShapeDtypeStruct((1, 1, NS), f32), jax.ShapeDtypeStruct((1,), jnp.int32)),
        in_specs=[hbm, hbm, hbm, smem, hbm, hbm],
        out_specs=(vmem, smem),
        scratch_shapes=[
            pltpu.VMEM(((SHOTS * NP + 1) * BEAMS, NS), f32),
            *[pltpu.VMEM((held, NP, NS), jnp.bfloat16) for _, _, _, held in CLASSES],
            pltpu.VMEM(travel.shape, f32),
            pltpu.VMEM(amp.shape, f32),
            pltpu.VMEM((8, NS), f32),
            pltpu.VMEM((2, 8, NS), f32),
            pltpu.VMEM((8, NS), f32),
            pltpu.VMEM((COLS, 8, NS), f32),
            pltpu.VMEM((8, SLOTS), jnp.int32),
            pltpu.SMEM((8, SLOTS), jnp.int32),
            *[pltpu.VMEM((9 * slots, NS), f32) for _, slots, _, _ in CLASSES],
            *[pltpu.VMEM((9 * slots, NS), f32) for _, slots, _, _ in CLASSES],
            pltpu.VMEM((8, NS), f32),
            pltpu.VMEM((ROWS, 8, NS), f32),
            pltpu.VMEM((COLS, 8, NS), f32),
            pltpu.VMEM((COLS, 8, NS), f32),
            pltpu.VMEM((2, COLS, 8, NS), f32),
            pltpu.VMEM(records.shape, records.dtype),
            pltpu.VMEM(owner.shape, jnp.int32),
            pltpu.VMEM(block.shape, jnp.int32),
            pltpu.SemaphoreType.REGULAR((2,)),
            dma((6,)),
            dma((COPIES,)),
            dma((COPIES,)),
            dma((2,)),
            dma((2,)),
            dma((COLS,)),
            dma((COLS,)),
            dma((ROWS,)),
            dma((ROWS,)),
            dma((COLS,)),
            dma((COLS,)),
            dma((2,)),
            dma((2,)),
            pltpu.VMEM((COLS, 8, NS), f32),
            pltpu.VMEM((COLS, 8, NS), f32),
            pltpu.VMEM((COLS, 8, NS), f32),
            pltpu.VMEM((10, 8, NS), f32),
            dma((10,)),
            dma((10,)),
            pltpu.VMEM((SLOTS, NS), f32),
        ],
        compiler_params=pltpu.CompilerParams(
            collective_id=0, has_side_effects=True, vmem_limit_bytes=40 << 20
        ),
        cost_estimate=pl.CostEstimate(flops=10_000_000, bytes_accessed=16_000_000, transcendentals=0),
        name="migrate",
    )(records, owner, block, count, travel, amp)


def per_device(records, beam_count, owner_list, block_list, travel_table, amp_table):
    travel_table = pltpu.with_memory_space_constraint(travel_table, pltpu.HBM)
    amp_table = pltpu.with_memory_space_constraint(amp_table, pltpu.HBM)
    by_slowness = records.reshape(SHOTS, BEAMS, NP, NS).transpose(0, 2, 1, 3)
    owner, block = owner_list.reshape(1, USES), block_list.reshape(1, USES)
    quick, flag = fused(by_slowness, owner, block, beam_count, travel_table, amp_table)
    return lax.cond(
        flag[0] > 0,
        lambda: imaged_by_any_count(records, beam_count, owner_list, block_list, travel_table, amp_table),
        lambda: quick,
    )


def solution(mesh):
    placed = (
        P(None, "inline", "xline", None, None),
        P("inline", "xline"),
        P(("inline", "xline"), None),
        P(("inline", "xline"), None),
        P("xline", None, None),
        P("xline", None, None),
    )
    return jax.shard_map(
        per_device,
        mesh=mesh,
        in_specs=placed,
        out_specs=P("inline", "xline", None),
        check_vma=False,
    )
```

```python
import jax
import jax.numpy as jnp
from jax import lax
from jax.experimental import pallas as pl
from jax.experimental.pallas import tpu as pltpu
from jax.sharding import PartitionSpec as P

NS = 128
NP = 64
BEAMS = 8
SHOTS = 2
RECS = SHOTS * BEAMS
SIDE = 4
COLS = SIDE * SIDE
ROWS = 8
USES = 5 * RECS
LIST = 512
TARGETS = 3 * COLS
GROUP = 8
MESH = pl.DeviceIdType.MESH

ENERGY = USES
COUNT = USES + RECS


def greet(row, col):
    barrier = pltpu.get_barrier_semaphore()
    for other in range(1, COLS):
        pl.semaphore_signal(
            barrier, inc=1, device_id=(row, lax.rem(col + other, COLS)), device_id_type=MESH
        )

    @pl.when(row > 0)
    def _():
        pl.semaphore_signal(barrier, inc=1, device_id=(row - 1, col), device_id_type=MESH)

    @pl.when(row < ROWS - 1)
    def _():
        pl.semaphore_signal(barrier, inc=1, device_id=(row + 1, col), device_id_type=MESH)

    edges = (row > 0).astype(jnp.int32) + (row < ROWS - 1).astype(jnp.int32)
    pl.semaphore_wait(barrier, COLS - 1 + edges)


def gather_kernel(
    records, index, travel, amp,
    held, travel_out, amp_out, uses_out, index_out,
    near, mixed, lines, uses_vmem, index_vmem,
    local_sems, send_sems, recv_sems, near_send, near_recv, line_send, line_recv,
):
    row, col = lax.axis_index("inline"), lax.axis_index("xline")
    z, x = col // SIDE, lax.rem(col, SIDE)
    loads = [
        pltpu.make_async_copy(travel, travel_out, local_sems.at[0]),
        pltpu.make_async_copy(amp, amp_out, local_sems.at[1]),
        pltpu.make_async_copy(records, held.at[pl.ds(col * RECS, RECS)], local_sems.at[2]),
    ]
    near[...] = jnp.zeros_like(near)
    greet(row, col)

    def at(dz, dx):
        return lax.rem(z + dz + SIDE, SIDE) * SIDE + lax.rem(x + dx + SIDE, SIDE)

    started = {}

    def block(route, first, second, lo, size):
        tile = at(second, first) if route == 0 else at(first, second)
        return pl.ds(tile * RECS + route * BEAMS + lo, size)

    def toward(route, axis, step):
        along_x = (axis == 0) == (route == 0)
        return (row, at(0, step) if along_x else at(step, 0))

    def send(key, route, axis, step, first, second, lo, size):
        here = block(route, first, second, lo, size)
        n = len(started)
        if first == 0 and second == 0:
            source = records.at[pl.ds(route * BEAMS + lo, size)]
        else:
            source = held.at[here]
        copy = pltpu.make_async_remote_copy(
            src_ref=source,
            dst_ref=held.at[here],
            send_sem=send_sems.at[n],
            recv_sem=recv_sems.at[n],
            device_id=toward(route, axis, step),
            device_id_type=MESH,
        )
        copy.start()
        started[key] = copy

    half = BEAMS // 2
    both = (0, 1)
    for route in both:
        for step in (1, -1):
            send(("a", route, step), route, 0, step, 0, 0, 0, BEAMS)
    for route in both:
        for step in (1, -1):
            send(("c", route, 0, step), route, 1, step, 0, 0, 0, BEAMS)
    for copy in loads:
        copy.start()

    up = pltpu.make_async_remote_copy(
        index, near.at[0], near_send.at[0], near_recv.at[0], device_id=(row + 1, col), device_id_type=MESH
    )
    down = pltpu.make_async_remote_copy(
        index, near.at[1], near_send.at[1], near_recv.at[1], device_id=(row - 1, col), device_id_type=MESH
    )
    @pl.when(row < ROWS - 1)
    def _():
        up.start()

    @pl.when(row > 0)
    def _():
        down.start()

    @pl.when(row > 0)
    def _():
        up.wait_recv()

    @pl.when(row < ROWS - 1)
    def _():
        down.wait_recv()

    @pl.when(row < ROWS - 1)
    def _():
        up.wait_send()

    @pl.when(row > 0)
    def _():
        down.wait_send()

    kind = lax.broadcasted_iota(jnp.int32, (8, NS), 1) // RECS
    mixed[...] = jnp.where(kind == 1, near[1], jnp.where(kind == 2, near[0], index[...]))
    shares = []
    for other in range(1, COLS):
        share = pltpu.make_async_remote_copy(
            mixed,
            lines.at[other],
            line_send.at[other],
            line_recv.at[other],
            device_id=(row, lax.rem(col + other, COLS)),
            device_id_type=MESH,
        )
        share.start()
        shares.append(share)
    lines[0] = mixed[...]

    for route in both:
        for step in (1, -1):
            started["a", route, step].wait_recv()
            lo = 0 if step > 0 else half
            send(("b", route, step), route, 0, step, -step, 0, lo, half)
            for way in (1, -1):
                send(("c", route, -step, way), route, 1, way, -step, 0, 0, BEAMS)
    for route in both:
        for way in (1, -1):
            started["c", route, 0, way].wait_recv()
            lo = 0 if way > 0 else half
            send(("d", route, 0, way), route, 1, way, 0, -way, lo, half)

    build_list(row, col, shares, lines, index_vmem, uses_vmem)

    for route in both:
        for step in (1, -1):
            started["b", route, step].wait_recv()
        for way in (1, -1):
            send(("c", route, 2, way), route, 1, way, 2, 0, 0, BEAMS)
    for first in (-1, 1, 2):
        for route in both:
            for way in (1, -1):
                started["c", route, first, way].wait_recv()
                lo = 0 if way > 0 else half
                send(("d", route, first, way), route, 1, way, first, -way, lo, half)
    finish = [
        pltpu.make_async_copy(uses_vmem, uses_out, local_sems.at[3]),
        pltpu.make_async_copy(index_vmem, index_out, local_sems.at[4]),
    ]
    for copy in finish:
        copy.start()
    for first in (0, -1, 1, 2):
        for route in both:
            for way in (1, -1):
                started["d", route, first, way].wait_recv()
    for copy in started.values():
        copy.wait_send()
    for share in shares:
        share.wait_send()
    for copy in loads + finish:
        copy.wait()


def build_list(row, col, shares, lines, index_vmem, uses_vmem):
    for share in shares:
        share.wait_recv()
    for tile in range(COLS):
        index_vmem[pl.ds(tile, 1), :] = lines[lax.rem(col - tile + COLS, COLS)][0:1, :]
    table = index_vmem[...]
    names = table.astype(jnp.int32)
    shape = (COLS, NS)
    lane = lax.broadcasted_iota(jnp.int32, shape, 1)
    tile = lax.broadcasted_iota(jnp.int32, shape, 0)
    kind, beam = lane // RECS, lax.rem(lane, BEAMS)
    counts = jnp.broadcast_to(names[:, COUNT : COUNT + 1], shape)
    before = jnp.where(tile > 0, pltpu.roll(counts, 1, 0), 0)
    after = jnp.where(tile < COLS - 1, pltpu.roll(counts, COLS - 1, 0), 0)
    last, first = (row == ROWS - 1).astype(jnp.int32), (row == 0).astype(jnp.int32)
    live = jnp.where(kind == 3, before, jnp.where(kind == 4, after, counts))
    live = jnp.where(kind == 1, counts * (1 - last), live)
    live = jnp.where(kind == 2, counts * (1 - first), live)
    wanted = (lane < USES) & (beam < live) & (names // 128 == col)
    marks = wanted.astype(jnp.float32)
    earlier = lax.broadcasted_iota(jnp.int32, (NS, NS), 0) <= lax.broadcasted_iota(jnp.int32, (NS, NS), 1)
    within = jnp.dot(marks, earlier.astype(jnp.float32), preferred_element_type=jnp.float32)
    above = lax.broadcasted_iota(jnp.int32, (COLS, COLS), 1) < lax.broadcasted_iota(jnp.int32, (COLS, COLS), 0)
    totals = jnp.broadcast_to(jnp.sum(marks, axis=1, keepdims=True), shape)
    ahead = jnp.dot(above.astype(jnp.float32), totals, preferred_element_type=jnp.float32)
    place = jnp.where(wanted, within + ahead - 1.0, -1.0)
    number = jnp.sum(marks)

    source = tile + (kind == 4).astype(jnp.int32) - (kind == 3).astype(jnp.int32)
    shift = 1 + (kind == 1).astype(jnp.int32) - (kind == 2).astype(jnp.int32)
    fields = (
        lax.rem(names, 128).astype(jnp.float32),
        (source * RECS + lax.rem(lane, RECS)).astype(jnp.float32),
        (shift * COLS + tile).astype(jnp.float32),
    )
    upright = jnp.transpose(place)
    slot = lax.broadcasted_iota(jnp.int32, (NS, LIST), 1).astype(jnp.float32)
    line = lax.broadcasted_iota(jnp.int32, (8, NS), 0)
    listed = jnp.zeros((8, LIST), jnp.float32)
    for t in range(COLS):
        here = (jnp.broadcast_to(upright[:, t : t + 1], (NS, LIST)) == slot).astype(jnp.bfloat16)
        rows = jnp.zeros((8, NS), jnp.float32)
        for f, field in enumerate(fields):
            rows = jnp.where(line == f, jnp.broadcast_to(field[t : t + 1, :], (8, NS)), rows)
        listed += jnp.dot(rows.astype(jnp.bfloat16), here, preferred_element_type=jnp.float32)
    place_in = lax.broadcasted_iota(jnp.int32, (8, LIST), 1).astype(jnp.float32)
    part = lax.broadcasted_iota(jnp.int32, (8, LIST), 0)
    listed = jnp.where((part == 2) & (place_in >= number), float(TARGETS), listed)
    listed = jnp.where(part == 3, number, listed)
    uses_vmem[...] = listed.astype(jnp.int32)


def gather(records, index, travel, amp):
    hbm = pl.BlockSpec(memory_space=pl.ANY)
    vmem = pl.BlockSpec(memory_space=pltpu.VMEM)
    smem = pl.BlockSpec(memory_space=pltpu.SMEM)
    return pl.pallas_call(
        gather_kernel,
        out_shape=(
            pltpu.VMEM((COLS * RECS, NP, NS), jnp.bfloat16),
            pltpu.VMEM(travel.shape, jnp.float32),
            pltpu.VMEM(amp.shape, jnp.float32),
            jax.ShapeDtypeStruct((8, LIST), jnp.int32),
            jax.ShapeDtypeStruct((COLS, NS), jnp.float32),
        ),
        in_specs=[hbm, vmem, hbm, hbm],
        out_specs=(vmem, vmem, vmem, hbm, hbm),
        scratch_shapes=[
            pltpu.VMEM((2, 8, NS), jnp.float32),
            pltpu.VMEM((8, NS), jnp.float32),
            pltpu.VMEM((COLS, 8, NS), jnp.float32),
            pltpu.VMEM((8, LIST), jnp.int32),
            pltpu.VMEM((COLS, NS), jnp.float32),
            pltpu.SemaphoreType.DMA((5,)),
            pltpu.SemaphoreType.DMA((40,)),
            pltpu.SemaphoreType.DMA((40,)),
            pltpu.SemaphoreType.DMA((2,)),
            pltpu.SemaphoreType.DMA((2,)),
            pltpu.SemaphoreType.DMA((COLS,)),
            pltpu.SemaphoreType.DMA((COLS,)),
        ],
        compiler_params=pltpu.CompilerParams(
            collective_id=1, has_side_effects=True, vmem_limit_bytes=32 << 20
        ),
        cost_estimate=pl.CostEstimate(flops=10_000_000, bytes_accessed=16_000_000, transcendentals=0),
        name="gather_records",
    )(records, index, travel, amp)


def image_kernel(uses, index, records, travel, amp, out, acc):
    acc[...] = jnp.zeros_like(acc)

    def step(i, carry):
        picked = []
        for d in range(GROUP):
            u = i * GROUP + d
            picked.append((uses[0, u], uses[1, u], uses[2, u]))
        totals = [jnp.zeros((8, NS), jnp.float32) for _ in picked]
        squares = [jnp.zeros((8, NS), jnp.float32) for _ in picked]
        for q in range(NP // 8):
            rows = pl.ds(8 * q, 8)
            for d, (block, rec, _) in enumerate(picked):
                t = travel[block, rows, :]
                a = amp[block, rows, :]
                pair = records[rec, pl.ds(16 * (q // 2), 16), :].astype(jnp.float32)
                r = pair[8 * (q % 2) : 8 * (q % 2) + 8]
                k = t.astype(jnp.int32)
                f = t - k.astype(jnp.float32)
                w0 = (1.0 - f).astype(jnp.bfloat16).astype(jnp.float32)
                w1 = f.astype(jnp.bfloat16).astype(jnp.float32)
                v0 = jnp.take_along_axis(r, k, axis=1, mode="promise_in_bounds")
                v1 = jnp.take_along_axis(r, k + 1, axis=1, mode="promise_in_bounds")
                totals[d] += a * (v0 * w0 + v1 * w1)
                squares[d] += a * a
        for d, (_, rec, target) in enumerate(picked):
            energy = index[rec // RECS, ENERGY + lax.rem(rec, RECS)]
            acc[target, 0] += totals[d]
            acc[target, 1] += squares[d] * energy
        return carry

    lax.fori_loop(0, (uses[3, 0] + GROUP - 1) // GROUP, step, 0)
    out[...] = jnp.sum(acc[pl.ds(0, TARGETS)], axis=2)


def image(uses, index, records, travel, amp):
    vmem = pl.BlockSpec(memory_space=pltpu.VMEM)
    smem = pl.BlockSpec(memory_space=pltpu.SMEM)
    return pl.pallas_call(
        image_kernel,
        out_shape=pltpu.VMEM((TARGETS, 2, NS), jnp.float32),
        in_specs=[smem, smem, vmem, vmem, vmem],
        out_specs=vmem,
        scratch_shapes=[pltpu.VMEM((TARGETS + 1, 2, 8, NS), jnp.float32)],
        compiler_params=pltpu.CompilerParams(vmem_limit_bytes=32 << 20),
        cost_estimate=pl.CostEstimate(flops=10_000_000, bytes_accessed=8_000_000, transcendentals=0),
        name="image_uses",
    )(uses, index, records, travel, amp)


def exchange_kernel(sums, out, near, total, parts, near_send, near_recv, part_send, part_recv):
    row, col = lax.axis_index("inline"), lax.axis_index("xline")
    greet(row, col)
    up = pltpu.make_async_remote_copy(
        sums.at[2], near.at[0], near_send.at[0], near_recv.at[0], device_id=(row + 1, col), device_id_type=MESH
    )
    down = pltpu.make_async_remote_copy(
        sums.at[0], near.at[1], near_send.at[1], near_recv.at[1], device_id=(row - 1, col), device_id_type=MESH
    )

    @pl.when(row < ROWS - 1)
    def _():
        up.start()

    @pl.when(row > 0)
    def _():
        down.start()

    total[...] = sums[1]

    @pl.when(row > 0)
    def _():
        up.wait_recv()
        total[...] += near[0]

    @pl.when(row < ROWS - 1)
    def _():
        down.wait_recv()
        total[...] += near[1]

    copies = []
    for other in range(1, COLS):
        there = lax.rem(col + other, COLS)
        copy = pltpu.make_async_remote_copy(
            total.at[there],
            parts.at[other],
            part_send.at[other],
            part_recv.at[other],
            device_id=(row, there),
            device_id_type=MESH,
        )
        copy.start()
        copies.append(copy)
    mine = total[col]
    for copy, other in zip(copies, range(1, COLS)):
        copy.wait_recv()
        mine += parts[other]
    out[0] = mine[0:1] / jnp.sqrt(1.0 + mine[1:2])
    for copy in copies:
        copy.wait_send()

    @pl.when(row < ROWS - 1)
    def _():
        up.wait_send()

    @pl.when(row > 0)
    def _():
        down.wait_send()


def exchange(sums):
    vmem = pl.BlockSpec(memory_space=pltpu.VMEM)
    return pl.pallas_call(
        exchange_kernel,
        out_shape=jax.ShapeDtypeStruct((1, 1, NS), jnp.float32),
        in_specs=[vmem],
        out_specs=vmem,
        scratch_shapes=[
            pltpu.VMEM((2, COLS, 2, NS), jnp.float32),
            pltpu.VMEM((COLS, 2, NS), jnp.float32),
            pltpu.VMEM((COLS, 2, NS), jnp.float32),
            pltpu.SemaphoreType.DMA((2,)),
            pltpu.SemaphoreType.DMA((2,)),
            pltpu.SemaphoreType.DMA((COLS,)),
            pltpu.SemaphoreType.DMA((COLS,)),
        ],
        compiler_params=pltpu.CompilerParams(collective_id=2, has_side_effects=True),
        cost_estimate=pl.CostEstimate(flops=10_000, bytes_accessed=100_000, transcendentals=0),
        name="exchange_sums",
    )(sums)


def imaged_by_any_count(records, beam_count, owner_list, block_list, travel_table, amp_table):
    records = records.reshape(RECS, NP, NS)
    named = (owner_list * 128 + block_list)[:, 0].astype(jnp.float32)
    named = named.reshape(SHOTS, 5, BEAMS).transpose(1, 0, 2).reshape(USES)
    energy = jnp.mean(jnp.square(records.astype(jnp.float32)), axis=(1, 2))
    count = jnp.broadcast_to(beam_count[0].astype(jnp.float32), (NS - COUNT,))
    index = jnp.broadcast_to(jnp.concatenate([named, energy, count]), (8, NS))
    gathered, travel, amp, uses, index = gather(records, index, travel_table, amp_table)
    sums = image(uses, index, gathered, travel, amp)
    return exchange(sums.reshape(3, COLS, 2, NS))


CLASSES = (
    (((0, 0), (1, 0), (-1, 0), (2, 0)), 48, 0, 64),
    (((0, 1), (0, -1), (1, 1), (1, -1), (-1, 1), (-1, -1)), 64, 64, 128),
    (((2, 1), (2, -1), (0, 2)), 40, 144, 64),
    (((1, 2), (-1, 2)), 32, 184, 32),
    (((2, 2),), 24, 216, 16),
)
WHERE = {tile: (c, n) for c, (tiles, _, _, _) in enumerate(CLASSES) for n, tile in enumerate(tiles)}
FAR_FIRST = sorted(
    ((dz, dx) for dz in (0, 1, -1, 2) for dx in (0, 1, -1, 2) if (dz, dx) != (0, 0)),
    key=lambda step: -abs(step[0]) - abs(step[1]),
)
SLOTS = 256
NBLOCKS = 128
COPIES = 40


def wrap(steps):
    return (steps + 1) % SIDE - 1


def fused_kernel(
    records, owner, block, count, travel, amp,
    out, flag_out,
    wide, buf0, buf1, buf2, buf3, buf4, travel_v, amp_v,
    mine, near, mixed, lines, uses_v, uses_s,
    con0, con1, con2, con3, con4, lit0, lit1, lit2, lit3, lit4,
    flag_mine, flags, sums, parts, edges, records_v, owner_v, block_v, met,
    local_sems, send_sems, recv_sems, near_send, near_recv, line_send, line_recv,
    flag_send, flag_recv, part_send, part_recv, edge_send, edge_recv,
    early_v, late_v, last_v, late_in, late_send, late_recv, energy_v,
):
    row, col = lax.axis_index("inline"), lax.axis_index("xline")
    z, x = col // SIDE, lax.rem(col, SIDE)
    bufs = (buf0, buf1, buf2, buf3, buf4)
    cons, lits = (con0, con1, con2, con3, con4), (lit0, lit1, lit2, lit3, lit4)
    near[...] = jnp.zeros_like(near)
    edges[...] = jnp.zeros_like(edges)

    def at(dz, dx):
        return lax.rem(z + dz + SIDE, SIDE) * SIDE + lax.rem(x + dx + SIDE, SIDE)

    beside = [(row, at(dz, dx)) for dz, dx in ((0, 1), (0, -1), (1, 0), (-1, 0))]
    beside += [(lax.rem(row + 1, ROWS), col), (lax.rem(row + ROWS - 1, ROWS), col)]
    barrier = pltpu.get_barrier_semaphore()
    for there in beside:
        pl.semaphore_signal(barrier, inc=1, device_id=there, device_id_type=MESH)
    inputs = [
        pltpu.make_async_copy(records, records_v, local_sems.at[3]),
        pltpu.make_async_copy(owner, owner_v, local_sems.at[4]),
        pltpu.make_async_copy(block, block_v, local_sems.at[5]),
    ]
    for copy in inputs:
        copy.start()
    loads = [
        pltpu.make_async_copy(travel, travel_v, local_sems.at[0]),
        pltpu.make_async_copy(amp, amp_v, local_sems.at[1]),
    ]
    for copy in loads:
        copy.start()

    for copy in inputs:
        copy.wait()

    wide[pl.ds(0, SHOTS * NP * BEAMS), :] = records_v[...].astype(jnp.float32).reshape(SHOTS * NP * BEAMS, NS)
    energies = jnp.zeros((8, NS), jnp.float32)
    lane8 = lax.broadcasted_iota(jnp.int32, (8, NS), 1)
    for s in range(SHOTS):
        for b in range(BEAMS):
            rec = wide[pl.ds(s * NP * BEAMS + b, NP, stride=BEAMS), :]
            bufs[0][row_of(s, 0, 0) + b] = rec.astype(jnp.bfloat16)
            energy = jnp.sum(rec * rec, keepdims=True) * (1.0 / (NP * NS))
            energies = jnp.where(lane8 == ENERGY + s * BEAMS + b, jnp.broadcast_to(energy, (8, NS)), energies)
    named = (owner_v[...] * 128 + block_v[...]).astype(jnp.float32)
    mine[...] = jnp.where(lane8 >= COUNT, count[0, 0].astype(jnp.float32), energies)
    mine[:, 0:USES] = jnp.broadcast_to(named, (8, USES))
    pl.semaphore_wait(barrier, len(beside))

    started = {}

    def send(kind, route, axis, step, first, second, lo, size):
        seen = (wrap(first - step), second) if axis == 0 else (first, wrap(second - step))
        here, there = WHERE[first, second][0], WHERE[seen][0]
        along_x = (axis == 0) == (route == 0)
        n = len(started)
        copy = pltpu.make_async_remote_copy(
            src_ref=bufs[here].at[pl.ds(row_of(route, first, second) + lo, size)],
            dst_ref=bufs[there].at[pl.ds(row_of(route, *seen) + lo, size)],
            send_sem=send_sems.at[n],
            recv_sem=recv_sems.at[n],
            device_id=(row, at(0, step) if along_x else at(step, 0)),
            device_id_type=MESH,
        )
        copy.start()
        key = (kind, route, step) if axis == 0 else (kind, route, first, step)
        started[key] = copy

    both, ways = (0, 1), (1, -1)
    half = BEAMS // 2

    def along_second(first):
        for way in ways:
            for route in both:
                send("c", route, 1, way, first, 0, 0, BEAMS)

    def pass_on(first):
        for way in ways:
            for route in both:
                started["c", route, first, way].wait_recv()
                send("d", route, 1, way, first, -way, 0 if way > 0 else half, half)

    def arrived(first):
        for route in both:
            for way in ways:
                started["d", route, first, way].wait_recv()

    def image_some(p, begin, end, group=GROUP):
        _, slots, base, held = CLASSES[p]
        buf, con, lit = bufs[p], cons[p], lits[p]

        def step(i, carry):
            places = [base + i * group + d for d in range(group)]
            picked = [(uses_s[0, u] & (NBLOCKS - 1), uses_s[1, u] & (held - 1)) for u in places]
            for d, (number, rec) in enumerate(picked):
                total, square = jnp.zeros((8, NS), jnp.float32), jnp.zeros((8, NS), jnp.float32)
                for q in range(NP // 8):
                    rows = pl.ds(8 * q, 8)
                    t = travel_v[number, rows, :]
                    a = amp_v[number, rows, :]
                    pair = buf[rec, pl.ds(16 * (q // 2), 16), :].astype(jnp.float32)
                    r = pair[8 * (q % 2) : 8 * (q % 2) + 8]
                    k = t.astype(jnp.int32)
                    f = t - k.astype(jnp.float32)
                    w0 = (1.0 - f).astype(jnp.bfloat16).astype(jnp.float32)
                    w1 = f.astype(jnp.bfloat16).astype(jnp.float32)
                    v0 = jnp.take_along_axis(r, k, axis=1, mode="promise_in_bounds")
                    v1 = jnp.take_along_axis(r, k + 1, axis=1, mode="promise_in_bounds")
                    total += a * (v0 * w0 + v1 * w1)
                    square += a * a
                con[pl.ds(i * group + d, 8, stride=slots), :] = total
                lit[pl.ds(i * group + d, 8, stride=slots), :] = square
            return carry

        if end - begin == group:
            step(begin // group, 0)
        else:
            lax.fori_loop(begin // group, end // group, step, 0)

    def total_of(p, listed):
        _, slots, base, _ = CLASSES[p]
        con = sum(cons[p][pl.ds(s * slots, slots), :] for s in range(8))
        lit = sum(lits[p][pl.ds(s * slots, slots), :] for s in range(8)) * energy_v[pl.ds(base, slots), :]
        target = jnp.broadcast_to(listed[2:3, base : base + slots], (NS, slots))
        line = (lax.broadcasted_iota(jnp.int32, (NS, slots), 0) + 1).astype(jnp.float32)
        to_tile = jnp.where(target == line, 1.0, 0.0).astype(jnp.bfloat16)
        rest = jnp.concatenate([con, lit], axis=1)
        total = jnp.zeros((NS, 2 * NS), jnp.float32)
        for _ in range(3):
            part = rest.astype(jnp.bfloat16)
            rest = rest - part.astype(jnp.float32)
            total += jnp.dot(to_tile, part, preferred_element_type=jnp.float32)
        return total[:, :NS] + pltpu.roll(total[:, NS:], 4, 0)

    for step in ways:
        for route in both:
            send("a", route, 0, step, 0, 0, 0, BEAMS)
    along_second(0)

    up = pltpu.make_async_remote_copy(
        mine, near.at[0], near_send.at[0], near_recv.at[0], device_id=(row + 1, col), device_id_type=MESH
    )
    down = pltpu.make_async_remote_copy(
        mine, near.at[1], near_send.at[1], near_recv.at[1], device_id=(row - 1, col), device_id_type=MESH
    )
    upward, downward = pl.when(row < ROWS - 1), pl.when(row > 0)
    upward(up.start)
    downward(down.start)
    apart = [(row, at(dz, dx)) for dz, dx in ((1, 1), (1, -1), (-1, 1), (-1, -1), (0, 2), (2, 0))]
    apart += [(lax.rem(row + 2, ROWS), col), (lax.rem(row + ROWS - 2, ROWS), col)]
    for turn, others in enumerate((beside, apart)):
        for there in others:
            pl.semaphore_signal(met.at[turn], inc=1, device_id=there, device_id_type=MESH)
        pl.semaphore_wait(met.at[turn], len(others))
    downward(up.wait_recv)
    upward(down.wait_recv)
    kind8 = lax.rem(lane8, 5 * BEAMS) // BEAMS
    kind8 = jnp.where(lane8 < USES, kind8, 0)
    mixed[...] = jnp.where(kind8 == 1, near[1], jnp.where(kind8 == 2, near[0], mine[...]))
    shares = []
    for other in range(1, COLS):
        share = pltpu.make_async_remote_copy(
            mixed, lines.at[other], line_send.at[other], line_recv.at[other],
            device_id=(row, lax.rem(col + other, COLS)), device_id_type=MESH,
        )
        share.start()
        shares.append(share)
    lines[0] = mixed[...]

    for step in ways:
        for route in both:
            started["a", route, step].wait_recv()
            send("b", route, 0, step, -step, 0, 0 if step > 0 else half, half)
        along_second(-step)

    for share in shares:
        share.wait_recv()
    listed, energy, over = list_uses(row, col, lines)
    energy_v[...] = jnp.transpose(jnp.broadcast_to(energy, (NS, SLOTS)))
    uses_v[...] = listed.astype(jnp.int32)
    to_smem = pltpu.make_async_copy(uses_v, uses_s, local_sems.at[2])
    to_smem.start()
    flag_mine[...] = over
    alarms = []
    for other in range(1, ROWS):
        alarm = pltpu.make_async_remote_copy(
            flag_mine, flags.at[other], flag_send.at[other], flag_recv.at[other],
            device_id=(lax.rem(row + other, ROWS), col), device_id_type=MESH,
        )
        alarm.start()
        alarms.append(alarm)

    for route in both:
        for step in ways:
            started["b", route, step].wait_recv()
    along_second(2)
    pass_on(0)
    to_smem.wait()
    for copy in loads:
        copy.wait()
    image_some(0, 0, 48, 16)
    pass_on(1)
    pass_on(-1)
    image_some(1, 0, 64, 16)
    pass_on(2)
    early = total_of(0, listed) + total_of(1, listed)
    arrived(0)
    image_some(2, 0, 40, 40)
    early += total_of(2, listed)
    early_v[...] = early.reshape(COLS, 8, NS)
    to_next = pltpu.make_async_remote_copy(
        early_v, edges.at[0], edge_send.at[0], edge_recv.at[0], device_id=(row + 1, col), device_id_type=MESH
    )
    to_prev = pltpu.make_async_remote_copy(
        early_v, edges.at[1], edge_send.at[1], edge_recv.at[1], device_id=(row - 1, col), device_id_type=MESH
    )
    upward(to_next.start)
    downward(to_prev.start)
    raised = flag_mine[...]
    for alarm, other in zip(alarms, range(1, ROWS)):
        alarm.wait_recv()
        raised = jnp.maximum(raised, flags[other])
    flag_out[0] = jnp.max(raised).astype(jnp.int32)
    arrived(1)
    arrived(-1)
    image_some(3, 0, 32, 32)
    late_v[...] = total_of(3, listed).reshape(COLS, 8, NS)
    next_row, prev_row = lax.rem(row + 1, ROWS), lax.rem(row + ROWS - 1, ROWS)
    direct = []

    def straight(source, dz, dx):
        for beside_row in (next_row, prev_row):
            n = len(direct)
            copy = pltpu.make_async_remote_copy(
                source.at[at(dz, dx)], late_in.at[n], late_send.at[n], late_recv.at[n],
                device_id=(beside_row, at(dz, dx)), device_id_type=MESH,
            )
            copy.start()
            direct.append(copy)

    for dz, dx in ((2, 1), (2, -1), (1, 2), (-1, 2)):
        straight(late_v, dz, dx)
    arrived(2)
    image_some(4, 0, 24, 24)
    last_v[...] = total_of(4, listed).reshape(COLS, 8, NS)
    straight(last_v, 2, 2)
    downward(to_next.wait_recv)
    upward(to_prev.wait_recv)
    own = early_v[...] + late_v[...] + last_v[...]
    sums[...] = own + pltpu.roll(edges[0], 7, 1) + pltpu.roll(edges[1], 1, 1)

    pieces = []
    for n, (dz, dx) in enumerate(FAR_FIRST):
        there = at(dz, dx)
        piece = pltpu.make_async_remote_copy(
            sums.at[there], parts.at[n], part_send.at[n], part_recv.at[n],
            device_id=(row, there), device_id_type=MESH,
        )
        piece.start()
        pieces.append(piece)
    for copy in started.values():
        copy.wait_send()
    for copy in shares + alarms + direct:
        copy.wait_send()
    upward(up.wait_send)
    downward(down.wait_send)
    upward(to_next.wait_send)
    downward(to_prev.wait_send)
    contrib, lighting = sums[col][1:2], sums[col][5:6]
    for n, copy in enumerate(direct):
        copy.wait_recv()
        line = 2 if n % 2 == 0 else 0
        contrib += late_in[n][line : line + 1]
        lighting += late_in[n][line + 4 : line + 5]
    whole = jnp.zeros((8, NS), jnp.float32)
    for n, piece in enumerate(pieces):
        piece.wait_recv()
        whole += parts[n]
    out[0] = (contrib + whole[1:2]) / jnp.sqrt(1.0 + (lighting + whole[5:6]))
    for piece in pieces:
        piece.wait_send()


def row_of(route, first, second):
    c, n = WHERE[first, second]
    return (route * len(CLASSES[c][0]) + n) * BEAMS


def list_uses(row, col, lines):
    table = jnp.concatenate([lines[lax.rem(col - tile + COLS, COLS)][0:1, :] for tile in range(COLS)], axis=0)
    shape = (COLS, NS)
    lane = lax.broadcasted_iota(jnp.int32, shape, 1)
    tile = lax.broadcasted_iota(jnp.int32, shape, 0)
    shot, kind, beam = lane // (5 * BEAMS), lax.rem(lane, 5 * BEAMS) // BEAMS, lax.rem(lane, BEAMS)
    names = table.astype(jnp.int32)

    def of_source(own):
        before, after = pltpu.roll(own, 1, 0), pltpu.roll(own, COLS - 1, 0)
        return jnp.where(kind == 3, before, jnp.where(kind == 4, after, own))

    last, first = (row == ROWS - 1).astype(jnp.int32), (row == 0).astype(jnp.int32)
    missing = (
        ((kind == 1) & (last == 1))
        | ((kind == 2) & (first == 1))
        | ((kind == 3) & (tile == 0))
        | ((kind == 4) & (tile == COLS - 1))
    )
    counts = of_source(jnp.broadcast_to(names[:, COUNT : COUNT + 1], shape))
    energy = of_source(
        jnp.take_along_axis(
            table, jnp.where(lane < USES, ENERGY + shot * BEAMS + beam, lane), axis=1, mode="promise_in_bounds"
        )
    )
    live = (lane < USES) & (beam < counts) & jnp.logical_not(missing)
    owners = names // 128

    source = tile + (kind == 4).astype(jnp.int32) - (kind == 3).astype(jnp.int32)
    along_z = (source // SIDE - owners // SIDE) & (SIDE - 1)
    along_x = (source - owners) & (SIDE - 1)
    code = jnp.where(shot == 0, along_x * SIDE + along_z, along_z * SIDE + along_x)
    group, record = jnp.zeros(shape, jnp.int32), jnp.zeros(shape, jnp.int32)
    for (first_step, second_step), (c, _) in WHERE.items():
        same = code == first_step % SIDE * SIDE + second_step % SIDE
        group = jnp.where(same, c, group)
        begin = [row_of(route, first_step, second_step) for route in (0, 1)]
        record = jnp.where(same, jnp.where(shot == 0, begin[0], begin[1]) + beam, record)

    column = lax.broadcasted_iota(jnp.int32, (NS, NS), 1)
    owned = jnp.where(live, owners * 8 + group, -1)
    over = jnp.zeros((1, 1), jnp.float32)
    for c, (_, slots, _, _) in enumerate(CLASSES):
        per_owner = jnp.concatenate(
            [jnp.sum((owned == o * 8 + c).astype(jnp.float32), axis=0, keepdims=True) for o in range(COLS)], axis=0
        )
        held = jnp.sum(per_owner, axis=1, keepdims=True)
        over = jnp.maximum(over, jnp.max((held > float(slots)).astype(jnp.float32), keepdims=True))

    earlier = lax.broadcasted_iota(jnp.int32, (NS, NS), 0) <= column
    above = lax.broadcasted_iota(jnp.int32, (COLS, COLS), 1) < lax.broadcasted_iota(jnp.int32, (COLS, COLS), 0)
    shift = 1 + (kind == 1).astype(jnp.int32) - (kind == 2).astype(jnp.int32)
    place = jnp.full(shape, -1.0)
    for c, (_, slots, base, _) in enumerate(CLASSES):
        marks = live & (owners == col) & (group == c)
        ones = marks.astype(jnp.float32)
        within = jnp.dot(ones, earlier.astype(jnp.float32), preferred_element_type=jnp.float32)
        totals = jnp.broadcast_to(jnp.sum(ones, axis=1, keepdims=True), shape)
        ahead = jnp.dot(above.astype(jnp.float32), totals, preferred_element_type=jnp.float32)
        rank = within + ahead - 1.0
        place = jnp.where(marks & (rank < float(slots)), rank + float(base), place)
    high = energy.astype(jnp.bfloat16).astype(jnp.float32)
    middle = (energy - high).astype(jnp.bfloat16).astype(jnp.float32)
    low = energy - high - middle
    fields = (
        lax.rem(names, 128).astype(jnp.float32),
        record.astype(jnp.float32),
        (tile * 8 + shift + 1).astype(jnp.float32),
        high,
        middle,
        low,
    )
    upright = jnp.transpose(place)
    slot = lax.broadcasted_iota(jnp.int32, (NS, SLOTS), 1).astype(jnp.float32)
    line = lax.broadcasted_iota(jnp.int32, (8, NS), 0)
    listed = jnp.zeros((8, SLOTS), jnp.float32)
    for t in range(COLS):
        here = (jnp.broadcast_to(upright[:, t : t + 1], (NS, SLOTS)) == slot).astype(jnp.bfloat16)
        rows = jnp.zeros((8, NS), jnp.float32)
        for f, field in enumerate(fields):
            rows = jnp.where(line == f, jnp.broadcast_to(field[t : t + 1, :], (8, NS)), rows)
        listed += jnp.dot(rows.astype(jnp.bfloat16), here, preferred_element_type=jnp.float32)
    return listed, listed[3:4] + listed[4:5] + listed[5:6], jnp.broadcast_to(over, (8, NS))


def fused(records, owner, block, count, travel, amp):
    vmem = pl.BlockSpec(memory_space=pltpu.VMEM)
    smem = pl.BlockSpec(memory_space=pltpu.SMEM)
    hbm = pl.BlockSpec(memory_space=pl.ANY)
    dma = pltpu.SemaphoreType.DMA
    f32 = jnp.float32
    return pl.pallas_call(
        fused_kernel,
        out_shape=(jax.ShapeDtypeStruct((1, 1, NS), f32), jax.ShapeDtypeStruct((1,), jnp.int32)),
        in_specs=[hbm, hbm, hbm, smem, hbm, hbm],
        out_specs=(vmem, smem),
        scratch_shapes=[
            pltpu.VMEM(((SHOTS * NP + 1) * BEAMS, NS), f32),
            *[pltpu.VMEM((held, NP, NS), jnp.bfloat16) for _, _, _, held in CLASSES],
            pltpu.VMEM(travel.shape, f32),
            pltpu.VMEM(amp.shape, f32),
            pltpu.VMEM((8, NS), f32),
            pltpu.VMEM((2, 8, NS), f32),
            pltpu.VMEM((8, NS), f32),
            pltpu.VMEM((COLS, 8, NS), f32),
            pltpu.VMEM((8, SLOTS), jnp.int32),
            pltpu.SMEM((8, SLOTS), jnp.int32),
            *[pltpu.VMEM((9 * slots, NS), f32) for _, slots, _, _ in CLASSES],
            *[pltpu.VMEM((9 * slots, NS), f32) for _, slots, _, _ in CLASSES],
            pltpu.VMEM((8, NS), f32),
            pltpu.VMEM((ROWS, 8, NS), f32),
            pltpu.VMEM((COLS, 8, NS), f32),
            pltpu.VMEM((COLS, 8, NS), f32),
            pltpu.VMEM((2, COLS, 8, NS), f32),
            pltpu.VMEM(records.shape, records.dtype),
            pltpu.VMEM(owner.shape, jnp.int32),
            pltpu.VMEM(block.shape, jnp.int32),
            pltpu.SemaphoreType.REGULAR((2,)),
            dma((6,)),
            dma((COPIES,)),
            dma((COPIES,)),
            dma((2,)),
            dma((2,)),
            dma((COLS,)),
            dma((COLS,)),
            dma((ROWS,)),
            dma((ROWS,)),
            dma((COLS,)),
            dma((COLS,)),
            dma((2,)),
            dma((2,)),
            pltpu.VMEM((COLS, 8, NS), f32),
            pltpu.VMEM((COLS, 8, NS), f32),
            pltpu.VMEM((COLS, 8, NS), f32),
            pltpu.VMEM((10, 8, NS), f32),
            dma((10,)),
            dma((10,)),
            pltpu.VMEM((SLOTS, NS), f32),
        ],
        compiler_params=pltpu.CompilerParams(
            collective_id=0, has_side_effects=True, vmem_limit_bytes=40 << 20
        ),
        cost_estimate=pl.CostEstimate(flops=10_000_000, bytes_accessed=16_000_000, transcendentals=0),
        name="migrate",
    )(records, owner, block, count, travel, amp)


def per_device(records, beam_count, owner_list, block_list, travel_table, amp_table):
    travel_table = pltpu.with_memory_space_constraint(travel_table, pltpu.HBM)
    amp_table = pltpu.with_memory_space_constraint(amp_table, pltpu.HBM)
    by_slowness = records.reshape(SHOTS, BEAMS, NP, NS).transpose(0, 2, 1, 3)
    owner, block = owner_list.reshape(1, USES), block_list.reshape(1, USES)
    quick, flag = fused(by_slowness, owner, block, beam_count, travel_table, amp_table)
    return lax.cond(
        flag[0] > 0,
        lambda: imaged_by_any_count(records, beam_count, owner_list, block_list, travel_table, amp_table),
        lambda: quick,
    )


def solution(mesh):
    placed = (
        P(None, "inline", "xline", None, None),
        P("inline", "xline"),
        P(("inline", "xline"), None),
        P(("inline", "xline"), None),
        P("xline", None, None),
        P("xline", None, None),
    )
    return jax.shard_map(
        per_device,
        mesh=mesh,
        in_specs=placed,
        out_specs=P("inline", "xline", None),
        check_vma=False,
    )
```
